128 devices in a mesh: section: 8 (over x, core), et: 16 (over y, z).
Axes of the slice: x: 4, y: 4, z: 4, core: 2. Of those that a mesh axis runs over, the one named last changes fastest.
Arguments:
- tokens_in: bfloat16 [512, 6144], P(('section', 'et')), may hold values from -6 to 6
- out_grad: bfloat16 [512, 6144], P('section', 'et'), may hold values from -6 to 6
- gate_weight: bfloat16 [2, 6144, 16384], P(None, None, ('section', 'et')), may hold values from -0.078125 to 0.078125
- up_weight: bfloat16 [2, 6144, 16384], P(None, None, ('section', 'et')), may hold values from -0.078125 to 0.078125
- down_weight: bfloat16 [2, 16384, 6144], P(None, ('section', 'et')), may hold values from -0.046875 to 0.046875
- slot_tokens: int32 [2, 256], replicated, may hold values from 0 to 511, as said below
- slot_counts: int32 [2], replicated, may hold values from 86 to 256, as said below
- slot_gates: float32 [2, 256], replicated, may hold values from 0.05 to 0.95
Outputs:
- input_grad: bfloat16 [512, 6144], P(('section', 'et'))
- gate_grad: bfloat16 [2, 6144, 16384], P(None, None, ('section', 'et'))
- up_grad: bfloat16 [2, 6144, 16384], P(None, None, ('section', 'et'))
- down_grad: bfloat16 [2, 16384, 6144], P(None, ('section', 'et'))
- router_grad: float32 [2, 256], replicated
The draws below stay inside these ranges and needn't reach their ends.
Inputs may be any that keep to these rules, and one draw needn't show every extreme that they name: `slot_tokens`: each expert's slots hold distinct tokens in ascending order. `slot_counts`: in every draw some expert has all 256 slots live.
All inputs are finite; a program needn't handle non-finite values.
Results may differ from the reference program's by a relative error of at most 0.01.
Values may be sent and summed in bfloat16 or wider, within the bound.
No kernel may reach another device: no remote copies, remote signals or barrier semaphores. Data moves between devices by JAX's collectives and lax.ppermute only.
A program may use at most 192 MiB of HBM per device.

```python
import jax
import jax.numpy as jnp
from jax import lax

D = 6144
FF = 16384
EW = 2
TOKENS = 512
CAP = 256


def draw_slot_tokens(key, part):
    key = jax.random.fold_in(key, 11)

    def one_expert(sub_key):
        return jnp.sort(jax.random.permutation(sub_key, TOKENS)[:CAP]).astype(jnp.int32)
    return jax.vmap(one_expert)(jax.random.split(key, EW))


def draw_slot_counts(key, part):
    key = jax.random.fold_in(key, 23)
    first, second = jax.random.split(key)
    counts = jax.random.randint(first, (EW,), CAP // 3 + 1, CAP + 1)
    full_one = jax.random.randint(second, (), 0, EW)
    return jnp.where(jnp.arange(EW) == full_one, CAP, counts).astype(jnp.int32)


def level_of(own_key, shape, shards, low, top_value):
    def one(axis_at, blocks):
        draws = jax.random.uniform(jax.random.fold_in(jax.random.fold_in(own_key, 6), axis_at), (blocks,), jnp.float32, low / len(shards), top_value / len(shards))
        return jnp.repeat(jnp.exp(draws), shape[axis_at] // blocks).reshape((-1,) + (1,) * (len(shape) - axis_at - 1))

    loudness = one(*shards[0])
    for cut in shards[1:]:
        loudness = loudness * one(*cut)
    return loudness


def noise(rng, extent, width, bound, shards=(), held_as=jnp.bfloat16):
    drawn = jax.random.normal(rng, extent, jnp.float32) * width
    if len(shards) > 0:
        drawn = level_of(rng, extent, shards, -0.22, 0.18) * drawn
    return jnp.clip(drawn, min=-bound, max=bound).astype(held_as)


def setup_inputs(seed: int = 0) -> dict:
    splits = jax.random.split(jax.random.key(seed), 9)
    return {
        "tokens_in": noise(splits[0], (TOKENS, D), 1.0, 6.0, ((0, 128),)),
        "out_grad": noise(splits[1], (TOKENS, D), 1.0, 6.0, ((0, 8), (1, 16))),
        "gate_weight": noise(splits[2], (EW, D, FF), D ** -0.5, 0.078125, ((2, 128),)),
        "up_weight": noise(splits[3], (EW, D, FF), D ** -0.5, 0.078125, ((2, 128),)),
        "down_weight": noise(splits[4], (EW, FF, D), FF ** -0.5, 0.046875, ((1, 128),)),
        "slot_tokens": draw_slot_tokens(jax.random.fold_in(splits[8], 71), 0),
        "slot_counts": draw_slot_counts(jax.random.fold_in(splits[8], 71), 0),
        "slot_gates": jnp.clip(jax.random.uniform(splits[7], (EW, CAP), jnp.float32, 0.05, 0.95), 0.05, 0.95),
    }


def contract_rows(left, right):
    return lax.dot_general(left, right, (((0,), (0,)), ((), ())), preferred_element_type=jnp.float32)


def contract_cols(left, right):
    return lax.dot_general(left, right, (((1,), (1,)), ((), ())), preferred_element_type=jnp.float32)


def expert_pass(rows, grads, gate_w, up_w, down_w, live, gates):
    pre_gate = jnp.dot(rows, gate_w, preferred_element_type=jnp.float32)
    pre_up = jnp.dot(rows, up_w, preferred_element_type=jnp.float32)
    sigma = jax.nn.sigmoid(pre_gate)
    active = pre_gate * sigma
    hidden = (active * pre_up).astype(jnp.bfloat16)
    back = contract_cols(grads, down_w)
    router_part = jnp.where(live, jnp.sum(hidden.astype(jnp.float32) * back, axis=1), 0.0)
    scale = jnp.where(live, gates, 0.0)
    hidden_grad = back * scale[:, None]
    gate_delta = (hidden_grad * pre_up * sigma * (1.0 + pre_gate * (1.0 - sigma))).astype(jnp.bfloat16)
    up_delta = (hidden_grad * active).astype(jnp.bfloat16)
    scaled = (grads.astype(jnp.float32) * scale[:, None]).astype(jnp.bfloat16)
    down_part = contract_rows(hidden, scaled)
    gate_part = contract_rows(rows, gate_delta)
    up_part = contract_rows(rows, up_delta)
    slot_input = contract_cols(gate_delta, gate_w) + contract_cols(up_delta, up_w)
    return router_part, gate_part, up_part, down_part, slot_input


def reference(tokens_in, out_grad, gate_weight, up_weight, down_weight, slot_tokens, slot_counts, slot_gates):
    input_grad = jnp.zeros((TOKENS, D), jnp.float32)
    routers, gates_out, ups_out, downs_out = [], [], [], []
    positions = jnp.arange(CAP)
    for expert in range(EW):
        token_ids = slot_tokens[expert].astype(jnp.int32)
        live = positions < slot_counts[expert]
        parts = expert_pass(tokens_in[token_ids], out_grad[token_ids], gate_weight[expert], up_weight[expert], down_weight[expert], live, slot_gates[expert])
        routers.append(parts[0])
        gates_out.append(parts[1])
        ups_out.append(parts[2])
        downs_out.append(parts[3])
        input_grad = input_grad.at[token_ids].add(parts[4])
    return (input_grad.astype(jnp.bfloat16), jnp.stack(gates_out).astype(jnp.bfloat16), jnp.stack(ups_out).astype(jnp.bfloat16), jnp.stack(downs_out).astype(jnp.bfloat16), jnp.stack(routers))
```

```python
import jax
import jax.numpy as jnp
from jax import lax
from jax.experimental import pallas as pl
from jax.experimental.pallas import tpu as pltpu
from jax.sharding import PartitionSpec as P

AXES = ("section", "et")
BF = jnp.bfloat16
F32 = jnp.float32
D = 6144
NX, NC, NY, NZ = 4, 2, 4, 4
H = 128
SHORT = 64
HALF = 256


def linear(x, c, y, z):
    return ((x * NC + c) * NY + y) * NZ + z


def shift_pairs(axis, step, by_core):
    pairs = []
    for x in range(NX):
        for c in range(NC):
            for y in range(NY):
                for z in range(NZ):
                    d = -step if (by_core and c == 1) else step
                    to = {
                        "x": ((x + d) % NX, c, y, z),
                        "y": (x, c, (y + d) % NY, z),
                        "z": (x, c, y, (z + d) % NZ),
                    }[axis]
                    pairs.append((linear(x, c, y, z), linear(*to)))
    return pairs


def shift(value, axis, step, by_core=False):
    return lax.ppermute(value, AXES, shift_pairs(axis, step, by_core))


def swap(value):
    pairs = [
        (linear(x, c, y, z), linear(x, 1 - c, y, z))
        for x in range(NX)
        for c in range(NC)
        for y in range(NY)
        for z in range(NZ)
    ]
    return lax.ppermute(value, AXES, pairs)


def position():
    section = lax.axis_index("section")
    et = lax.axis_index("et")
    return section // NC, section % NC, et // NZ, et % NZ


def nt(left, right):
    return lax.dot_general(left, right, (((1,), (1,)), ((), ())), preferred_element_type=F32)


def tn(left, right):
    return lax.dot_general(left, right, (((0,), (0,)), ((), ())), preferred_element_type=F32)


def row_copies(pieces, rows, sem, first, y):
    copies = []
    for r, piece in enumerate(pieces):
        for k in range(NY):
            start = pl.multiple_of(first + r * 64 + 16 * ((y - k) % NY), 16)
            copies.append(
                pltpu.make_async_copy(
                    piece.at[k], rows.at[pl.ds(start, 16), :], sem.at[r * NY + k]
                )
            )
    return copies


def grad_copies(pieces, grads, sem, first, y, z, sign):
    copies = []
    for j, piece in enumerate(pieces):
        for m in range(NZ):
            block = ((y - sign * j) % NY) * NZ + (z - m) % NZ
            start = pl.multiple_of(block * 384, 128)
            copies.append(
                pltpu.make_async_copy(
                    piece.at[m],
                    grads.at[pl.ds(first, HALF), pl.ds(start, 384)],
                    sem.at[j * NZ + m],
                )
            )
    return copies


KT = 1024
FT = 512


def main_kernel(where, *refs):
    t_in, g_in = refs[0:4], refs[4:8]
    weights = refs[8:14]
    scale_ref = refs[14]
    pa, pb = refs[15:19], refs[19:23]
    dl_own, dl_sib, hs_own, hs_sib, rp_ref = refs[23:28]
    rows, grads, wv, dv, acc_g, acc_b, deltas, tile, rbuf = refs[28:37]
    sem_t, sem_g, sem_w = refs[37:40]
    x, y, z, sign = where[0], where[1], where[2], where[3]
    copies_t = row_copies(t_in, rows, sem_t, 0, y)
    copies_g = grad_copies(g_in, grads, sem_g, 0, y, z, sign)
    wcopies = {}
    for s in range(2):
        gate, up, down = weights[3 * s : 3 * s + 3]
        for e in range(2):
            j = s * 2 + e
            wcopies[s, e, 0] = pltpu.make_async_copy(gate.at[e], wv.at[j, 0], sem_w.at[j * 3])
            wcopies[s, e, 1] = pltpu.make_async_copy(up.at[e], wv.at[j, 1], sem_w.at[j * 3 + 1])
            wcopies[s, e, 2] = pltpu.make_async_copy(
                down.at[e], dv.at[s, pl.ds(e * H, H), :], sem_w.at[j * 3 + 2]
            )
    for c in copies_t:
        c.start()
    for e in range(2):
        wcopies[0, e, 0].start()
        wcopies[0, e, 1].start()
    for c in copies_g:
        c.start()
    for e in range(2):
        wcopies[0, e, 2].start()
    for e in range(2):
        wcopies[1, e, 0].start()
        wcopies[1, e, 1].start()
    for e in range(2):
        wcopies[1, e, 2].start()
    for c in copies_t:
        c.wait()
    router = []
    for s in range(2):
        for e in range(2):
            j = s * 2 + e
            wcopies[s, e, 0].wait()
            wcopies[s, e, 1].wait()
            acc_g[e] = jnp.zeros((HALF, 2 * H), F32)

            @pl.loop(0, D // KT)
            def _(i, e=e, j=j):
                k = pl.ds(pl.multiple_of(i * KT, KT), KT)
                both = jnp.concatenate([wv[j, 0, k, :], wv[j, 1, k, :]], axis=1)
                acc_g[e] += jnp.dot(rows[:, k], both, preferred_element_type=F32)

        if s == 0:
            for c in copies_g:
                c.wait()
        for e in range(2):
            wcopies[s, e, 2].wait()
        acc_b[...] = jnp.zeros((HALF, 2 * H), F32)

        @pl.loop(0, D // KT)
        def _(i, s=s):
            k = pl.ds(pl.multiple_of(i * KT, KT), KT)
            acc_b[...] += nt(grads[:, k], dv[s, :, k])

        for e in range(2):
            j = s * 2 + e
            pre_gate = acc_g[e, :, 0:H]
            pre_up = acc_g[e, :, H : 2 * H]
            back = acc_b[:, e * H : (e + 1) * H]
            scale = scale_ref[:, e : e + 1]
            sigma = jax.nn.sigmoid(pre_gate)
            active = pre_gate * sigma
            hidden = active * pre_up
            part = jnp.sum(hidden.astype(BF).astype(F32) * back, axis=1, keepdims=True)
            if s == 0:
                router.append(part)
            else:
                router[e] += part
            hidden_grad = back * scale
            gate_delta = (hidden_grad * pre_up * sigma * (1.0 + pre_gate * (1.0 - sigma))).astype(BF)
            up_delta = (hidden_grad * active).astype(BF)
            scaled = (hidden * scale).astype(BF)
            deltas[:, j * 256 : j * 256 + H] = gate_delta
            deltas[:, j * 256 + H : (j + 1) * 256] = up_delta
            out, hs = (dl_own, hs_own) if s == 0 else (dl_sib, hs_sib)
            out[e, :, 0:H] = gate_delta
            out[e, :, H : 2 * H] = up_delta
            hs[e] = scaled
    lane = lax.broadcasted_iota(jnp.int32, (HALF, 128), 1)
    spread = jnp.where(lane == 0, router[0], jnp.where(lane == 1, router[1], 0.0))
    for k in range(NX):
        to = pl.multiple_of(((x - sign * k) % NX) * 64, 64)
        rbuf[pl.ds(to, 64), :] = spread[k * 64 : (k + 1) * 64]
    rp_ref[...] = rbuf[...].T[0:8]

    @pl.loop(0, D // FT)
    def _(i):
        f = pl.ds(pl.multiple_of(i * FT, FT), FT)
        wide = jnp.concatenate([wv[j, g, f, :] for j in range(4) for g in range(2)], axis=1)
        tile[...] = nt(deltas[...], wide)
        half = D // 2 // FT

        @pl.when(i < half)
        def _():
            for k in range(NX):
                pa[k][:, f] = tile[k * 64 : (k + 1) * 64, :].astype(BF)

        @pl.when(i >= half)
        def _():
            f2 = pl.ds(pl.multiple_of((i - half) * FT, FT), FT)
            for k in range(NY):
                for b in range(NX):
                    src = pl.multiple_of(b * 64 + ((y + k) % NY) * 16, 16)
                    pb[k][b, :, f2] = tile[pl.ds(src, 16), :].astype(BF)


def run_main(where, t, g, weights, scale):
    any_spec = pl.BlockSpec(memory_space=pl.ANY)
    vmem = pl.BlockSpec(memory_space=pltpu.VMEM)
    out_shape = (
        [jax.ShapeDtypeStruct((64, D // 2), BF)] * 4
        + [jax.ShapeDtypeStruct((4, 16, D // 2), BF)] * 4
        + [jax.ShapeDtypeStruct((2, HALF, 256), BF)] * 2
        + [jax.ShapeDtypeStruct((2, HALF, H), BF)] * 2
        + [jax.ShapeDtypeStruct((8, 256), F32)]
    )
    return pl.pallas_call(
        main_kernel,
        out_shape=out_shape,
        in_specs=[pl.BlockSpec(memory_space=pltpu.SMEM)] + [any_spec] * 14 + [vmem],
        out_specs=[vmem] * len(out_shape),
        scratch_shapes=[
            pltpu.VMEM((HALF, D), BF),
            pltpu.VMEM((HALF, D), BF),
            pltpu.VMEM((4, 2, D, H), BF),
            pltpu.VMEM((2, 2 * H, D), BF),
            pltpu.VMEM((2, HALF, 2 * H), F32),
            pltpu.VMEM((HALF, 2 * H), F32),
            pltpu.VMEM((HALF, 1024), BF),
            pltpu.VMEM((HALF, FT), F32),
            pltpu.VMEM((HALF, 128), F32),
            pltpu.SemaphoreType.DMA((16,)),
            pltpu.SemaphoreType.DMA((16,)),
            pltpu.SemaphoreType.DMA((12,)),
        ],
        compiler_params=pltpu.CompilerParams(vmem_limit_bytes=48 * 2**20),
        cost_estimate=pl.CostEstimate(
            flops=8_000_000_000, bytes_accessed=30_000_000, transcendentals=262144
        ),
        name="main",
    )(where, *t, *g, *weights, scale)


def grads_kernel(where, *refs):
    t_own, t_sib, g_own, g_sib = refs[0:4], refs[4:8], refs[8:12], refs[12:16]
    dl_own, dl_sib, hs_own, hs_sib = refs[16:20]
    gate_out, up_out, down_out = refs[20:23]
    rows, grads, deltas, hidden_t = refs[23:27]
    sems = refs[27]
    y, z, sign = where[1], where[2], where[3]
    i = pl.program_id(0)

    @pl.when(i == 0)
    def _():
        copies = row_copies(t_own, rows, sems.at[0], 0, y)
        copies += row_copies(t_sib, rows, sems.at[1], HALF, y)
        copies += grad_copies(g_own, grads, sems.at[2], 0, y, z, sign)
        copies += grad_copies(g_sib, grads, sems.at[3], HALF, y, z, -sign)
        for c in copies:
            c.start()
        for e in range(2):
            deltas[0:HALF, e * 256 : (e + 1) * 256] = dl_own[e]
            deltas[HALF:512, e * 256 : (e + 1) * 256] = dl_sib[e]
            hidden_t[e * H : (e + 1) * H, 0:HALF] = hs_own[e].T
            hidden_t[e * H : (e + 1) * H, HALF:512] = hs_sib[e].T
        for c in copies:
            c.wait()

    f = pl.ds(pl.multiple_of(i * FT, FT), FT)
    part = tn(rows[:, f], deltas[...])
    for e in range(2):
        gate_out[e] = part[:, e * 256 : e * 256 + H].astype(BF)
        up_out[e] = part[:, e * 256 + H : (e + 1) * 256].astype(BF)
    down = jnp.dot(hidden_t[...], grads[:, f], preferred_element_type=F32)
    for e in range(2):
        down_out[e] = down[e * H : (e + 1) * H].astype(BF)


def run_grads(where, t_own, t_sib, g_own, g_sib, dl_own, dl_sib, hs_own, hs_sib):
    any_spec = pl.BlockSpec(memory_space=pl.ANY)
    vmem = pl.BlockSpec(memory_space=pltpu.VMEM)
    return pl.pallas_call(
        grads_kernel,
        grid=(D // FT,),
        out_shape=[
            jax.ShapeDtypeStruct((2, D, H), BF),
            jax.ShapeDtypeStruct((2, D, H), BF),
            jax.ShapeDtypeStruct((2, H, D), BF),
        ],
        in_specs=[pl.BlockSpec(memory_space=pltpu.SMEM)] + [any_spec] * 16 + [vmem] * 4,
        out_specs=[
            pl.BlockSpec((2, FT, H), lambda i: (0, i, 0)),
            pl.BlockSpec((2, FT, H), lambda i: (0, i, 0)),
            pl.BlockSpec((2, H, FT), lambda i: (0, 0, i)),
        ],
        scratch_shapes=[
            pltpu.VMEM((512, D), BF),
            pltpu.VMEM((512, D), BF),
            pltpu.VMEM((512, 512), BF),
            pltpu.VMEM((256, 512), BF),
            pltpu.SemaphoreType.DMA((4, 16)),
        ],
        compiler_params=pltpu.CompilerParams(
            dimension_semantics=("arbitrary",), vmem_limit_bytes=40 * 2**20
        ),
        cost_estimate=pl.CostEstimate(
            flops=4_800_000_000, bytes_accessed=25_000_000, transcendentals=0
        ),
        name="weight_grads",
    )(where, *t_own, *t_sib, *g_own, *g_sib, dl_own, dl_sib, hs_own, hs_sib)


def total(first, rest):
    out = first.astype(F32)
    for r in rest:
        out = out + r.astype(F32)
    return out


def on_device(
    tokens_in, out_grad, gate_weight, up_weight, down_weight, slot_tokens, slot_counts, slot_gates
):
    x, c, y, z = position()
    sign = 1 - 2 * c
    where = jnp.stack([x, y, z, sign]).astype(jnp.int32)

    t_z = [tokens_in] + [shift(tokens_in, "z", k) for k in (1, 2, 3)]
    g_x = [out_grad] + [shift(out_grad, "x", k, True) for k in (1, 2, 3)]
    ring = jnp.stack([t_z[3], t_z[2], t_z[1], t_z[0], t_z[3], t_z[2], t_z[1]])
    t16 = lax.dynamic_slice(ring, (3 - z, 0, 0), (4, 4, D)).reshape(16, D)
    g4 = jnp.stack(g_x)
    t_y = jnp.stack([t16] + [shift(t16, "y", k) for k in (1, 2, 3)])
    g_z = jnp.stack([g4] + [shift(g4, "z", k) for k in (1, 2, 3)]).reshape(NZ, HALF, 384)
    t, g = [t_y], [g_z]
    for _ in range(3):
        t.append(shift(t[-1], "x", 1, True))
        g.append(shift(g[-1], "y", 1, True))

    gate_sib = swap(gate_weight)
    up_in, gate_sib = lax.optimization_barrier((up_weight, gate_sib))
    up_sib = swap(up_in)
    down_in, up_sib = lax.optimization_barrier((down_weight, up_sib))
    down_sib = swap(down_in)
    t_sib = [swap(p) for p in t]
    g_sib = [swap(p) for p in g]

    slots = jnp.arange(slot_tokens.shape[1])
    live = slots[None, :] < slot_counts[:, None]
    own = jnp.arange(HALF)
    own_token = ((x - sign * (own // 64)) % NX) * 128 + c * 64 + own % 64
    hit = (slot_tokens[None] == own_token[:, None, None]) & live[None]
    scale = jnp.sum(jnp.where(hit, slot_gates[None], 0.0), axis=2)

    weights = (gate_weight, up_weight, down_weight, gate_sib, up_sib, down_sib)
    outs = run_main(where, t, g, weights, scale)
    pa, pb = outs[0:4], outs[4:8]
    dl_own, dl_sib, hs_own, hs_sib, rp = outs[8:]

    ra = [shift(pa[k], "x", -k, True) for k in (1, 2, 3)]
    rb = [shift(pb[k], "y", k) for k in (1, 2, 3)]
    dl_got = swap(dl_sib)
    hs_got = swap(hs_sib)
    gate_grad, up_grad, down_grad = run_grads(
        where, t, t_sib, g, g_sib, dl_own, dl_got, hs_own, hs_got
    )
    qa = total(pa[0], ra).astype(BF).reshape(NY, 16, D // 2)
    qb = total(pb[0], rb).astype(BF)
    qa = lax.dynamic_slice(jnp.concatenate([qa, qa]), (y, 0, 0), (NY, 16, D // 2))
    ra = [shift(qa[k], "y", k) for k in (1, 2, 3)]
    rb = [shift(qb[k], "x", -k, True) for k in (1, 2, 3)]
    q = jnp.concatenate([total(qa[0], ra), total(qb[0], rb)], axis=1).astype(BF)
    q = q.reshape(NZ, 4, D)
    q = lax.dynamic_slice(jnp.concatenate([q, q]), (z, 0, 0), (NZ, 4, D))
    rz = [shift(q[k], "z", k) for k in (1, 2, 3)]
    input_grad = total(q[0], rz).astype(BF)

    for axis in ("x", "y", "z"):
        rp = rp + (shift(rp, axis, 1) + shift(rp, axis, 2) + shift(rp, axis, 3))
    other = swap(rp)
    pair = jnp.where(c == 0, jnp.stack([rp, other]), jnp.stack([other, rp]))
    by_token = pair[:, 0:2].reshape(2, 2, NX, 64).transpose(1, 2, 0, 3).reshape(2, 512)
    hit = slot_tokens[:, :, None] == jnp.arange(512)[None, None]
    router_grad = jnp.sum(jnp.where(hit, by_token[:, None, :], 0.0), axis=2)
    router_grad = jnp.where(live, router_grad, 0.0)
    return (input_grad, gate_grad, up_grad, down_grad, router_grad)


def solution(mesh):
    return jax.shard_map(
        on_device,
        mesh=mesh,
        in_specs=(
            P(("section", "et"), None),
            P("section", "et"),
            P(None, None, ("section", "et")),
            P(None, None, ("section", "et")),
            P(None, ("section", "et"), None),
            P(),
            P(),
            P(),
        ),
        out_specs=(
            P(("section", "et"), None),
            P(None, None, ("section", "et")),
            P(None, None, ("section", "et")),
            P(None, ("section", "et"), None),
            P(),
        ),
        check_vma=False,
    )
```

```python
import jax
import jax.numpy as jnp
from jax import lax
from jax.experimental import pallas as pl
from jax.experimental.pallas import tpu as pltpu
from jax.sharding import PartitionSpec as P

AXES = ("section", "et")
BF = jnp.bfloat16
F32 = jnp.float32
D = 6144
NX, NC, NY, NZ = 4, 2, 4, 4
H = 128
SHORT = 64
HALF = 256


def linear(x, c, y, z):
    return ((x * NC + c) * NY + y) * NZ + z


def shift_pairs(axis, step, by_core):
    pairs = []
    for x in range(NX):
        for c in range(NC):
            for y in range(NY):
                for z in range(NZ):
                    d = -step if (by_core and c == 1) else step
                    to = {
                        "x": ((x + d) % NX, c, y, z),
                        "y": (x, c, (y + d) % NY, z),
                        "z": (x, c, y, (z + d) % NZ),
                    }[axis]
                    pairs.append((linear(x, c, y, z), linear(*to)))
    return pairs


def shift(value, axis, step, by_core=False):
    return lax.ppermute(value, AXES, shift_pairs(axis, step, by_core))


def swap(value):
    pairs = [
        (linear(x, c, y, z), linear(x, 1 - c, y, z))
        for x in range(NX)
        for c in range(NC)
        for y in range(NY)
        for z in range(NZ)
    ]
    return lax.ppermute(value, AXES, pairs)


def position():
    section = lax.axis_index("section")
    et = lax.axis_index("et")
    return section // NC, section % NC, et // NZ, et % NZ


def nt(left, right):
    return lax.dot_general(left, right, (((1,), (1,)), ((), ())), preferred_element_type=F32)


def tn(left, right):
    return lax.dot_general(left, right, (((0,), (0,)), ((), ())), preferred_element_type=F32)


def total(first, rest):
    out = first.astype(F32)
    for r in rest:
        out = out + r.astype(F32)
    return out


KT = 1024
FT = 512
MIB = 2**20


def vmem_specs(n):
    return [pl.BlockSpec(memory_space=pltpu.VMEM)] * n


SMEM_SPEC = pl.BlockSpec(memory_space=pltpu.SMEM)


def first_stage_kernel(where, *refs):
    t, g, t_out, g_out, buf = refs[0:4], refs[4:8], refs[8], refs[9], refs[10]
    for k in range(NZ):
        buf[(where[2] - k) % NZ] = t[k][...].astype(F32)
    t_out[...] = jnp.concatenate([buf[k] for k in range(NZ)], axis=0).astype(BF)
    for k in range(NX):
        g_out[k * 64 : (k + 1) * 64, :] = g[k][...]


def run_first_stage(where, t, g):
    return pl.pallas_call(
        first_stage_kernel,
        out_shape=[jax.ShapeDtypeStruct((16, D), BF), jax.ShapeDtypeStruct((HALF, 384), BF)],
        in_specs=[SMEM_SPEC] + vmem_specs(8),
        out_specs=vmem_specs(2),
        scratch_shapes=[pltpu.VMEM((NZ, 4, D), F32)],
        compiler_params=pltpu.CompilerParams(vmem_limit_bytes=4 * MIB),
        name="first_stage",
    )(where, *t, *g)


def second_stage_kernel(where, *refs):
    t, g, t_out, g_out = refs[0:4], refs[4:8], refs[8], refs[9]
    for k in range(NY):
        start = pl.multiple_of(16 * ((where[1] - k) % NY), 16)
        t_out[pl.ds(start, 16), :] = t[k][...]
    for k in range(NZ):
        start = pl.multiple_of(384 * ((where[2] - k) % NZ), 128)
        g_out[:, pl.ds(start, 384)] = g[k][...]


def run_second_stage(where, t, g):
    return pl.pallas_call(
        second_stage_kernel,
        out_shape=[jax.ShapeDtypeStruct((64, D), BF), jax.ShapeDtypeStruct((HALF, 1536), BF)],
        in_specs=[SMEM_SPEC] + vmem_specs(8),
        out_specs=vmem_specs(2),
        compiler_params=pltpu.CompilerParams(vmem_limit_bytes=4 * MIB),
        name="second_stage",
    )(where, *t, *g)


def relay_kernel(*refs):
    value, (out, sem) = refs[0], refs[-2:]
    copy = pltpu.make_async_copy(value, out, sem)
    copy.start()
    copy.wait()


def run_relay(value, before):
    hbm = [pl.BlockSpec(memory_space=pltpu.HBM)]
    return pl.pallas_call(
        relay_kernel,
        out_shape=jax.ShapeDtypeStruct(value.shape, value.dtype),
        in_specs=hbm * (1 + len(before)),
        out_specs=hbm[0],
        scratch_shapes=[pltpu.SemaphoreType.DMA],
        compiler_params=pltpu.CompilerParams(vmem_limit_bytes=1 * MIB),
        cost_estimate=pl.CostEstimate(flops=0, bytes_accessed=6_000_000, transcendentals=0),
        name="relay",
    )(value, *before)


def row_copies(pieces, rows, sem):
    return [
        pltpu.make_async_copy(piece, rows.at[pl.ds(r * 64, 64), :], sem.at[r])
        for r, piece in enumerate(pieces)
    ]


def grad_copies(pieces, grads, sem, y, sign):
    copies = []
    for j, piece in enumerate(pieces):
        start = pl.multiple_of(((y - sign * j) % NY) * 1536, 128)
        copies.append(
            pltpu.make_async_copy(piece, grads.at[:, pl.ds(start, 1536)], sem.at[j])
        )
    return copies


def main_kernel(where, *refs):
    t_in, g_in = refs[0:4], refs[4:8]
    weights = (refs[8:11], refs[11:14])
    slots_ref, gates_ref = refs[14:16]
    pa_out, pb_out = refs[16:20], refs[20:24]
    own_out, sib_out, rp_ref, rows_out, grads_out = refs[24:29]
    rows, grads, wv, dv, pa, pb = refs[29:35]
    acc_g, acc_b, deltas, tile, rbuf, packed = refs[35:41]
    sem_t, sem_g, sem_w, sem_d, sem_o = refs[41:46]
    x, y, sign, core = where[0], where[1], where[3], where[4]
    copies_t = row_copies(t_in, rows, sem_t)
    copies_g = grad_copies(g_in, grads, sem_g, y, sign)
    tiles = D // KT

    def wide_copies(i):
        k = pl.ds(pl.multiple_of(i * KT, KT), KT)
        return [
            pltpu.make_async_copy(
                weights[s][n].at[:, k, :], wv.at[s, n, :, k, :], sem_w.at[i, s * 2 + n]
            )
            for s in range(2)
            for n in range(2)
        ]

    def tall_copies(i):
        k = pl.ds(pl.multiple_of(i * KT, KT), KT)
        return [
            pltpu.make_async_copy(weights[s][2].at[:, :, k], dv.at[s, :, :, k], sem_d.at[i, s])
            for s in range(2)
        ]

    for copy in copies_t:
        copy.start()
    for i in range(tiles):
        for copy in wide_copies(i):
            copy.start()
    for copy in copies_g:
        copy.start()
    for i in range(tiles):
        for copy in tall_copies(i):
            copy.start()
    acc_g[...] = jnp.zeros(acc_g.shape, F32)
    acc_b[...] = jnp.zeros(acc_b.shape, F32)
    scales = []
    slot = lax.broadcasted_iota(jnp.int32, (HALF, 256), 1)
    row = lax.broadcasted_iota(jnp.int32, (HALF, 256), 0)
    block = row // 64
    token = ((x - sign * block + NX) % NX) * 128 + core * 64 + (row - block * 64)
    for e in range(2):
        hit = (token == slots_ref[e : e + 1, :]) & (slot < where[5 + e])
        gate = jnp.broadcast_to(gates_ref[e : e + 1, :], (HALF, 256))
        scales.append(jnp.sum(jnp.where(hit, gate, 0.0), axis=1, keepdims=True))
    for copy in copies_t:
        copy.wait()
    rows_copy = pltpu.make_async_copy(rows, rows_out, sem_o.at[0])
    grads_copy = pltpu.make_async_copy(grads, grads_out, sem_o.at[1])

    @pl.loop(0, tiles)
    def _(i):
        for copy in wide_copies(i):
            copy.wait()
        k = pl.ds(pl.multiple_of(i * KT, KT), KT)
        wide = jnp.concatenate(
            [wv[s, n, e, k, :] for s in range(2) for e in range(2) for n in range(2)], axis=1
        )
        acc_g[...] += jnp.dot(rows[:, k], wide, preferred_element_type=F32)

    for copy in copies_g:
        copy.wait()

    @pl.loop(0, tiles)
    def _(i):
        for copy in tall_copies(i):
            copy.wait()
        k = pl.ds(pl.multiple_of(i * KT, KT), KT)
        tall = jnp.concatenate([dv[s, e, :, k] for s in range(2) for e in range(2)], axis=0)
        acc_b[...] += nt(grads[:, k], tall)

    rows_copy.start()
    grads_copy.start()
    router = [0.0, 0.0]
    for s in range(2):
        for e in range(2):
            j = s * 2 + e
            pre_gate = acc_g[:, j * 256 : j * 256 + H]
            pre_up = acc_g[:, j * 256 + H : (j + 1) * 256]
            back = acc_b[:, j * H : (j + 1) * H]
            scale = scales[e]
            sigma = jax.nn.sigmoid(pre_gate)
            active = pre_gate * sigma
            hidden = active * pre_up
            router[e] += jnp.sum(hidden.astype(BF).astype(F32) * back, axis=1, keepdims=True)
            hidden_grad = back * scale
            gate_delta = (hidden_grad * pre_up * sigma * (1.0 + pre_gate * (1.0 - sigma))).astype(BF)
            up_delta = (hidden_grad * active).astype(BF)
            deltas[:, j * 256 : j * 256 + H] = gate_delta
            deltas[:, j * 256 + H : (j + 1) * 256] = up_delta
            packed[s, :, e * 256 : e * 256 + H] = gate_delta
            packed[s, :, e * 256 + H : (e + 1) * 256] = up_delta
            packed[s, :, 512 + e * H : 512 + (e + 1) * H] = (hidden * scale).astype(BF)
    own_copy = pltpu.make_async_copy(packed.at[0], own_out, sem_o.at[2])
    sib_copy = pltpu.make_async_copy(packed.at[1], sib_out, sem_o.at[3])
    own_copy.start()
    sib_copy.start()
    lane = lax.broadcasted_iota(jnp.int32, (HALF, 128), 1)
    spread = jnp.where(lane == 0, router[0], jnp.where(lane == 1, router[1], 0.0))
    for k in range(NX):
        to = pl.multiple_of(((x - sign * k) % NX) * 64, 64)
        rbuf[pl.ds(to, 64), :] = spread[k * 64 : (k + 1) * 64]
    rp_ref[...] = rbuf[...].T[0:8]

    def partial(i):
        f = pl.ds(pl.multiple_of(i * FT, FT), FT)
        wide = jnp.concatenate(
            [wv[s, n, e, f, :] for s in range(2) for e in range(2) for n in range(2)], axis=1
        )
        return nt(deltas[...], wide)

    half = D // 2 // FT

    @pl.loop(0, half)
    def _(i):
        f = pl.ds(pl.multiple_of(i * FT, FT), FT)
        part = partial(i).astype(BF)
        for k in range(NX):
            pa[k, :, f] = part[k * 64 : (k + 1) * 64, :]

    copies = [pltpu.make_async_copy(pa.at[k], pa_out[k], sem_o.at[4 + k]) for k in range(NX)]
    for copy in copies:
        copy.start()

    @pl.loop(0, half)
    def _(i):
        f = pl.ds(pl.multiple_of(i * FT, FT), FT)
        tile[...] = partial(i + half).astype(BF)
        for k in range(NY):
            for b in range(NX):
                src = pl.multiple_of(b * 64 + ((y + k) % NY) * 16, 16)
                pb[k, b, :, f] = tile[pl.ds(src, 16), :]

    more = [pltpu.make_async_copy(pb.at[k], pb_out[k], sem_o.at[8 + k]) for k in range(NY)]
    for copy in more:
        copy.start()
    for copy in [rows_copy, grads_copy, own_copy, sib_copy] + copies + more:
        copy.wait()


def run_main(where, t, g, weights, slots, gates):
    hbm = [pl.BlockSpec(memory_space=pltpu.HBM)]
    out_shape = (
        [jax.ShapeDtypeStruct((64, D // 2), BF)] * 4
        + [jax.ShapeDtypeStruct((4, 16, D // 2), BF)] * 4
        + [jax.ShapeDtypeStruct((HALF, 768), BF)] * 2
        + [jax.ShapeDtypeStruct((8, 256), F32)]
        + [jax.ShapeDtypeStruct((HALF, D), BF)] * 2
    )
    return pl.pallas_call(
        main_kernel,
        out_shape=out_shape,
        in_specs=[SMEM_SPEC] + hbm * 14 + vmem_specs(2),
        out_specs=hbm * 10 + vmem_specs(1) + hbm * 2,
        scratch_shapes=[
            pltpu.VMEM((HALF, D), BF),
            pltpu.VMEM((HALF, D), BF),
            pltpu.VMEM((2, 2, 2, D, H), BF),
            pltpu.VMEM((2, 2, H, D), BF),
            pltpu.VMEM((4, 64, D // 2), BF),
            pltpu.VMEM((4, 4, 16, D // 2), BF),
            pltpu.VMEM((HALF, 1024), F32),
            pltpu.VMEM((HALF, 512), F32),
            pltpu.VMEM((HALF, 1024), BF),
            pltpu.VMEM((HALF, FT), BF),
            pltpu.VMEM((HALF, 128), F32),
            pltpu.VMEM((2, HALF, 768), BF),
            pltpu.SemaphoreType.DMA((4,)),
            pltpu.SemaphoreType.DMA((4,)),
            pltpu.SemaphoreType.DMA((D // KT, 4)),
            pltpu.SemaphoreType.DMA((D // KT, 2)),
            pltpu.SemaphoreType.DMA((12,)),
        ],
        compiler_params=pltpu.CompilerParams(vmem_limit_bytes=44 * MIB),
        cost_estimate=pl.CostEstimate(
            flops=8_000_000_000, bytes_accessed=30_000_000, transcendentals=262144
        ),
        name="main",
    )(where, *t, *g, *weights, slots, gates)


def up_kernel(*refs):
    rows_own, rows_sib, own, sib = refs[0:4]
    gate_out, up_out, token = refs[-3:]
    token[...] = jnp.zeros(token.shape, F32)
    part = tn(rows_own[...], own[:, 0:512]) + tn(rows_sib[...], sib[:, 0:512])
    for e in range(2):
        gate_out[e] = part[:, e * 256 : e * 256 + H].astype(BF)
        up_out[e] = part[:, e * 256 + H : (e + 1) * 256].astype(BF)


def run_up(rows_own, rows_sib, own, sib, before):
    tile = pl.BlockSpec((HALF, FT), lambda i: (0, i))
    whole = pl.BlockSpec((HALF, 768), lambda i: (0, 0))
    out = pl.BlockSpec((2, FT, H), lambda i: (0, i, 0))
    return pl.pallas_call(
        up_kernel,
        grid=(D // FT,),
        out_shape=[
            jax.ShapeDtypeStruct((2, D, H), BF),
            jax.ShapeDtypeStruct((2, D, H), BF),
            jax.ShapeDtypeStruct((8, 128), F32),
        ],
        in_specs=[tile, tile, whole, whole]
        + [pl.BlockSpec(memory_space=pl.ANY)] * len(before),
        out_specs=[out, out, pl.BlockSpec((8, 128), lambda i: (0, 0))],
        compiler_params=pltpu.CompilerParams(
            dimension_semantics=("arbitrary",), vmem_limit_bytes=16 * MIB
        ),
        cost_estimate=pl.CostEstimate(
            flops=3_200_000_000, bytes_accessed=13_000_000, transcendentals=0
        ),
        name="up_grads",
    )(rows_own, rows_sib, own, sib, *before)


def down_kernel(grads_own, grads_sib, own, sib, out, token, hidden):
    token[...] = jnp.zeros(token.shape, F32)

    @pl.when(pl.program_id(0) == 0)
    def _():
        hidden[:, 0:HALF] = own[:, 512:768].T
        hidden[:, HALF:512] = sib[:, 512:768].T

    part = jnp.dot(hidden[:, 0:HALF], grads_own[...], preferred_element_type=F32)
    part += jnp.dot(hidden[:, HALF:512], grads_sib[...], preferred_element_type=F32)
    for e in range(2):
        out[e] = part[e * H : (e + 1) * H].astype(BF)


def run_down(grads_own, grads_sib, own, sib):
    tile = pl.BlockSpec((HALF, 2 * FT), lambda i: (0, i))
    whole = pl.BlockSpec((HALF, 768), lambda i: (0, 0))
    return pl.pallas_call(
        down_kernel,
        grid=(D // FT // 2,),
        out_shape=[
            jax.ShapeDtypeStruct((2, H, D), BF),
            jax.ShapeDtypeStruct((8, 128), F32),
        ],
        in_specs=[tile, tile, whole, whole],
        out_specs=[
            pl.BlockSpec((2, H, 2 * FT), lambda i: (0, 0, i)),
            pl.BlockSpec((8, 128), lambda i: (0, 0)),
        ],
        scratch_shapes=[pltpu.VMEM((256, 512), BF)],
        compiler_params=pltpu.CompilerParams(
            dimension_semantics=("arbitrary",), vmem_limit_bytes=16 * MIB
        ),
        cost_estimate=pl.CostEstimate(
            flops=1_600_000_000, bytes_accessed=10_000_000, transcendentals=0
        ),
        name="down_grads",
    )(grads_own, grads_sib, own, sib)


def first_sum_kernel(where, *refs):
    ra, rb, rp, qa, qb, rp_out, buf = (
        refs[0:4],
        refs[4:8],
        refs[8:12],
        refs[12:16],
        refs[16:20],
        refs[20],
        refs[21],
    )
    y = where[1]
    rp_out[...] = total(rp[0][...], [r[...] for r in rp[1:]])
    buf[...] = total(ra[0][...], [r[...] for r in ra[1:]]).astype(BF)
    for k in range(NY):
        start = pl.multiple_of(((y + k) % NY) * 16, 16)
        qa[k][...] = buf[pl.ds(start, 16), :]
    for k in range(NX):
        qb[k][...] = total(rb[0][k], [r[k] for r in rb[1:]]).astype(BF)


def run_first_sum(where, ra, rb, rp):
    return pl.pallas_call(
        first_sum_kernel,
        out_shape=[jax.ShapeDtypeStruct((16, D // 2), BF)] * 8
        + [jax.ShapeDtypeStruct((8, 256), F32)],
        in_specs=[SMEM_SPEC] + vmem_specs(12),
        out_specs=vmem_specs(9),
        scratch_shapes=[pltpu.VMEM((64, D // 2), BF)],
        compiler_params=pltpu.CompilerParams(vmem_limit_bytes=8 * MIB),
        name="first_sum",
    )(where, *ra, *rb, *rp)


def second_sum_kernel(where, *refs):
    ra, rb, rp, own, out, rp_out, buf = (
        refs[0:4],
        refs[4:8],
        refs[8:12],
        refs[14],
        refs[15:18],
        refs[18],
        refs[19],
    )
    z = where[2]
    rp_out[...] = total(rp[0][...], [r[...] for r in rp[1:]])
    for n, r in enumerate((ra, rb)):
        part = total(r[0][...], [p[...] for p in r[1:]])
        for k in range(NZ):
            buf[k, :, n * (D // 2) : (n + 1) * (D // 2)] = part[4 * k : 4 * k + 4]
    for k in range(NZ):
        rows = buf[(z + k) % NZ]
        if k == 0:
            own[...] = rows
        else:
            out[k - 1][...] = rows.astype(BF)


def run_second_sum(where, ra, rb, rp, token, other):
    return pl.pallas_call(
        second_sum_kernel,
        out_shape=[jax.ShapeDtypeStruct((4, D), F32)]
        + [jax.ShapeDtypeStruct((4, D), BF)] * 3
        + [jax.ShapeDtypeStruct((8, 256), F32)],
        in_specs=[SMEM_SPEC] + vmem_specs(14),
        out_specs=vmem_specs(5),
        scratch_shapes=[pltpu.VMEM((NZ, 4, D), F32)],
        compiler_params=pltpu.CompilerParams(vmem_limit_bytes=8 * MIB),
        name="second_sum",
    )(where, *ra, *rb, *rp, token, other)


def last_sum_kernel(*refs):
    out, rp_out = refs[8], refs[9]
    out[...] = total(refs[0][...], [r[...] for r in refs[1:4]]).astype(BF)
    rp_out[...] = total(refs[4][...], [r[...] for r in refs[5:8]])


def run_last_sum(pieces, rp):
    return pl.pallas_call(
        last_sum_kernel,
        out_shape=[jax.ShapeDtypeStruct((4, D), BF), jax.ShapeDtypeStruct((8, 256), F32)],
        in_specs=vmem_specs(8),
        out_specs=vmem_specs(2),
        compiler_params=pltpu.CompilerParams(vmem_limit_bytes=4 * MIB),
        name="last_sum",
    )(*pieces, *rp)


def router_kernel(where, own, other, slots_ref, out):
    first = jnp.where(where[4] == 0, own[...], other[...])
    second = jnp.where(where[4] == 0, other[...], own[...])
    slots = slots_ref[...].T
    index = lax.broadcasted_iota(jnp.int32, (256, 256), 1)
    lane = lax.broadcasted_iota(jnp.int32, (256, 128), 1)
    spread = jnp.zeros((256, 128), F32)
    for e in range(2):
        picked = jnp.zeros((256, 1), F32)
        for core, values in enumerate((first, second)):
            token = (index // 64) * 128 + core * 64 + index % 64
            hit = slots[:, e : e + 1] == token
            line = jnp.broadcast_to(values[e : e + 1, :], (256, 256))
            picked += jnp.sum(jnp.where(hit, line, 0.0), axis=1, keepdims=True)
        spread = jnp.where(lane == e, picked, spread)
    lines = spread.T
    at = lax.broadcasted_iota(jnp.int32, (1, 256), 1)
    for e in range(2):
        out[e : e + 1, :] = jnp.where(at < where[5 + e], lines[e : e + 1, :], 0.0)


def run_router(where, own, other, slots):
    return pl.pallas_call(
        router_kernel,
        out_shape=jax.ShapeDtypeStruct((2, 256), F32),
        in_specs=[SMEM_SPEC] + vmem_specs(3),
        out_specs=vmem_specs(1)[0],
        compiler_params=pltpu.CompilerParams(vmem_limit_bytes=4 * MIB),
        name="router",
    )(where, own, other, slots)


def on_device(
    tokens_in, out_grad, gate_weight, up_weight, down_weight, slot_tokens, slot_counts, slot_gates
):
    x, c, y, z = position()
    where = jnp.stack([x, y, z, 1 - 2 * c, c, slot_counts[0], slot_counts[1]]).astype(jnp.int32)

    t = [tokens_in] + [shift(tokens_in, "z", k) for k in (1, 2, 3)]
    g = [out_grad] + [shift(out_grad, "x", k, True) for k in (1, 2, 3)]
    t16, g4 = run_first_stage(where, t, g)
    weights = (gate_weight, up_weight, down_weight)
    weights += tuple(swap(w) for w in weights)
    t = [t16] + [shift(t16, "y", k) for k in (1, 2, 3)]
    g = [g4] + [shift(g4, "z", k) for k in (1, 2, 3)]
    t64, g_z = run_second_stage(where, t, g)
    t, g = [t64], [g_z]
    for _ in range(3):
        t.append(shift(t[-1], "x", 1, True))
        g.append(shift(g[-1], "y", 1, True))
    outs = run_main(where, t, g, weights, slot_tokens, slot_gates)
    pa, pb = outs[0:4], outs[4:8]
    dl_own, dl_sib, rp, rows, grads = outs[8:]

    ra = [pa[0]] + [shift(pa[k], "x", -k, True) for k in (1, 2, 3)]
    rb = [pb[0]] + [shift(pb[k], "y", k) for k in (1, 2, 3)]
    dl_got, rows_sib = swap(dl_sib), swap(rows)
    before = [ra[1], ra[3], rb[1], rb[3]]
    grads_sib = swap(run_relay(grads, before))
    gate_grad, up_grad, up_token = run_up(rows, rows_sib, dl_own, dl_got, before)
    rps = [rp] + [shift(rp, "z", k) for k in (1, 2, 3)]
    q = run_first_sum(where, ra, rb, rps)
    qa, qb, rp = q[0:4], q[4:8], q[8]
    ra = [qa[0]] + [shift(qa[k], "y", k) for k in (1, 2, 3)]
    rb = [qb[0]] + [shift(qb[k], "x", -k, True) for k in (1, 2, 3)]
    rps = [rp] + [shift(rp, "x", k) for k in (1, 2, 3)]
    down_grad, token = run_down(grads, grads_sib, dl_own, dl_got)
    q = run_second_sum(where, ra, rb, rps, up_token, token)
    rz = [q[0]] + [shift(q[k], "z", k) for k in (1, 2, 3)]
    rps = [q[4]] + [shift(q[4], "y", k) for k in (1, 2, 3)]
    input_grad, rp = run_last_sum(rz, rps)
    router_grad = run_router(where, rp, swap(rp), slot_tokens)
    return (input_grad, gate_grad, up_grad, down_grad, router_grad)


def solution(mesh):
    return jax.shard_map(
        on_device,
        mesh=mesh,
        in_specs=(
            P(("section", "et"), None),
            P("section", "et"),
            P(None, None, ("section", "et")),
            P(None, None, ("section", "et")),
            P(None, ("section", "et"), None),
            P(),
            P(),
            P(),
        ),
        out_specs=(
            P(("section", "et"), None),
            P(None, None, ("section", "et")),
            P(None, None, ("section", "et")),
            P(None, ("section", "et"), None),
            P(),
        ),
        check_vma=False,
    )
```

```python
import jax
import jax.numpy as jnp
from jax import lax
from jax.experimental import pallas as pl
from jax.experimental.pallas import tpu as pltpu
from jax.sharding import PartitionSpec as P

AXES = ("section", "et")
BF = jnp.bfloat16
F32 = jnp.float32
D = 6144
NX, NC, NY, NZ = 4, 2, 4, 4
H = 128
SHORT = 64
HALF = 256


def linear(x, c, y, z):
    return ((x * NC + c) * NY + y) * NZ + z


def shift_pairs(axis, step):
    pairs = []
    for x in range(NX):
        for c in range(NC):
            for y in range(NY):
                for z in range(NZ):
                    to = {
                        "x": ((x + step) % NX, c, y, z),
                        "y": (x, c, (y + step) % NY, z),
                        "z": (x, c, y, (z + step) % NZ),
                    }[axis]
                    pairs.append((linear(x, c, y, z), linear(*to)))
    return pairs


def shift(value, axis, step):
    return lax.ppermute(value, AXES, shift_pairs(axis, step))


def swap(value):
    pairs = [
        (linear(x, c, y, z), linear(x, 1 - c, y, z))
        for x in range(NX)
        for c in range(NC)
        for y in range(NY)
        for z in range(NZ)
    ]
    return lax.ppermute(value, AXES, pairs)


def position():
    section = lax.axis_index("section")
    et = lax.axis_index("et")
    return section // NC, section % NC, et // NZ, et % NZ


def nt(left, right):
    return lax.dot_general(left, right, (((1,), (1,)), ((), ())), preferred_element_type=F32)


def tn(left, right):
    return lax.dot_general(left, right, (((0,), (0,)), ((), ())), preferred_element_type=F32)


def total(first, rest):
    out = first.astype(F32)
    for r in rest:
        out = out + r.astype(F32)
    return out


KT = 1024
FT = 512
MIB = 2**20
WIDE = D // 2 + 384


def vmem_specs(n):
    return [pl.BlockSpec(memory_space=pltpu.VMEM)] * n


SMEM_SPEC = pl.BlockSpec(memory_space=pltpu.SMEM)


def pack_kernel(tokens, grads, out):
    out[0:64, :] = grads[...]
    rows = tokens[...].astype(F32)
    for b in range(0, 16, 4):
        four = [rows[:, (b + i) * 384 : (b + i + 1) * 384] for i in range(4)]
        out[64 + 4 * b : 80 + 4 * b, :] = jnp.concatenate(four, axis=0).astype(BF)


def run_pack(tokens, grads):
    return pl.pallas_call(
        pack_kernel,
        out_shape=jax.ShapeDtypeStruct((128, 384), BF),
        in_specs=vmem_specs(2),
        out_specs=vmem_specs(1)[0],
        compiler_params=pltpu.CompilerParams(vmem_limit_bytes=4 * MIB),
        name="pack",
    )(tokens, grads)


def first_stage_kernel(where, *refs):
    packed, t_out, g_out, buf = refs[0:4], refs[4], refs[5], refs[6]
    for k in range(NZ):
        at = (where[2] - k) % NZ
        rows = packed[k][64:128, :].astype(F32)
        for b in range(16):
            buf[at, :, 384 * b : 384 * (b + 1)] = rows[4 * b : 4 * b + 4]
        start = pl.multiple_of(384 * at, 128)
        g_out[:, pl.ds(start, 384)] = packed[k][0:64, :]
    t_out[...] = jnp.concatenate([buf[k] for k in range(NZ)], axis=0).astype(BF)


def run_first_stage(where, packed):
    return pl.pallas_call(
        first_stage_kernel,
        out_shape=[jax.ShapeDtypeStruct((16, D), BF), jax.ShapeDtypeStruct((64, 1536), BF)],
        in_specs=[SMEM_SPEC] + vmem_specs(4),
        out_specs=vmem_specs(2),
        scratch_shapes=[pltpu.VMEM((NZ, 4, D), F32)],
        compiler_params=pltpu.CompilerParams(vmem_limit_bytes=4 * MIB),
        name="first_stage",
    )(where, *packed)


def second_stage_kernel(where, *refs):
    t, g, t_out, g_out = refs[0:4], refs[4:8], refs[-2], refs[-1]
    for k in range(NY):
        start = pl.multiple_of(16 * ((where[1] - k) % NY), 16)
        t_out[pl.ds(start, 16), :] = t[k][...]
    for k in range(NX):
        g_out[k * 64 : (k + 1) * 64, :] = g[k][...]


def run_second_stage(where, t, g, before):
    return pl.pallas_call(
        second_stage_kernel,
        out_shape=[jax.ShapeDtypeStruct((64, D), BF), jax.ShapeDtypeStruct((HALF, 1536), BF)],
        in_specs=[SMEM_SPEC] + vmem_specs(8) + [pl.BlockSpec(memory_space=pl.ANY)] * len(before),
        out_specs=vmem_specs(2),
        compiler_params=pltpu.CompilerParams(vmem_limit_bytes=4 * MIB),
        name="second_stage",
    )(where, *t, *g, *before)


def halves_kernel(t_low, t_high, g_low, g_high, a, b, c, d):
    a[...] = t_low[0:32, :]
    b[...] = t_high[32:64, :]
    c[...] = g_low[0:128, :]
    d[...] = g_high[128:256, :]


def run_halves(t_low, t_high, g_low, g_high):
    return pl.pallas_call(
        halves_kernel,
        out_shape=[jax.ShapeDtypeStruct((32, D), BF)] * 2
        + [jax.ShapeDtypeStruct((128, 1536), BF)] * 2,
        in_specs=vmem_specs(4),
        out_specs=vmem_specs(4),
        compiler_params=pltpu.CompilerParams(vmem_limit_bytes=4 * MIB),
        name="halves",
    )(t_low, t_high, g_low, g_high)


def relay_kernel(*refs):
    value, (out, sem) = refs[0], refs[-2:]
    copy = pltpu.make_async_copy(value, out, sem)
    copy.start()
    copy.wait()


def run_relay(value, before):
    hbm = [pl.BlockSpec(memory_space=pltpu.HBM)]
    return pl.pallas_call(
        relay_kernel,
        out_shape=jax.ShapeDtypeStruct(value.shape, value.dtype),
        in_specs=hbm * (1 + len(before)),
        out_specs=hbm[0],
        scratch_shapes=[pltpu.SemaphoreType.DMA],
        compiler_params=pltpu.CompilerParams(vmem_limit_bytes=1 * MIB),
        cost_estimate=pl.CostEstimate(flops=0, bytes_accessed=6_000_000, transcendentals=0),
        name="relay",
    )(value, *before)


def row_copies(pieces, rows, sem):
    places = (0, 64, 192, 128, 160)
    return [
        pltpu.make_async_copy(piece, rows.at[pl.ds(at, piece.shape[0]), :], sem.at[r])
        for r, (piece, at) in enumerate(zip(pieces, places))
    ]


def grad_copies(pieces, grads, sem, y):
    places = ((0, 0), (-1, 0), (1, 0), (2, 0), (2, 128))
    copies = []
    for j, (piece, (step, at)) in enumerate(zip(pieces, places)):
        start = pl.multiple_of(((y + step + NY) % NY) * 1536, 128)
        copies.append(
            pltpu.make_async_copy(
                piece, grads.at[pl.ds(at, piece.shape[0]), pl.ds(start, 1536)], sem.at[j]
            )
        )
    return copies


def split_three(value):
    high = value.astype(BF)
    rest = value - high.astype(F32)
    middle = rest.astype(BF)
    low = (rest - middle.astype(F32)).astype(BF)
    return jnp.concatenate([high, middle, low], axis=1)


def join_three(parts):
    out = parts.astype(F32)
    return out[:, 0:128] + out[:, 128:256] + out[:, 256:384]


def main_kernel(where, *refs):
    t_in, g_in = refs[0:5], refs[5:10]
    weights = (refs[10:13], refs[13:16])
    slots_ref, gates_ref = refs[16:18]
    pa_out, pb_out = refs[18:22], refs[22:26]
    own_out, rows_out, grads_out = refs[26:29]
    rows, grads, wv, dv, pa, pb = refs[29:35]
    acc_g, acc_b, deltas, tile, rbuf, packed = refs[35:41]
    sem_t, sem_g, sem_w, sem_d, sem_o = refs[41:46]
    x, y, core = where[0], where[1], where[4]
    copies_t = row_copies(t_in, rows, sem_t)
    copies_g = grad_copies(g_in, grads, sem_g, y)
    tiles = D // KT

    def wide_copies(i):
        k = pl.ds(pl.multiple_of(i * KT, KT), KT)
        return [
            pltpu.make_async_copy(
                weights[s][n].at[:, k, :], wv.at[s, n, :, k, :], sem_w.at[i, s * 2 + n]
            )
            for s in range(2)
            for n in range(2)
        ]

    def tall_copies(i):
        k = pl.ds(pl.multiple_of(i * KT, KT), KT)
        return [
            pltpu.make_async_copy(weights[s][2].at[:, :, k], dv.at[s, :, :, k], sem_d.at[i, s])
            for s in range(2)
        ]

    for copy in copies_t:
        copy.start()
    for i in range(tiles):
        for copy in wide_copies(i):
            copy.start()
    for copy in copies_g:
        copy.start()
    for i in range(tiles):
        for copy in tall_copies(i):
            copy.start()
    acc_g[...] = jnp.zeros(acc_g.shape, F32)
    acc_b[...] = jnp.zeros(acc_b.shape, F32)
    scales = []
    slot = lax.broadcasted_iota(jnp.int32, (HALF, 256), 1)
    row = lax.broadcasted_iota(jnp.int32, (HALF, 256), 0)
    block = row // 64
    token = ((x - block + NX) % NX) * 128 + core * 64 + (row - block * 64)
    for e in range(2):
        hit = (token == slots_ref[e : e + 1, :]) & (slot < where[5 + e])
        gate = jnp.broadcast_to(gates_ref[e : e + 1, :], (HALF, 256))
        scales.append(jnp.sum(jnp.where(hit, gate, 0.0), axis=1, keepdims=True))
    for copy in copies_t:
        copy.wait()
    rows_copy = pltpu.make_async_copy(rows, rows_out.at[:, pl.ds(0, D)], sem_o.at[0])
    grads_copy = pltpu.make_async_copy(grads, grads_out, sem_o.at[1])

    @pl.loop(0, tiles)
    def _(i):
        for copy in wide_copies(i):
            copy.wait()
        k = pl.ds(pl.multiple_of(i * KT, KT), KT)
        wide = jnp.concatenate(
            [wv[s, n, e, k, :] for s in range(2) for e in range(2) for n in range(2)], axis=1
        )
        acc_g[...] += jnp.dot(rows[:, k], wide, preferred_element_type=F32)

    for copy in copies_g:
        copy.wait()

    @pl.loop(0, tiles)
    def _(i):
        for copy in tall_copies(i):
            copy.wait()
        k = pl.ds(pl.multiple_of(i * KT, KT), KT)
        tall = jnp.concatenate([dv[s, e, :, k] for s in range(2) for e in range(2)], axis=0)
        acc_b[...] += nt(grads[:, k], tall)

    rows_copy.start()
    grads_copy.start()
    router = [0.0, 0.0]
    for s in range(2):
        for e in range(2):
            j = s * 2 + e
            pre_gate = acc_g[:, j * 256 : j * 256 + H]
            pre_up = acc_g[:, j * 256 + H : (j + 1) * 256]
            back = acc_b[:, j * H : (j + 1) * H]
            scale = scales[e]
            sigma = jax.nn.sigmoid(pre_gate)
            active = pre_gate * sigma
            hidden = active * pre_up
            router[e] += jnp.sum(hidden.astype(BF).astype(F32) * back, axis=1, keepdims=True)
            hidden_grad = back * scale
            gate_delta = (hidden_grad * pre_up * sigma * (1.0 + pre_gate * (1.0 - sigma))).astype(BF)
            up_delta = (hidden_grad * active).astype(BF)
            deltas[:, j * 256 : j * 256 + H] = gate_delta
            deltas[:, j * 256 + H : (j + 1) * 256] = up_delta
            packed[s, :, e * 256 : e * 256 + H] = gate_delta
            packed[s, :, e * 256 + H : (e + 1) * 256] = up_delta
            packed[s, :, 512 + e * H : 512 + (e + 1) * H] = (hidden * scale).astype(BF)
    own_copy = pltpu.make_async_copy(packed.at[0], own_out, sem_o.at[2])
    sib_copy = pltpu.make_async_copy(packed.at[1], rows_out.at[:, pl.ds(D, 768)], sem_o.at[3])
    own_copy.start()
    sib_copy.start()
    lane = lax.broadcasted_iota(jnp.int32, (HALF, 128), 1)
    spread = jnp.where(lane == 0, router[0], jnp.where(lane == 1, router[1], 0.0))
    for k in range(NX):
        to = pl.multiple_of(((x - k) % NX) * 64, 64)
        rbuf[pl.ds(to, 64), :] = spread[k * 64 : (k + 1) * 64]
    line = rbuf[...].T[0:2]
    four = [line[e : e + 1, h * 128 : (h + 1) * 128] for e in range(2) for h in range(2)]
    sums = split_three(jnp.concatenate(four + [jnp.zeros((12, 128), F32)], axis=0))
    for k in range(NX):
        pa[k, :, D // 2 :] = jnp.zeros((64, 384), BF)
        pa[k, 0:16, D // 2 :] = sums

    def partial(i):
        f = pl.ds(pl.multiple_of(i * FT, FT), FT)
        wide = jnp.concatenate(
            [wv[s, n, e, f, :] for s in range(2) for e in range(2) for n in range(2)], axis=1
        )
        return nt(deltas[...], wide)

    half = D // 2 // FT

    @pl.loop(0, half)
    def _(i):
        f = pl.ds(pl.multiple_of(i * FT, FT), FT)
        part = partial(i).astype(BF)
        for k in range(NX):
            pa[k, :, f] = part[k * 64 : (k + 1) * 64, :]

    copies = [pltpu.make_async_copy(pa.at[k], pa_out[k], sem_o.at[4 + k]) for k in range(NX)]
    for copy in copies:
        copy.start()

    @pl.loop(0, half)
    def _(i):
        f = pl.ds(pl.multiple_of(i * FT, FT), FT)
        tile[...] = partial(i + half).astype(BF)
        for k in range(NY):
            for b in range(NX):
                src = pl.multiple_of(b * 64 + ((y + k) % NY) * 16, 16)
                pb[k, b, :, f] = tile[pl.ds(src, 16), :]

    more = [pltpu.make_async_copy(pb.at[k], pb_out[k], sem_o.at[8 + k]) for k in range(NY)]
    for copy in more:
        copy.start()
    for copy in [rows_copy, grads_copy, own_copy, sib_copy] + copies + more:
        copy.wait()


def run_main(where, t, g, weights, slots, gates):
    hbm = [pl.BlockSpec(memory_space=pltpu.HBM)]
    out_shape = (
        [jax.ShapeDtypeStruct((64, WIDE), BF)] * 4
        + [jax.ShapeDtypeStruct((4, 16, D // 2), BF)] * 4
        + [jax.ShapeDtypeStruct((HALF, 768), BF)]
        + [jax.ShapeDtypeStruct((HALF, D + 768), BF)]
        + [jax.ShapeDtypeStruct((HALF, D), BF)]
    )
    return pl.pallas_call(
        main_kernel,
        out_shape=out_shape,
        in_specs=[SMEM_SPEC] + hbm * 16 + vmem_specs(2),
        out_specs=hbm * 11,
        scratch_shapes=[
            pltpu.VMEM((HALF, D), BF),
            pltpu.VMEM((HALF, D), BF),
            pltpu.VMEM((2, 2, 2, D, H), BF),
            pltpu.VMEM((2, 2, H, D), BF),
            pltpu.VMEM((4, 64, WIDE), BF),
            pltpu.VMEM((4, 4, 16, D // 2), BF),
            pltpu.VMEM((HALF, 1024), F32),
            pltpu.VMEM((HALF, 512), F32),
            pltpu.VMEM((HALF, 1024), BF),
            pltpu.VMEM((HALF, FT), BF),
            pltpu.VMEM((HALF, 128), F32),
            pltpu.VMEM((2, HALF, 768), BF),
            pltpu.SemaphoreType.DMA((5,)),
            pltpu.SemaphoreType.DMA((5,)),
            pltpu.SemaphoreType.DMA((D // KT, 4)),
            pltpu.SemaphoreType.DMA((D // KT, 2)),
            pltpu.SemaphoreType.DMA((12,)),
        ],
        compiler_params=pltpu.CompilerParams(vmem_limit_bytes=44 * MIB),
        cost_estimate=pl.CostEstimate(
            flops=8_000_000_000, bytes_accessed=30_000_000, transcendentals=262144
        ),
        name="main",
    )(where, *t, *g, *weights, slots, gates)


def up_kernel(*refs):
    rows_own, rows_sib, own, sib = refs[0:4]
    gate_out, up_out, token = refs[-3:]
    token[...] = jnp.zeros(token.shape, F32)
    part = tn(rows_own[...], own[:, 0:512]) + tn(rows_sib[...], sib[:, 0:512])
    for e in range(2):
        gate_out[e] = part[:, e * 256 : e * 256 + H].astype(BF)
        up_out[e] = part[:, e * 256 + H : (e + 1) * 256].astype(BF)


def run_up(rows_own, rows_sib, own, before):
    tile = pl.BlockSpec((HALF, FT), lambda i: (0, i))
    whole = pl.BlockSpec((HALF, 768), lambda i: (0, 0))
    tail = pl.BlockSpec((HALF, 768), lambda i: (0, D // 768))
    out = pl.BlockSpec((2, FT, H), lambda i: (0, i, 0))
    return pl.pallas_call(
        up_kernel,
        grid=(D // FT,),
        out_shape=[
            jax.ShapeDtypeStruct((2, D, H), BF),
            jax.ShapeDtypeStruct((2, D, H), BF),
            jax.ShapeDtypeStruct((8, 128), F32),
        ],
        in_specs=[tile, tile, whole, tail]
        + [pl.BlockSpec(memory_space=pl.ANY)] * len(before),
        out_specs=[out, out, pl.BlockSpec((8, 128), lambda i: (0, 0))],
        compiler_params=pltpu.CompilerParams(
            dimension_semantics=("arbitrary",), vmem_limit_bytes=16 * MIB
        ),
        cost_estimate=pl.CostEstimate(
            flops=3_200_000_000, bytes_accessed=13_000_000, transcendentals=0
        ),
        name="up_grads",
    )(rows_own, rows_sib, own, rows_sib, *before)


def down_kernel(grads_own, grads_sib, own, sib, out, token, hidden):
    token[...] = jnp.zeros(token.shape, F32)

    @pl.when(pl.program_id(0) == 0)
    def _():
        hidden[:, 0:HALF] = own[:, 512:768].T
        hidden[:, HALF:512] = sib[:, 512:768].T

    part = jnp.dot(hidden[:, 0:HALF], grads_own[...], preferred_element_type=F32)
    part += jnp.dot(hidden[:, HALF:512], grads_sib[...], preferred_element_type=F32)
    for e in range(2):
        out[e] = part[e * H : (e + 1) * H].astype(BF)


def run_down(grads_own, grads_sib, own, rows_sib):
    tile = pl.BlockSpec((HALF, 2 * FT), lambda i: (0, i))
    whole = pl.BlockSpec((HALF, 768), lambda i: (0, 0))
    tail = pl.BlockSpec((HALF, 768), lambda i: (0, D // 768))
    return pl.pallas_call(
        down_kernel,
        grid=(D // FT // 2,),
        out_shape=[
            jax.ShapeDtypeStruct((2, H, D), BF),
            jax.ShapeDtypeStruct((8, 128), F32),
        ],
        in_specs=[tile, tile, whole, tail],
        out_specs=[
            pl.BlockSpec((2, H, 2 * FT), lambda i: (0, 0, i)),
            pl.BlockSpec((8, 128), lambda i: (0, 0)),
        ],
        scratch_shapes=[pltpu.VMEM((256, 512), BF)],
        compiler_params=pltpu.CompilerParams(
            dimension_semantics=("arbitrary",), vmem_limit_bytes=16 * MIB
        ),
        cost_estimate=pl.CostEstimate(
            flops=1_600_000_000, bytes_accessed=10_000_000, transcendentals=0
        ),
        name="down_grads",
    )(grads_own, grads_sib, own, rows_sib)


def first_sum_kernel(where, *refs):
    ra, rb, qa, qb, buf = refs[0:4], refs[4:8], refs[9:13], refs[13:17], refs[17]
    half = D // 2
    buf[...] = total(ra[0][:, 0:half], [r[:, 0:half] for r in ra[1:]]).astype(BF)
    sums = join_three(ra[0][0:16, half:])
    for r in ra[1:]:
        sums += join_three(r[0:16, half:])
    sums = split_three(sums)
    for k in range(NY):
        start = pl.multiple_of(((where[1] + k) % NY) * 16, 16)
        qa[k][:, 0:half] = buf[pl.ds(start, 16), :]
        qa[k][:, half:] = sums
    for k in range(NX):
        qb[k][...] = total(rb[0][k], [r[k] for r in rb[1:]]).astype(BF)


def run_first_sum(where, ra, rb, token):
    return pl.pallas_call(
        first_sum_kernel,
        out_shape=[jax.ShapeDtypeStruct((16, WIDE), BF)] * 4
        + [jax.ShapeDtypeStruct((16, D // 2), BF)] * 4,
        in_specs=[SMEM_SPEC] + vmem_specs(9),
        out_specs=vmem_specs(8),
        scratch_shapes=[pltpu.VMEM((64, D // 2), BF)],
        compiler_params=pltpu.CompilerParams(vmem_limit_bytes=8 * MIB),
        name="first_sum",
    )(where, *ra, *rb, token)


def second_sum_kernel(where, *refs):
    ra, rb, own, out, buf = refs[0:4], refs[4:8], refs[9], refs[10:13], refs[13]
    half = D // 2
    for n, r in enumerate((ra, rb)):
        part = total(r[0][:, 0:half], [p[:, 0:half] for p in r[1:]])
        for k in range(NZ):
            buf[k, :, n * half : (n + 1) * half] = part[4 * k : 4 * k + 4]
    sums = join_three(ra[0][:, half:])
    for r in ra[1:]:
        sums += join_three(r[:, half:])
    parts = split_three(sums)[0:4]
    for k in range(NZ):
        rows = buf[(where[2] + k) % NZ]
        if k == 0:
            own[:, 0:D] = rows
            own[:, D:] = sums[0:4]
        else:
            out[k - 1][:, 0:D] = rows.astype(BF)
            out[k - 1][:, D:] = parts


def run_second_sum(where, ra, rb, token):
    return pl.pallas_call(
        second_sum_kernel,
        out_shape=[jax.ShapeDtypeStruct((4, D + 128), F32)]
        + [jax.ShapeDtypeStruct((4, D + 384), BF)] * 3,
        in_specs=[SMEM_SPEC] + vmem_specs(9),
        out_specs=vmem_specs(4),
        scratch_shapes=[pltpu.VMEM((NZ, 4, D), F32)],
        compiler_params=pltpu.CompilerParams(vmem_limit_bytes=8 * MIB),
        name="second_sum",
    )(where, *ra, *rb, token)


def last_sum_kernel(own, *refs):
    out, sums_out = refs[3], refs[4]
    out[...] = total(own[:, 0:D], [r[:, 0:D] for r in refs[0:3]]).astype(BF)
    sums = own[:, D:]
    for r in refs[0:3]:
        sums += join_three(r[:, D:])
    sums_out[0:4, :] = sums
    sums_out[4:8, :] = jnp.zeros((4, 128), F32)


def run_last_sum(pieces):
    return pl.pallas_call(
        last_sum_kernel,
        out_shape=[jax.ShapeDtypeStruct((4, D), BF), jax.ShapeDtypeStruct((8, 128), F32)],
        in_specs=vmem_specs(4),
        out_specs=vmem_specs(2),
        compiler_params=pltpu.CompilerParams(vmem_limit_bytes=4 * MIB),
        name="last_sum",
    )(*pieces)


def router_kernel(where, own, other, slots_ref, out):
    first = jnp.where(where[4] == 0, own[...], other[...])
    second = jnp.where(where[4] == 0, other[...], own[...])
    slots = slots_ref[...].T
    index = lax.broadcasted_iota(jnp.int32, (256, 128), 1)
    spread = jnp.zeros((256, 128), F32)
    for e in range(2):
        picked = jnp.zeros((256, 1), F32)
        for core, values in enumerate((first, second)):
            for h in range(2):
                at = index + h * 128
                token = (at // 64) * 128 + core * 64 + at % 64
                hit = slots[:, e : e + 1] == token
                line = jnp.broadcast_to(values[2 * e + h : 2 * e + h + 1, :], (256, 128))
                picked += jnp.sum(jnp.where(hit, line, 0.0), axis=1, keepdims=True)
        spread = jnp.where(index == e, picked, spread)
    lines = spread.T
    at = lax.broadcasted_iota(jnp.int32, (1, 256), 1)
    for e in range(2):
        out[e : e + 1, :] = jnp.where(at < where[5 + e], lines[e : e + 1, :], 0.0)


def run_router(where, own, other, slots):
    return pl.pallas_call(
        router_kernel,
        out_shape=jax.ShapeDtypeStruct((2, 256), F32),
        in_specs=[SMEM_SPEC] + vmem_specs(3),
        out_specs=vmem_specs(1)[0],
        compiler_params=pltpu.CompilerParams(vmem_limit_bytes=4 * MIB),
        name="router",
    )(where, own, other, slots)


def on_device(
    tokens_in, out_grad, gate_weight, up_weight, down_weight, slot_tokens, slot_counts, slot_gates
):
    x, c, y, z = position()
    where = jnp.stack([x, y, z, c, c, slot_counts[0], slot_counts[1]]).astype(jnp.int32)
    gate_sib, up_sib = swap(gate_weight), swap(up_weight)

    packed = run_pack(tokens_in, out_grad)
    t16, g64 = run_first_stage(where, [packed] + [shift(packed, "z", k) for k in (1, 2, 3)])
    t = [t16] + [shift(t16, "y", k) for k in (1, 2, 3)]
    g = [g64] + [shift(g64, "x", k) for k in (1, 2, 3)]
    down_sib = swap(down_weight)
    t64, g256 = run_second_stage(where, t, g, [gate_sib, up_sib])
    t_low, t_high = shift(t64, "x", 1), shift(t64, "x", -1)
    g_low, g_high = shift(g256, "y", 1), shift(g256, "y", -1)
    a, b, e, f = run_halves(t_low, t_high, g_low, g_high)
    t = (t64, t_low, t_high, shift(a, "x", 1), shift(b, "x", -1))
    g = (g256, g_low, g_high, shift(e, "y", 1), shift(f, "y", -1))
    weights = (gate_weight, up_weight, down_weight, gate_sib, up_sib, down_sib)
    outs = run_main(where, t, g, weights, slot_tokens, slot_gates)
    pa, pb = outs[0:4], outs[4:8]
    dl_own, rows, grads = outs[8:]

    ra = [pa[0]] + [shift(pa[k], "x", -k) for k in (1, 2, 3)]
    rb = [pb[0]] + [shift(pb[k], "y", k) for k in (1, 2, 3)]
    rows_sib = swap(rows)
    before = [ra[1], ra[3], rb[1], rb[3]]
    grads_sib = swap(run_relay(grads, before))
    gate_grad, up_grad, token = run_up(rows, rows_sib, dl_own, before)
    q = run_first_sum(where, ra, rb, token)
    qa, qb = q[0:4], q[4:8]
    ra = [qa[0]] + [shift(qa[k], "y", k) for k in (1, 2, 3)]
    rb = [qb[0]] + [shift(qb[k], "x", -k) for k in (1, 2, 3)]
    down_grad, token = run_down(grads, grads_sib, dl_own, rows_sib)
    q = run_second_sum(where, ra, rb, token)
    input_grad, sums = run_last_sum([q[0]] + [shift(q[k], "z", k) for k in (1, 2, 3)])
    router_grad = run_router(where, sums, swap(sums), slot_tokens)
    return (input_grad, gate_grad, up_grad, down_grad, router_grad)


def solution(mesh):
    return jax.shard_map(
        on_device,
        mesh=mesh,
        in_specs=(
            P(("section", "et"), None),
            P("section", "et"),
            P(None, None, ("section", "et")),
            P(None, None, ("section", "et")),
            P(None, ("section", "et"), None),
            P(),
            P(),
            P(),
        ),
        out_specs=(
            P(("section", "et"), None),
            P(None, None, ("section", "et")),
            P(None, None, ("section", "et")),
            P(None, ("section", "et"), None),
            P(),
        ),
        check_vma=False,
    )
```

```python
import jax
import jax.numpy as jnp
from jax import lax
from jax.experimental import pallas as pl
from jax.experimental.pallas import tpu as pltpu
from jax.sharding import PartitionSpec as P

AXES = ("x", "core", "y", "z")
BF = jnp.bfloat16
F32 = jnp.float32
D = 6144
NX, NC, NY, NZ = 4, 2, 4, 4
H = 128
SHORT = 64
HALF = 256


def linear(x, c, y, z):
    return ((x * NC + c) * NY + y) * NZ + z


def shift_pairs(axis, step):
    pairs = []
    for x in range(NX):
        for c in range(NC):
            for y in range(NY):
                for z in range(NZ):
                    to = {
                        "x": ((x + step) % NX, c, y, z),
                        "y": (x, c, (y + step) % NY, z),
                        "z": (x, c, y, (z + step) % NZ),
                    }[axis]
                    pairs.append((linear(x, c, y, z), linear(*to)))
    return pairs


def shift(value, axis, step):
    return lax.ppermute(value, AXES, shift_pairs(axis, step))


def swap(value):
    pairs = [
        (linear(x, c, y, z), linear(x, 1 - c, y, z))
        for x in range(NX)
        for c in range(NC)
        for y in range(NY)
        for z in range(NZ)
    ]
    return lax.ppermute(value, AXES, pairs)


def position():
    return tuple(lax.axis_index(axis) for axis in AXES)


def nt(left, right):
    return lax.dot_general(left, right, (((1,), (1,)), ((), ())), preferred_element_type=F32)


def tn(left, right):
    return lax.dot_general(left, right, (((0,), (0,)), ((), ())), preferred_element_type=F32)


def total(first, rest):
    out = first.astype(F32)
    for r in rest:
        out = out + r.astype(F32)
    return out


KT = 1024
FT = 512
MIB = 2**20
WIDE = D // 2 + 384


def vmem_specs(n):
    return [pl.BlockSpec(memory_space=pltpu.VMEM)] * n


SMEM_SPEC = pl.BlockSpec(memory_space=pltpu.SMEM)


def pack_kernel(tokens, grads, out):
    out[0:64, :] = grads[...]
    rows = tokens[...].astype(F32)
    for b in range(0, 16, 4):
        four = [rows[:, (b + i) * 384 : (b + i + 1) * 384] for i in range(4)]
        out[64 + 4 * b : 80 + 4 * b, :] = jnp.concatenate(four, axis=0).astype(BF)


def run_pack(tokens, grads):
    return pl.pallas_call(
        pack_kernel,
        out_shape=jax.ShapeDtypeStruct((128, 384), BF),
        in_specs=vmem_specs(2),
        out_specs=vmem_specs(1)[0],
        compiler_params=pltpu.CompilerParams(vmem_limit_bytes=4 * MIB),
        name="pack",
    )(tokens, grads)


def first_stage_kernel(where, *refs):
    packed, t_out, g_out, buf = refs[0:4], refs[4], refs[5], refs[6]
    for k in range(NZ):
        at = (where[2] - k) % NZ
        rows = packed[k][64:128, :].astype(F32)
        for b in range(16):
            buf[at, :, 384 * b : 384 * (b + 1)] = rows[4 * b : 4 * b + 4]
        start = pl.multiple_of(384 * at, 128)
        g_out[:, pl.ds(start, 384)] = packed[k][0:64, :]
    t_out[...] = jnp.concatenate([buf[k] for k in range(NZ)], axis=0).astype(BF)


def run_first_stage(where, packed):
    return pl.pallas_call(
        first_stage_kernel,
        out_shape=[jax.ShapeDtypeStruct((16, D), BF), jax.ShapeDtypeStruct((64, 1536), BF)],
        in_specs=[SMEM_SPEC] + vmem_specs(4),
        out_specs=vmem_specs(2),
        scratch_shapes=[pltpu.VMEM((NZ, 4, D), F32)],
        compiler_params=pltpu.CompilerParams(vmem_limit_bytes=4 * MIB),
        name="first_stage",
    )(where, *packed)


def second_stage_kernel(where, *refs):
    t, g, t_out, g_out = refs[0:4], refs[4:8], refs[-2], refs[-1]
    for k in range(NY):
        start = pl.multiple_of(16 * ((where[1] - k) % NY), 16)
        t_out[pl.ds(start, 16), :] = t[k][...]
    for k in range(NX):
        g_out[k * 64 : (k + 1) * 64, :] = g[k][...]


def run_second_stage(where, t, g, before):
    return pl.pallas_call(
        second_stage_kernel,
        out_shape=[jax.ShapeDtypeStruct((64, D), BF), jax.ShapeDtypeStruct((HALF, 1536), BF)],
        in_specs=[SMEM_SPEC] + vmem_specs(8) + [pl.BlockSpec(memory_space=pl.ANY)] * len(before),
        out_specs=vmem_specs(2),
        compiler_params=pltpu.CompilerParams(vmem_limit_bytes=4 * MIB),
        name="second_stage",
    )(where, *t, *g, *before)


def halves_kernel(t_low, t_high, g_low, g_high, a, b, c, d):
    a[...] = t_low[0:32, :]
    b[...] = t_high[32:64, :]
    c[...] = g_low[0:128, :]
    d[...] = g_high[128:256, :]


def run_halves(t_low, t_high, g_low, g_high):
    return pl.pallas_call(
        halves_kernel,
        out_shape=[jax.ShapeDtypeStruct((32, D), BF)] * 2
        + [jax.ShapeDtypeStruct((128, 1536), BF)] * 2,
        in_specs=vmem_specs(4),
        out_specs=vmem_specs(4),
        compiler_params=pltpu.CompilerParams(vmem_limit_bytes=4 * MIB),
        name="halves",
    )(t_low, t_high, g_low, g_high)


def relay_kernel(*refs):
    value, (out, sem) = refs[0], refs[-2:]
    copy = pltpu.make_async_copy(value, out, sem)
    copy.start()
    copy.wait()


def run_relay(value, before):
    hbm = [pl.BlockSpec(memory_space=pltpu.HBM)]
    return pl.pallas_call(
        relay_kernel,
        out_shape=jax.ShapeDtypeStruct(value.shape, value.dtype),
        in_specs=hbm * (1 + len(before)),
        out_specs=hbm[0],
        scratch_shapes=[pltpu.SemaphoreType.DMA],
        compiler_params=pltpu.CompilerParams(vmem_limit_bytes=1 * MIB),
        cost_estimate=pl.CostEstimate(flops=0, bytes_accessed=6_000_000, transcendentals=0),
        name="relay",
    )(value, *before)


def row_copies(pieces, rows, sem):
    places = (0, 64, 192, 128, 160)
    return [
        pltpu.make_async_copy(piece, rows.at[pl.ds(at, piece.shape[0]), :], sem.at[r])
        for r, (piece, at) in enumerate(zip(pieces, places))
    ]


def grad_copies(pieces, grads, sem, y):
    places = ((0, 0), (-1, 0), (1, 0), (2, 0), (2, 128))
    copies = []
    for j, (piece, (step, at)) in enumerate(zip(pieces, places)):
        start = pl.multiple_of(((y + step + NY) % NY) * 1536, 128)
        copies.append(
            pltpu.make_async_copy(
                piece, grads.at[pl.ds(at, piece.shape[0]), pl.ds(start, 1536)], sem.at[j]
            )
        )
    return copies


def split_three(value):
    high = value.astype(BF)
    rest = value - high.astype(F32)
    middle = rest.astype(BF)
    low = (rest - middle.astype(F32)).astype(BF)
    return jnp.concatenate([high, middle, low], axis=1)


def join_three(parts):
    out = parts.astype(F32)
    return out[:, 0:128] + out[:, 128:256] + out[:, 256:384]


def main_kernel(where, *refs):
    t_in, g_in = refs[0:5], refs[5:10]
    other = 1 - where[4]
    weights = (refs[10:13], (refs[13].at[other], refs[14].at[other], refs[15]))
    slots_ref, gates_ref = refs[16:18]
    pa_out, pb_out = refs[18:22], refs[22:26]
    own_out, rows_out, grads_out = refs[26:29]
    rows, grads, wv, dv, pa, pb = refs[29:35]
    acc_g, acc_b, deltas, tile, rbuf, packed = refs[35:41]
    sem_t, sem_g, sem_w, sem_d, sem_o = refs[41:46]
    x, y, core = where[0], where[1], where[4]
    copies_t = row_copies(t_in, rows, sem_t)
    copies_g = grad_copies(g_in, grads, sem_g, y)
    tiles = D // KT

    def wide_copies(i):
        k = pl.ds(pl.multiple_of(i * KT, KT), KT)
        return [
            pltpu.make_async_copy(
                weights[s][n].at[:, k, :], wv.at[s, n, :, k, :], sem_w.at[i, s * 2 + n]
            )
            for s in range(2)
            for n in range(2)
        ]

    def tall_copies(i):
        k = pl.ds(pl.multiple_of(i * KT, KT), KT)
        return [
            pltpu.make_async_copy(weights[s][2].at[:, :, k], dv.at[s, :, :, k], sem_d.at[i, s])
            for s in range(2)
        ]

    for copy in copies_t:
        copy.start()
    for i in range(tiles):
        for copy in wide_copies(i):
            copy.start()
    for copy in copies_g:
        copy.start()
    for i in range(tiles):
        for copy in tall_copies(i):
            copy.start()
    acc_g[...] = jnp.zeros(acc_g.shape, F32)
    acc_b[...] = jnp.zeros(acc_b.shape, F32)
    scales = []
    slot = lax.broadcasted_iota(jnp.int32, (HALF, 256), 1)
    row = lax.broadcasted_iota(jnp.int32, (HALF, 256), 0)
    block = row // 64
    token = ((x - block + NX) % NX) * 128 + core * 64 + (row - block * 64)
    for e in range(2):
        hit = (token == slots_ref[e : e + 1, :]) & (slot < where[5 + e])
        gate = jnp.broadcast_to(gates_ref[e : e + 1, :], (HALF, 256))
        scales.append(jnp.sum(jnp.where(hit, gate, 0.0), axis=1, keepdims=True))
    for copy in copies_t:
        copy.wait()
    rows_copy = pltpu.make_async_copy(rows, rows_out.at[:, pl.ds(0, D)], sem_o.at[0])
    grads_copy = pltpu.make_async_copy(grads, grads_out, sem_o.at[1])

    @pl.loop(0, tiles)
    def _(i):
        for copy in wide_copies(i):
            copy.wait()
        k = pl.ds(pl.multiple_of(i * KT, KT), KT)
        wide = jnp.concatenate(
            [wv[s, n, e, k, :] for s in range(2) for e in range(2) for n in range(2)], axis=1
        )
        acc_g[...] += jnp.dot(rows[:, k], wide, preferred_element_type=F32)

    for copy in copies_g:
        copy.wait()

    @pl.loop(0, tiles)
    def _(i):
        for copy in tall_copies(i):
            copy.wait()
        k = pl.ds(pl.multiple_of(i * KT, KT), KT)
        tall = jnp.concatenate([dv[s, e, :, k] for s in range(2) for e in range(2)], axis=0)
        acc_b[...] += nt(grads[:, k], tall)

    rows_copy.start()
    grads_copy.start()
    router = [0.0, 0.0]
    for s in range(2):
        for e in range(2):
            j = s * 2 + e
            pre_gate = acc_g[:, j * 256 : j * 256 + H]
            pre_up = acc_g[:, j * 256 + H : (j + 1) * 256]
            back = acc_b[:, j * H : (j + 1) * H]
            scale = scales[e]
            sigma = jax.nn.sigmoid(pre_gate)
            active = pre_gate * sigma
            hidden = active * pre_up
            router[e] += jnp.sum(hidden.astype(BF).astype(F32) * back, axis=1, keepdims=True)
            hidden_grad = back * scale
            gate_delta = (hidden_grad * pre_up * sigma * (1.0 + pre_gate * (1.0 - sigma))).astype(BF)
            up_delta = (hidden_grad * active).astype(BF)
            deltas[:, j * 256 : j * 256 + H] = gate_delta
            deltas[:, j * 256 + H : (j + 1) * 256] = up_delta
            packed[s, :, e * 256 : e * 256 + H] = gate_delta
            packed[s, :, e * 256 + H : (e + 1) * 256] = up_delta
            packed[s, :, 512 + e * H : 512 + (e + 1) * H] = (hidden * scale).astype(BF)
    own_copy = pltpu.make_async_copy(packed.at[0], own_out, sem_o.at[2])
    sib_copy = pltpu.make_async_copy(packed.at[1], rows_out.at[:, pl.ds(D, 768)], sem_o.at[3])
    own_copy.start()
    sib_copy.start()
    lane = lax.broadcasted_iota(jnp.int32, (HALF, 128), 1)
    spread = jnp.where(lane == 0, router[0], jnp.where(lane == 1, router[1], 0.0))
    for k in range(NX):
        to = pl.multiple_of(((x - k) % NX) * 64, 64)
        rbuf[pl.ds(to, 64), :] = spread[k * 64 : (k + 1) * 64]
    line = rbuf[...].T[0:2]
    four = [line[e : e + 1, h * 128 : (h + 1) * 128] for e in range(2) for h in range(2)]
    sums = split_three(jnp.concatenate(four + [jnp.zeros((12, 128), F32)], axis=0))
    for k in range(NX):
        pa[k, :, D // 2 :] = jnp.zeros((64, 384), BF)
        pa[k, 0:16, D // 2 :] = sums

    def partial(i):
        f = pl.ds(pl.multiple_of(i * FT, FT), FT)
        wide = jnp.concatenate(
            [wv[s, n, e, f, :] for s in range(2) for e in range(2) for n in range(2)], axis=1
        )
        return nt(deltas[...], wide)

    half = D // 2 // FT

    @pl.loop(0, half)
    def _(i):
        f = pl.ds(pl.multiple_of(i * FT, FT), FT)
        part = partial(i).astype(BF)
        for k in range(NX):
            pa[k, :, f] = part[k * 64 : (k + 1) * 64, :]

    copies = [pltpu.make_async_copy(pa.at[k], pa_out[k], sem_o.at[4 + k]) for k in range(NX)]
    for copy in copies:
        copy.start()

    @pl.loop(0, half)
    def _(i):
        f = pl.ds(pl.multiple_of(i * FT, FT), FT)
        tile[...] = partial(i + half).astype(BF)
        for k in range(NY):
            for b in range(NX):
                src = pl.multiple_of(b * 64 + ((y + k) % NY) * 16, 16)
                pb[k, b, :, f] = tile[pl.ds(src, 16), :]

    more = [pltpu.make_async_copy(pb.at[k], pb_out[k], sem_o.at[8 + k]) for k in range(NY)]
    for copy in more:
        copy.start()
    for copy in [rows_copy, grads_copy, own_copy, sib_copy] + copies + more:
        copy.wait()


def run_main(where, t, g, weights, slots, gates):
    hbm = [pl.BlockSpec(memory_space=pltpu.HBM)]
    out_shape = (
        [jax.ShapeDtypeStruct((64, WIDE), BF)] * 4
        + [jax.ShapeDtypeStruct((4, 16, D // 2), BF)] * 4
        + [jax.ShapeDtypeStruct((HALF, 768), BF)]
        + [jax.ShapeDtypeStruct((HALF, D + 768), BF)]
        + [jax.ShapeDtypeStruct((HALF, D), BF)]
    )
    return pl.pallas_call(
        main_kernel,
        out_shape=out_shape,
        in_specs=[SMEM_SPEC] + hbm * 16 + vmem_specs(2),
        out_specs=hbm * 11,
        scratch_shapes=[
            pltpu.VMEM((HALF, D), BF),
            pltpu.VMEM((HALF, D), BF),
            pltpu.VMEM((2, 2, 2, D, H), BF),
            pltpu.VMEM((2, 2, H, D), BF),
            pltpu.VMEM((4, 64, WIDE), BF),
            pltpu.VMEM((4, 4, 16, D // 2), BF),
            pltpu.VMEM((HALF, 1024), F32),
            pltpu.VMEM((HALF, 512), F32),
            pltpu.VMEM((HALF, 1024), BF),
            pltpu.VMEM((HALF, FT), BF),
            pltpu.VMEM((HALF, 128), F32),
            pltpu.VMEM((2, HALF, 768), BF),
            pltpu.SemaphoreType.DMA((5,)),
            pltpu.SemaphoreType.DMA((5,)),
            pltpu.SemaphoreType.DMA((D // KT, 4)),
            pltpu.SemaphoreType.DMA((D // KT, 2)),
            pltpu.SemaphoreType.DMA((12,)),
        ],
        compiler_params=pltpu.CompilerParams(vmem_limit_bytes=58 * MIB),
        cost_estimate=pl.CostEstimate(
            flops=8_000_000_000, bytes_accessed=30_000_000, transcendentals=262144
        ),
        name="main",
    )(where, *t, *g, *weights, slots, gates)


def up_kernel(*refs):
    rows_own, rows_sib, own, sib = refs[0:4]
    gate_out, up_out, token = refs[-3:]
    token[...] = jnp.zeros(token.shape, F32)
    part = tn(rows_own[...], own[:, 0:512]) + tn(rows_sib[...], sib[:, 0:512])
    for e in range(2):
        gate_out[e] = part[:, e * 256 : e * 256 + H].astype(BF)
        up_out[e] = part[:, e * 256 + H : (e + 1) * 256].astype(BF)


def run_up(rows_own, rows_sib, own, before):
    tile = pl.BlockSpec((HALF, FT), lambda i: (0, i))
    whole = pl.BlockSpec((HALF, 768), lambda i: (0, 0))
    tail = pl.BlockSpec((HALF, 768), lambda i: (0, D // 768))
    out = pl.BlockSpec((2, FT, H), lambda i: (0, i, 0))
    return pl.pallas_call(
        up_kernel,
        grid=(D // FT,),
        out_shape=[
            jax.ShapeDtypeStruct((2, D, H), BF),
            jax.ShapeDtypeStruct((2, D, H), BF),
            jax.ShapeDtypeStruct((8, 128), F32),
        ],
        in_specs=[tile, tile, whole, tail]
        + [pl.BlockSpec(memory_space=pl.ANY)] * len(before),
        out_specs=[out, out, pl.BlockSpec((8, 128), lambda i: (0, 0))],
        compiler_params=pltpu.CompilerParams(
            dimension_semantics=("arbitrary",), vmem_limit_bytes=16 * MIB
        ),
        cost_estimate=pl.CostEstimate(
            flops=3_200_000_000, bytes_accessed=13_000_000, transcendentals=0
        ),
        name="up_grads",
    )(rows_own, rows_sib, own, rows_sib, *before)


def down_kernel(grads_own, grads_sib, own, sib, out, token, hidden):
    token[...] = jnp.zeros(token.shape, F32)

    @pl.when(pl.program_id(0) == 0)
    def _():
        hidden[:, 0:HALF] = own[:, 512:768].T
        hidden[:, HALF:512] = sib[:, 512:768].T

    part = jnp.dot(hidden[:, 0:HALF], grads_own[...], preferred_element_type=F32)
    part += jnp.dot(hidden[:, HALF:512], grads_sib[...], preferred_element_type=F32)
    for e in range(2):
        out[e] = part[e * H : (e + 1) * H].astype(BF)


def run_down(grads_own, grads_sib, own, rows_sib):
    tile = pl.BlockSpec((HALF, 2 * FT), lambda i: (0, i))
    whole = pl.BlockSpec((HALF, 768), lambda i: (0, 0))
    tail = pl.BlockSpec((HALF, 768), lambda i: (0, D // 768))
    return pl.pallas_call(
        down_kernel,
        grid=(D // FT // 2,),
        out_shape=[
            jax.ShapeDtypeStruct((2, H, D), BF),
            jax.ShapeDtypeStruct((8, 128), F32),
        ],
        in_specs=[tile, tile, whole, tail],
        out_specs=[
            pl.BlockSpec((2, H, 2 * FT), lambda i: (0, 0, i)),
            pl.BlockSpec((8, 128), lambda i: (0, 0)),
        ],
        scratch_shapes=[pltpu.VMEM((256, 512), BF)],
        compiler_params=pltpu.CompilerParams(
            dimension_semantics=("arbitrary",), vmem_limit_bytes=16 * MIB
        ),
        cost_estimate=pl.CostEstimate(
            flops=1_600_000_000, bytes_accessed=10_000_000, transcendentals=0
        ),
        name="down_grads",
    )(grads_own, grads_sib, own, rows_sib)


def first_sum_kernel(where, *refs):
    ra, rb, qa, qb, buf = refs[0:4], refs[4:8], refs[9:13], refs[13:17], refs[17]
    half = D // 2
    buf[...] = total(ra[0][:, 0:half], [r[:, 0:half] for r in ra[1:]]).astype(BF)
    sums = join_three(ra[0][0:16, half:])
    for r in ra[1:]:
        sums += join_three(r[0:16, half:])
    sums = split_three(sums)
    for k in range(NY):
        start = pl.multiple_of(((where[1] + k) % NY) * 16, 16)
        qa[k][:, 0:half] = buf[pl.ds(start, 16), :]
        qa[k][:, half:] = sums
    for k in range(NX):
        qb[k][...] = total(rb[0][k], [r[k] for r in rb[1:]]).astype(BF)


def run_first_sum(where, ra, rb, token):
    return pl.pallas_call(
        first_sum_kernel,
        out_shape=[jax.ShapeDtypeStruct((16, WIDE), BF)] * 4
        + [jax.ShapeDtypeStruct((16, D // 2), BF)] * 4,
        in_specs=[SMEM_SPEC] + vmem_specs(9),
        out_specs=vmem_specs(8),
        scratch_shapes=[pltpu.VMEM((64, D // 2), BF)],
        compiler_params=pltpu.CompilerParams(vmem_limit_bytes=8 * MIB),
        name="first_sum",
    )(where, *ra, *rb, token)


def second_sum_kernel(where, *refs):
    ra, rb, own, out, buf = refs[0:4], refs[4:8], refs[9], refs[10:13], refs[13]
    half = D // 2
    for n, r in enumerate((ra, rb)):
        part = total(r[0][:, 0:half], [p[:, 0:half] for p in r[1:]])
        for k in range(NZ):
            buf[k, :, n * half : (n + 1) * half] = part[4 * k : 4 * k + 4]
    sums = join_three(ra[0][:, half:])
    for r in ra[1:]:
        sums += join_three(r[:, half:])
    parts = split_three(sums)[0:4]
    for k in range(NZ):
        rows = buf[(where[2] + k) % NZ]
        if k == 0:
            own[:, 0:D] = rows
            own[:, D:] = sums[0:4]
        else:
            out[k - 1][:, 0:D] = rows.astype(BF)
            out[k - 1][:, D:] = parts


def run_second_sum(where, ra, rb, token):
    return pl.pallas_call(
        second_sum_kernel,
        out_shape=[jax.ShapeDtypeStruct((4, D + 128), F32)]
        + [jax.ShapeDtypeStruct((4, D + 384), BF)] * 3,
        in_specs=[SMEM_SPEC] + vmem_specs(9),
        out_specs=vmem_specs(4),
        scratch_shapes=[pltpu.VMEM((NZ, 4, D), F32)],
        compiler_params=pltpu.CompilerParams(vmem_limit_bytes=8 * MIB),
        name="second_sum",
    )(where, *ra, *rb, token)


def last_sum_kernel(own, *refs):
    out, sums_out = refs[3], refs[4]
    out[...] = total(own[:, 0:D], [r[:, 0:D] for r in refs[0:3]]).astype(BF)
    sums = own[:, D:]
    for r in refs[0:3]:
        sums += join_three(r[:, D:])
    sums_out[0:4, :] = sums
    sums_out[4:8, :] = jnp.zeros((4, 128), F32)


def run_last_sum(pieces):
    return pl.pallas_call(
        last_sum_kernel,
        out_shape=[jax.ShapeDtypeStruct((4, D), BF), jax.ShapeDtypeStruct((8, 128), F32)],
        in_specs=vmem_specs(4),
        out_specs=vmem_specs(2),
        compiler_params=pltpu.CompilerParams(vmem_limit_bytes=4 * MIB),
        name="last_sum",
    )(*pieces)


def router_kernel(where, own, other, slots_ref, out):
    first = jnp.where(where[4] == 0, own[...], other[...])
    second = jnp.where(where[4] == 0, other[...], own[...])
    slots = slots_ref[...].T
    index = lax.broadcasted_iota(jnp.int32, (256, 128), 1)
    spread = jnp.zeros((256, 128), F32)
    for e in range(2):
        picked = jnp.zeros((256, 1), F32)
        for core, values in enumerate((first, second)):
            for h in range(2):
                at = index + h * 128
                token = (at // 64) * 128 + core * 64 + at % 64
                hit = slots[:, e : e + 1] == token
                line = jnp.broadcast_to(values[2 * e + h : 2 * e + h + 1, :], (256, 128))
                picked += jnp.sum(jnp.where(hit, line, 0.0), axis=1, keepdims=True)
        spread = jnp.where(index == e, picked, spread)
    lines = spread.T
    at = lax.broadcasted_iota(jnp.int32, (1, 256), 1)
    for e in range(2):
        out[e : e + 1, :] = jnp.where(at < where[5 + e], lines[e : e + 1, :], 0.0)


def run_router(where, own, other, slots):
    return pl.pallas_call(
        router_kernel,
        out_shape=jax.ShapeDtypeStruct((2, 256), F32),
        in_specs=[SMEM_SPEC] + vmem_specs(3),
        out_specs=vmem_specs(1)[0],
        compiler_params=pltpu.CompilerParams(vmem_limit_bytes=4 * MIB),
        name="router",
    )(where, own, other, slots)


def on_device(
    tokens_in, out_grad, gate_weight, up_weight, down_weight, slot_tokens, slot_counts, slot_gates
):
    x, c, y, z = position()
    where = jnp.stack([x, y, z, c, c, slot_counts[0], slot_counts[1]]).astype(jnp.int32)
    gates, ups = (lax.all_gather(w, "core", axis=0) for w in (gate_weight, up_weight))

    packed = run_pack(tokens_in, out_grad)
    t16, g64 = run_first_stage(where, [packed] + [shift(packed, "z", k) for k in (1, 2, 3)])
    t = [t16] + [shift(t16, "y", k) for k in (1, 2, 3)]
    g = [g64] + [shift(g64, "x", k) for k in (1, 2, 3)]
    down_sib = swap(down_weight)
    t64, g256 = run_second_stage(where, t, g, [])
    t_low, t_high = shift(t64, "x", 1), shift(t64, "x", -1)
    g_low, g_high = shift(g256, "y", 1), shift(g256, "y", -1)
    a, b, e, f = run_halves(t_low, t_high, g_low, g_high)
    t = (t64, t_low, t_high, shift(a, "x", 1), shift(b, "x", -1))
    g = (g256, g_low, g_high, shift(e, "y", 1), shift(f, "y", -1))
    weights = (gate_weight, up_weight, down_weight, gates, ups, down_sib)
    outs = run_main(where, t, g, weights, slot_tokens, slot_gates)
    pa, pb = outs[0:4], outs[4:8]
    dl_own, rows, grads = outs[8:]

    ra = [pa[0]] + [shift(pa[k], "x", -k) for k in (1, 2, 3)]
    rb = [pb[0]] + [shift(pb[k], "y", k) for k in (1, 2, 3)]
    rows_sib = swap(rows)
    before = [ra[1], ra[3], rb[1], rb[3]]
    grads_sib = swap(run_relay(grads, before))
    gate_grad, up_grad, token = run_up(rows, rows_sib, dl_own, before)
    q = run_first_sum(where, ra, rb, token)
    qa, qb = q[0:4], q[4:8]
    ra = [qa[0]] + [shift(qa[k], "y", k) for k in (1, 2, 3)]
    rb = [qb[0]] + [shift(qb[k], "x", -k) for k in (1, 2, 3)]
    down_grad, token = run_down(grads, grads_sib, dl_own, rows_sib)
    q = run_second_sum(where, ra, rb, token)
    input_grad, sums = run_last_sum([q[0]] + [shift(q[k], "z", k) for k in (1, 2, 3)])
    router_grad = run_router(where, sums, swap(sums), slot_tokens)
    return (input_grad, gate_grad, up_grad, down_grad, router_grad)


def solution(mesh):
    by_axis = jax.sharding.Mesh(mesh.devices.reshape(NX, NC, NY, NZ), AXES)
    section, et = AXES[0:2], AXES[2:4]
    return jax.shard_map(
        on_device,
        mesh=by_axis,
        in_specs=(
            P(AXES, None),
            P(section, et),
            P(None, None, AXES),
            P(None, None, AXES),
            P(None, AXES, None),
            P(),
            P(),
            P(),
        ),
        out_specs=(P(AXES, None), P(None, None, AXES), P(None, None, AXES), P(None, AXES, None), P()),
        check_vma=False,
    )
```

```python
import jax
import jax.numpy as jnp
from jax import lax
from jax.experimental import pallas as pl
from jax.experimental.pallas import tpu as pltpu
from jax.sharding import PartitionSpec as P

AXES = ("section", "et")
BF = jnp.bfloat16
F32 = jnp.float32
D = 6144
NX, NC, NY, NZ = 4, 2, 4, 4
H = 128
SHORT = 64
HALF = 256


def linear(x, c, y, z):
    return ((x * NC + c) * NY + y) * NZ + z


def shift_pairs(axis, step):
    pairs = []
    for x in range(NX):
        for c in range(NC):
            for y in range(NY):
                for z in range(NZ):
                    to = {
                        "x": ((x + step) % NX, c, y, z),
                        "y": (x, c, (y + step) % NY, z),
                        "z": (x, c, y, (z + step) % NZ),
                    }[axis]
                    pairs.append((linear(x, c, y, z), linear(*to)))
    return pairs


def shift(value, axis, step):
    return lax.ppermute(value, AXES, shift_pairs(axis, step))


def swap(value):
    pairs = [
        (linear(x, c, y, z), linear(x, 1 - c, y, z))
        for x in range(NX)
        for c in range(NC)
        for y in range(NY)
        for z in range(NZ)
    ]
    return lax.ppermute(value, AXES, pairs)


def position():
    section = lax.axis_index("section")
    et = lax.axis_index("et")
    return section // NC, section % NC, et // NZ, et % NZ


def nt(left, right):
    return lax.dot_general(left, right, (((1,), (1,)), ((), ())), preferred_element_type=F32)


def tn(left, right):
    return lax.dot_general(left, right, (((0,), (0,)), ((), ())), preferred_element_type=F32)


def total(first, rest):
    out = first.astype(F32)
    for r in rest:
        out = out + r.astype(F32)
    return out


KT = 1024
FT = 512
MIB = 2**20
WIDE = D // 2 + 384


def vmem_specs(n):
    return [pl.BlockSpec(memory_space=pltpu.VMEM)] * n


SMEM_SPEC = pl.BlockSpec(memory_space=pltpu.SMEM)


def pack_kernel(tokens, grads, out):
    out[0:64, :] = grads[...]
    rows = tokens[...].astype(F32)
    for b in range(0, 16, 4):
        four = [rows[:, (b + i) * 384 : (b + i + 1) * 384] for i in range(4)]
        out[64 + 4 * b : 80 + 4 * b, :] = jnp.concatenate(four, axis=0).astype(BF)


def run_pack(tokens, grads):
    return pl.pallas_call(
        pack_kernel,
        out_shape=jax.ShapeDtypeStruct((128, 384), BF),
        in_specs=vmem_specs(2),
        out_specs=vmem_specs(1)[0],
        compiler_params=pltpu.CompilerParams(vmem_limit_bytes=4 * MIB),
        name="pack",
    )(tokens, grads)


def first_stage_kernel(where, *refs):
    packed, t_out, g_out, buf = refs[0:4], refs[4], refs[5], refs[6]
    for k in range(NZ):
        at = (where[2] - k) % NZ
        rows = packed[k][64:128, :].astype(F32)
        for b in range(16):
            buf[at, :, 384 * b : 384 * (b + 1)] = rows[4 * b : 4 * b + 4]
        start = pl.multiple_of(384 * at, 128)
        g_out[:, pl.ds(start, 384)] = packed[k][0:64, :]
    t_out[...] = jnp.concatenate([buf[k] for k in range(NZ)], axis=0).astype(BF)


def run_first_stage(where, packed):
    return pl.pallas_call(
        first_stage_kernel,
        out_shape=[jax.ShapeDtypeStruct((16, D), BF), jax.ShapeDtypeStruct((64, 1536), BF)],
        in_specs=[SMEM_SPEC] + vmem_specs(4),
        out_specs=vmem_specs(2),
        scratch_shapes=[pltpu.VMEM((NZ, 4, D), F32)],
        compiler_params=pltpu.CompilerParams(vmem_limit_bytes=4 * MIB),
        name="first_stage",
    )(where, *packed)


def second_stage_kernel(where, *refs):
    t, g, t_out, g_out = refs[0:4], refs[4:8], refs[-2], refs[-1]
    for k in range(NY):
        start = pl.multiple_of(16 * ((where[1] - k) % NY), 16)
        t_out[pl.ds(start, 16), :] = t[k][...]
    for k in range(NX):
        g_out[k * 64 : (k + 1) * 64, :] = g[k][...]


def run_second_stage(where, t, g, before):
    return pl.pallas_call(
        second_stage_kernel,
        out_shape=[jax.ShapeDtypeStruct((64, D), BF), jax.ShapeDtypeStruct((HALF, 1536), BF)],
        in_specs=[SMEM_SPEC] + vmem_specs(8) + [pl.BlockSpec(memory_space=pl.ANY)] * len(before),
        out_specs=vmem_specs(2),
        compiler_params=pltpu.CompilerParams(vmem_limit_bytes=4 * MIB),
        name="second_stage",
    )(where, *t, *g, *before)


def halves_kernel(t_low, t_high, g_low, g_high, a, b, c, d):
    a[...] = t_low[0:32, :]
    b[...] = t_high[32:64, :]
    c[...] = g_low[0:128, :]
    d[...] = g_high[128:256, :]


def run_halves(t_low, t_high, g_low, g_high):
    return pl.pallas_call(
        halves_kernel,
        out_shape=[jax.ShapeDtypeStruct((32, D), BF)] * 2
        + [jax.ShapeDtypeStruct((128, 1536), BF)] * 2,
        in_specs=vmem_specs(4),
        out_specs=vmem_specs(4),
        compiler_params=pltpu.CompilerParams(vmem_limit_bytes=4 * MIB),
        name="halves",
    )(t_low, t_high, g_low, g_high)


def relay_kernel(*refs):
    value, (out, sem) = refs[0], refs[-2:]
    copy = pltpu.make_async_copy(value, out, sem)
    copy.start()
    copy.wait()


def run_relay(value, before):
    hbm = [pl.BlockSpec(memory_space=pltpu.HBM)]
    return pl.pallas_call(
        relay_kernel,
        out_shape=jax.ShapeDtypeStruct(value.shape, value.dtype),
        in_specs=hbm * (1 + len(before)),
        out_specs=hbm[0],
        scratch_shapes=[pltpu.SemaphoreType.DMA],
        compiler_params=pltpu.CompilerParams(vmem_limit_bytes=1 * MIB),
        cost_estimate=pl.CostEstimate(flops=0, bytes_accessed=6_000_000, transcendentals=0),
        name="relay",
    )(value, *before)


def row_copies(pieces, rows, sem):
    places = (0, 64, 192, 128, 160)
    return [
        pltpu.make_async_copy(piece, rows.at[pl.ds(at, piece.shape[0]), :], sem.at[r])
        for r, (piece, at) in enumerate(zip(pieces, places))
    ]


def grad_copies(pieces, grads, sem, y):
    places = ((0, 0), (-1, 0), (1, 0), (2, 0), (2, 128))
    copies = []
    for j, (piece, (step, at)) in enumerate(zip(pieces, places)):
        start = pl.multiple_of(((y + step + NY) % NY) * 1536, 128)
        copies.append(
            pltpu.make_async_copy(
                piece, grads.at[pl.ds(at, piece.shape[0]), pl.ds(start, 1536)], sem.at[j]
            )
        )
    return copies


def split_three(value):
    high = value.astype(BF)
    rest = value - high.astype(F32)
    middle = rest.astype(BF)
    low = (rest - middle.astype(F32)).astype(BF)
    return jnp.concatenate([high, middle, low], axis=1)


def join_three(parts):
    out = parts.astype(F32)
    return out[:, 0:128] + out[:, 128:256] + out[:, 256:384]


def early_kernel(where, *refs):
    t, g, weights = refs[0:3], refs[3:6], (refs[6:9], refs[9:12])
    acc_g, acc_b, wv, dv, sem_w, sem_d = refs[12:18]
    y = where[1]
    tiles = D // KT

    def wide_copies(i):
        k = pl.ds(pl.multiple_of(i * KT, KT), KT)
        return [
            pltpu.make_async_copy(
                weights[s][n].at[:, k, :], wv.at[s, n, :, k, :], sem_w.at[i, s * 2 + n]
            )
            for s in range(2)
            for n in range(2)
        ]

    tall_copies = []
    for j, step in enumerate((0, -1, 1)):
        block = pl.ds(pl.multiple_of(((y + step + NY) % NY) * 1536, 128), 1536)
        tall_copies.append(
            [
                pltpu.make_async_copy(weights[s][2].at[:, :, block], dv.at[j, s], sem_d.at[j, s])
                for s in range(2)
            ]
        )
    for i in range(tiles):
        for copy in wide_copies(i):
            copy.start()
    for group in tall_copies:
        for copy in group:
            copy.start()
    acc_g[...] = jnp.zeros(acc_g.shape, F32)
    acc_b[...] = jnp.zeros(acc_b.shape, F32)

    @pl.loop(0, tiles)
    def _(i):
        for copy in wide_copies(i):
            copy.wait()
        k = pl.ds(pl.multiple_of(i * KT, KT), KT)
        wide = jnp.concatenate(
            [wv[s, n, e, k, :] for s in range(2) for e in range(2) for n in range(2)], axis=1
        )
        rows = jnp.concatenate([piece[:, k] for piece in t], axis=0)
        acc_g[...] += jnp.dot(rows, wide, preferred_element_type=F32)

    for j, group in enumerate(tall_copies):
        for copy in group:
            copy.wait()
        tall = jnp.concatenate([dv[j, s, e] for s in range(2) for e in range(2)], axis=0)
        acc_b[...] += nt(g[j][...], tall)


def run_early(where, t, g, weights):
    hbm = [pl.BlockSpec(memory_space=pltpu.HBM)]
    return pl.pallas_call(
        early_kernel,
        out_shape=[
            jax.ShapeDtypeStruct((192, 1024), F32),
            jax.ShapeDtypeStruct((HALF, 512), F32),
        ],
        in_specs=[SMEM_SPEC] + vmem_specs(6) + hbm * 6,
        out_specs=vmem_specs(2),
        scratch_shapes=[
            pltpu.VMEM((2, 2, 2, D, H), BF),
            pltpu.VMEM((3, 2, 2, H, 1536), BF),
            pltpu.SemaphoreType.DMA((D // KT, 4)),
            pltpu.SemaphoreType.DMA((3, 2)),
        ],
        compiler_params=pltpu.CompilerParams(vmem_limit_bytes=30 * MIB),
        cost_estimate=pl.CostEstimate(
            flops=3_600_000_000, bytes_accessed=20_000_000, transcendentals=0
        ),
        name="early",
    )(where, *t, *g, *weights)


def main_kernel(where, *refs):
    t_in, g_in = refs[0:5], refs[5:10]
    weights = (refs[10:13], refs[13:16])
    slots_ref, gates_ref, early_g, early_b = refs[16:20]
    pa_out, pb_out = refs[20:25], refs[25:30]
    own_out, rows_out, grads_out = refs[30:33]
    rows, grads, wv, dv, pa, pb = refs[33:39]
    acc_g, acc_b, deltas, tile, rbuf, packed = refs[39:45]
    sem_t, sem_g, sem_w, sem_d, sem_o = refs[45:50]
    x, y, core = where[0], where[1], where[4]
    copies_t = row_copies(t_in, rows, sem_t)
    copies_g = grad_copies(g_in, grads, sem_g, y)
    tiles = D // KT

    def wide_copies(i):
        k = pl.ds(pl.multiple_of(i * KT, KT), KT)
        return [
            pltpu.make_async_copy(
                weights[s][n].at[:, k, :], wv.at[s, n, :, k, :], sem_w.at[i, s * 2 + n]
            )
            for s in range(2)
            for n in range(2)
        ]

    far = pl.ds(pl.multiple_of(((y + 2) % NY) * 1536, 128), 1536)
    tall_copies = [
        pltpu.make_async_copy(weights[s][2].at[:, :, far], dv.at[s], sem_d.at[s]) for s in range(2)
    ]
    for copy in copies_t:
        copy.start()
    for i in range(tiles):
        for copy in wide_copies(i):
            copy.start()
    for copy in copies_g + tall_copies:
        copy.start()
    acc_g[0:128, :] = early_g[0:128, :]
    acc_g[128:192, :] = jnp.zeros((64, 1024), F32)
    acc_g[192:256, :] = early_g[128:192, :]
    scales = []
    slot = lax.broadcasted_iota(jnp.int32, (HALF, 256), 1)
    row = lax.broadcasted_iota(jnp.int32, (HALF, 256), 0)
    block = row // 64
    token = ((x - block + NX) % NX) * 128 + core * 64 + (row - block * 64)
    for e in range(2):
        hit = (token == slots_ref[e : e + 1, :]) & (slot < where[5 + e])
        gate = jnp.broadcast_to(gates_ref[e : e + 1, :], (HALF, 256))
        scales.append(jnp.sum(jnp.where(hit, gate, 0.0), axis=1, keepdims=True))
    for copy in copies_t:
        copy.wait()
    rows_copy = pltpu.make_async_copy(rows, rows_out.at[:, pl.ds(0, D)], sem_o.at[0])
    grads_copy = pltpu.make_async_copy(grads, grads_out, sem_o.at[1])

    @pl.loop(0, tiles)
    def _(i):
        for copy in wide_copies(i):
            copy.wait()
        k = pl.ds(pl.multiple_of(i * KT, KT), KT)
        wide = jnp.concatenate(
            [wv[s, n, e, k, :] for s in range(2) for e in range(2) for n in range(2)], axis=1
        )
        acc_g[128:192, :] += jnp.dot(rows[128:192, k], wide, preferred_element_type=F32)

    for copy in copies_g + tall_copies:
        copy.wait()
    tall = jnp.concatenate([dv[s, e] for s in range(2) for e in range(2)], axis=0)
    acc_b[...] = early_b[...] + nt(grads[:, far], tall)
    rows_copy.start()
    grads_copy.start()
    router = [0.0, 0.0]
    for s in range(2):
        for e in range(2):
            j = s * 2 + e
            pre_gate = acc_g[:, j * 256 : j * 256 + H]
            pre_up = acc_g[:, j * 256 + H : (j + 1) * 256]
            back = acc_b[:, j * H : (j + 1) * H]
            scale = scales[e]
            sigma = jax.nn.sigmoid(pre_gate)
            active = pre_gate * sigma
            hidden = active * pre_up
            router[e] += jnp.sum(hidden.astype(BF).astype(F32) * back, axis=1, keepdims=True)
            hidden_grad = back * scale
            gate_delta = (hidden_grad * pre_up * sigma * (1.0 + pre_gate * (1.0 - sigma))).astype(BF)
            up_delta = (hidden_grad * active).astype(BF)
            deltas[:, j * 256 : j * 256 + H] = gate_delta
            deltas[:, j * 256 + H : (j + 1) * 256] = up_delta
            packed[s, :, e * 256 : e * 256 + H] = gate_delta
            packed[s, :, e * 256 + H : (e + 1) * 256] = up_delta
            packed[s, :, 512 + e * H : 512 + (e + 1) * H] = (hidden * scale).astype(BF)
    own_copy = pltpu.make_async_copy(packed.at[0], own_out, sem_o.at[2])
    sib_copy = pltpu.make_async_copy(packed.at[1], rows_out.at[:, pl.ds(D, 768)], sem_o.at[3])
    own_copy.start()
    sib_copy.start()
    lane = lax.broadcasted_iota(jnp.int32, (HALF, 128), 1)
    spread = jnp.where(lane == 0, router[0], jnp.where(lane == 1, router[1], 0.0))
    for k in range(NX):
        to = pl.multiple_of(((x - k) % NX) * 64, 64)
        rbuf[pl.ds(to, 64), :] = spread[k * 64 : (k + 1) * 64]
    line = rbuf[...].T[0:2]
    four = [line[e : e + 1, h * 128 : (h + 1) * 128] for e in range(2) for h in range(2)]
    sums = split_three(jnp.concatenate(four + [jnp.zeros((12, 128), F32)], axis=0))
    for k in range(NX):
        pa[k, :, D // 2 :] = jnp.zeros((64, 384), BF)
        pa[k, 0:16, D // 2 :] = sums

    def partial(i):
        f = pl.ds(pl.multiple_of(i * FT, FT), FT)
        wide = jnp.concatenate(
            [wv[s, n, e, f, :] for s in range(2) for e in range(2) for n in range(2)], axis=1
        )
        return nt(deltas[...], wide)

    half = D // 2 // FT

    @pl.loop(0, half)
    def _(i):
        f = pl.ds(pl.multiple_of(i * FT, FT), FT)
        part = partial(i).astype(BF)
        for k in range(NX):
            pa[k, :, f] = part[k * 64 : (k + 1) * 64, :]

    parts = (pa.at[0], pa.at[1], pa.at[3], pa.at[2, pl.ds(0, 32), :], pa.at[2, pl.ds(32, 32), :])
    copies = [
        pltpu.make_async_copy(part, pa_out[k], sem_o.at[4 + k]) for k, part in enumerate(parts)
    ]
    for copy in copies:
        copy.start()

    @pl.loop(0, half)
    def _(i):
        f = pl.ds(pl.multiple_of(i * FT, FT), FT)
        tile[...] = partial(i + half).astype(BF)
        for k in range(NY):
            for b in range(NX):
                src = pl.multiple_of(b * 64 + ((y + k) % NY) * 16, 16)
                pb[k, b, :, f] = tile[pl.ds(src, 16), :]

    parts = (pb.at[0], pb.at[1], pb.at[3], pb.at[2, pl.ds(0, 2)], pb.at[2, pl.ds(2, 2)])
    more = [
        pltpu.make_async_copy(part, pb_out[k], sem_o.at[9 + k]) for k, part in enumerate(parts)
    ]
    for copy in more:
        copy.start()
    for copy in [rows_copy, grads_copy, own_copy, sib_copy] + copies + more:
        copy.wait()


def run_main(where, t, g, weights, slots, gates, early):
    hbm = [pl.BlockSpec(memory_space=pltpu.HBM)]
    out_shape = (
        [jax.ShapeDtypeStruct((64, WIDE), BF)] * 3
        + [jax.ShapeDtypeStruct((32, WIDE), BF)] * 2
        + [jax.ShapeDtypeStruct((4, 16, D // 2), BF)] * 3
        + [jax.ShapeDtypeStruct((2, 16, D // 2), BF)] * 2
        + [jax.ShapeDtypeStruct((HALF, 768), BF)]
        + [jax.ShapeDtypeStruct((HALF, D + 768), BF)]
        + [jax.ShapeDtypeStruct((HALF, D), BF)]
    )
    return pl.pallas_call(
        main_kernel,
        out_shape=out_shape,
        in_specs=[SMEM_SPEC] + hbm * 16 + vmem_specs(4),
        out_specs=hbm * 13,
        scratch_shapes=[
            pltpu.VMEM((HALF, D), BF),
            pltpu.VMEM((HALF, D), BF),
            pltpu.VMEM((2, 2, 2, D, H), BF),
            pltpu.VMEM((2, 2, H, 1536), BF),
            pltpu.VMEM((4, 64, WIDE), BF),
            pltpu.VMEM((4, 4, 16, D // 2), BF),
            pltpu.VMEM((HALF, 1024), F32),
            pltpu.VMEM((HALF, 512), F32),
            pltpu.VMEM((HALF, 1024), BF),
            pltpu.VMEM((HALF, FT), BF),
            pltpu.VMEM((HALF, 128), F32),
            pltpu.VMEM((2, HALF, 768), BF),
            pltpu.SemaphoreType.DMA((5,)),
            pltpu.SemaphoreType.DMA((5,)),
            pltpu.SemaphoreType.DMA((D // KT, 4)),
            pltpu.SemaphoreType.DMA((2,)),
            pltpu.SemaphoreType.DMA((14,)),
        ],
        compiler_params=pltpu.CompilerParams(vmem_limit_bytes=38 * MIB),
        cost_estimate=pl.CostEstimate(
            flops=8_000_000_000, bytes_accessed=30_000_000, transcendentals=262144
        ),
        name="main",
    )(where, *t, *g, *weights, slots, gates, *early)


def up_kernel(*refs):
    rows_own, rows_sib, own, sib = refs[0:4]
    gate_out, up_out, token = refs[-3:]
    token[...] = jnp.zeros(token.shape, F32)
    part = tn(rows_own[...], own[:, 0:512]) + tn(rows_sib[...], sib[:, 0:512])
    for e in range(2):
        gate_out[e] = part[:, e * 256 : e * 256 + H].astype(BF)
        up_out[e] = part[:, e * 256 + H : (e + 1) * 256].astype(BF)


def run_up(rows_own, rows_sib, own, before):
    tile = pl.BlockSpec((HALF, FT), lambda i: (0, i))
    whole = pl.BlockSpec((HALF, 768), lambda i: (0, 0))
    tail = pl.BlockSpec((HALF, 768), lambda i: (0, D // 768))
    out = pl.BlockSpec((2, FT, H), lambda i: (0, i, 0))
    return pl.pallas_call(
        up_kernel,
        grid=(D // FT,),
        out_shape=[
            jax.ShapeDtypeStruct((2, D, H), BF),
            jax.ShapeDtypeStruct((2, D, H), BF),
            jax.ShapeDtypeStruct((8, 128), F32),
        ],
        in_specs=[tile, tile, whole, tail]
        + [pl.BlockSpec(memory_space=pl.ANY)] * len(before),
        out_specs=[out, out, pl.BlockSpec((8, 128), lambda i: (0, 0))],
        compiler_params=pltpu.CompilerParams(
            dimension_semantics=("arbitrary",), vmem_limit_bytes=16 * MIB
        ),
        cost_estimate=pl.CostEstimate(
            flops=3_200_000_000, bytes_accessed=13_000_000, transcendentals=0
        ),
        name="up_grads",
    )(rows_own, rows_sib, own, rows_sib, *before)


def down_kernel(grads_own, grads_sib, own, sib, out, token, hidden):
    token[...] = jnp.zeros(token.shape, F32)

    @pl.when(pl.program_id(0) == 0)
    def _():
        hidden[:, 0:HALF] = own[:, 512:768].T
        hidden[:, HALF:512] = sib[:, 512:768].T

    part = jnp.dot(hidden[:, 0:HALF], grads_own[...], preferred_element_type=F32)
    part += jnp.dot(hidden[:, HALF:512], grads_sib[...], preferred_element_type=F32)
    for e in range(2):
        out[e] = part[e * H : (e + 1) * H].astype(BF)


def run_down(grads_own, grads_sib, own, rows_sib):
    tile = pl.BlockSpec((HALF, 2 * FT), lambda i: (0, i))
    whole = pl.BlockSpec((HALF, 768), lambda i: (0, 0))
    tail = pl.BlockSpec((HALF, 768), lambda i: (0, D // 768))
    return pl.pallas_call(
        down_kernel,
        grid=(D // FT // 2,),
        out_shape=[
            jax.ShapeDtypeStruct((2, H, D), BF),
            jax.ShapeDtypeStruct((8, 128), F32),
        ],
        in_specs=[tile, tile, whole, tail],
        out_specs=[
            pl.BlockSpec((2, H, 2 * FT), lambda i: (0, 0, i)),
            pl.BlockSpec((8, 128), lambda i: (0, 0)),
        ],
        scratch_shapes=[pltpu.VMEM((256, 512), BF)],
        compiler_params=pltpu.CompilerParams(
            dimension_semantics=("arbitrary",), vmem_limit_bytes=16 * MIB
        ),
        cost_estimate=pl.CostEstimate(
            flops=1_600_000_000, bytes_accessed=10_000_000, transcendentals=0
        ),
        name="down_grads",
    )(grads_own, grads_sib, own, rows_sib)


def middle_sum_kernel(*refs):
    a_down, a_up, b_up, b_down = refs[0:4]
    low_a, high_a, low_b, high_b = refs[4:8]
    out_a_down, out_a_up, out_b_up, out_b_down = refs[8:12]
    half = D // 2
    out_a_down[0:32, 0:half] = total(a_down[0:32, 0:half], [low_a[:, 0:half]]).astype(BF)
    out_a_down[32:64, :] = a_down[32:64, :]
    sums = join_three(a_down[0:16, half:]) + join_three(low_a[0:16, half:])
    out_a_down[0:16, half:] = split_three(sums)
    out_a_down[16:32, half:] = a_down[16:32, half:]
    out_a_up[0:32, :] = a_up[0:32, :]
    out_a_up[32:64, :] = total(a_up[32:64, :], [high_a[...]]).astype(BF)
    for k in range(2):
        out_b_up[k] = total(b_up[k], [low_b[k]]).astype(BF)
        out_b_up[2 + k] = b_up[2 + k]
        out_b_down[k] = b_down[k]
        out_b_down[2 + k] = total(b_down[2 + k], [high_b[k]]).astype(BF)


def run_middle_sum(blocks, halves):
    return pl.pallas_call(
        middle_sum_kernel,
        out_shape=[jax.ShapeDtypeStruct((64, WIDE), BF)] * 2
        + [jax.ShapeDtypeStruct((4, 16, D // 2), BF)] * 2,
        in_specs=vmem_specs(8),
        out_specs=vmem_specs(4),
        compiler_params=pltpu.CompilerParams(vmem_limit_bytes=8 * MIB),
        name="middle_sum",
    )(*blocks, *halves)


def first_sum_kernel(where, *refs):
    ra, rb, qa, qb, buf = refs[0:3], refs[3:6], refs[7:11], refs[11:15], refs[15]
    half = D // 2
    buf[...] = total(ra[0][:, 0:half], [r[:, 0:half] for r in ra[1:]]).astype(BF)
    sums = join_three(ra[0][0:16, half:])
    for r in ra[1:]:
        sums += join_three(r[0:16, half:])
    sums = split_three(sums)
    for k in range(NY):
        start = pl.multiple_of(((where[1] + k) % NY) * 16, 16)
        qa[k][:, 0:half] = buf[pl.ds(start, 16), :]
        qa[k][:, half:] = sums
    for k in range(NX):
        qb[k][...] = total(rb[0][k], [r[k] for r in rb[1:]]).astype(BF)


def run_first_sum(where, ra, rb, token):
    return pl.pallas_call(
        first_sum_kernel,
        out_shape=[jax.ShapeDtypeStruct((16, WIDE), BF)] * 4
        + [jax.ShapeDtypeStruct((16, D // 2), BF)] * 4,
        in_specs=[SMEM_SPEC] + vmem_specs(7),
        out_specs=vmem_specs(8),
        scratch_shapes=[pltpu.VMEM((64, D // 2), BF)],
        compiler_params=pltpu.CompilerParams(vmem_limit_bytes=8 * MIB),
        name="first_sum",
    )(where, *ra, *rb, token)


def second_sum_kernel(where, *refs):
    ra, rb, own, out, buf = refs[0:4], refs[4:8], refs[9], refs[10:13], refs[13]
    half = D // 2
    for n, r in enumerate((ra, rb)):
        part = total(r[0][:, 0:half], [p[:, 0:half] for p in r[1:]])
        for k in range(NZ):
            buf[k, :, n * half : (n + 1) * half] = part[4 * k : 4 * k + 4]
    sums = join_three(ra[0][:, half:])
    for r in ra[1:]:
        sums += join_three(r[:, half:])
    parts = split_three(sums)[0:4]
    for k in range(NZ):
        rows = buf[(where[2] + k) % NZ]
        if k == 0:
            own[:, 0:D] = rows
            own[:, D:] = sums[0:4]
        else:
            out[k - 1][:, 0:D] = rows.astype(BF)
            out[k - 1][:, D:] = parts


def run_second_sum(where, ra, rb, token):
    return pl.pallas_call(
        second_sum_kernel,
        out_shape=[jax.ShapeDtypeStruct((4, D + 128), F32)]
        + [jax.ShapeDtypeStruct((4, D + 384), BF)] * 3,
        in_specs=[SMEM_SPEC] + vmem_specs(9),
        out_specs=vmem_specs(4),
        scratch_shapes=[pltpu.VMEM((NZ, 4, D), F32)],
        compiler_params=pltpu.CompilerParams(vmem_limit_bytes=8 * MIB),
        name="second_sum",
    )(where, *ra, *rb, token)


def last_sum_kernel(own, *refs):
    out, sums_out = refs[3], refs[4]
    out[...] = total(own[:, 0:D], [r[:, 0:D] for r in refs[0:3]]).astype(BF)
    sums = own[:, D:]
    for r in refs[0:3]:
        sums += join_three(r[:, D:])
    sums_out[0:4, :] = sums
    sums_out[4:8, :] = jnp.zeros((4, 128), F32)


def run_last_sum(pieces):
    return pl.pallas_call(
        last_sum_kernel,
        out_shape=[jax.ShapeDtypeStruct((4, D), BF), jax.ShapeDtypeStruct((8, 128), F32)],
        in_specs=vmem_specs(4),
        out_specs=vmem_specs(2),
        compiler_params=pltpu.CompilerParams(vmem_limit_bytes=4 * MIB),
        name="last_sum",
    )(*pieces)


def router_kernel(where, own, other, slots_ref, out):
    first = jnp.where(where[4] == 0, own[...], other[...])
    second = jnp.where(where[4] == 0, other[...], own[...])
    slots = slots_ref[...].T
    index = lax.broadcasted_iota(jnp.int32, (256, 128), 1)
    spread = jnp.zeros((256, 128), F32)
    for e in range(2):
        picked = jnp.zeros((256, 1), F32)
        for core, values in enumerate((first, second)):
            for h in range(2):
                at = index + h * 128
                token = (at // 64) * 128 + core * 64 + at % 64
                hit = slots[:, e : e + 1] == token
                line = jnp.broadcast_to(values[2 * e + h : 2 * e + h + 1, :], (256, 128))
                picked += jnp.sum(jnp.where(hit, line, 0.0), axis=1, keepdims=True)
        spread = jnp.where(index == e, picked, spread)
    lines = spread.T
    at = lax.broadcasted_iota(jnp.int32, (1, 256), 1)
    for e in range(2):
        out[e : e + 1, :] = jnp.where(at < where[5 + e], lines[e : e + 1, :], 0.0)


def run_router(where, own, other, slots):
    return pl.pallas_call(
        router_kernel,
        out_shape=jax.ShapeDtypeStruct((2, 256), F32),
        in_specs=[SMEM_SPEC] + vmem_specs(3),
        out_specs=vmem_specs(1)[0],
        compiler_params=pltpu.CompilerParams(vmem_limit_bytes=4 * MIB),
        name="router",
    )(where, own, other, slots)


def on_device(
    tokens_in, out_grad, gate_weight, up_weight, down_weight, slot_tokens, slot_counts, slot_gates
):
    x, c, y, z = position()
    where = jnp.stack([x, y, z, c, c, slot_counts[0], slot_counts[1]]).astype(jnp.int32)
    gate_sib, up_sib = swap(gate_weight), swap(up_weight)

    packed = run_pack(tokens_in, out_grad)
    t16, g64 = run_first_stage(where, [packed] + [shift(packed, "z", k) for k in (1, 2, 3)])
    t = [t16] + [shift(t16, "y", k) for k in (1, 2, 3)]
    g = [g64] + [shift(g64, "x", k) for k in (1, 2, 3)]
    down_sib = swap(down_weight)
    t64, g256 = run_second_stage(where, t, g, [gate_sib, up_sib])
    t_low, t_high = shift(t64, "x", 1), shift(t64, "x", -1)
    g_low, g_high = shift(g256, "y", 1), shift(g256, "y", -1)
    a, b, e, f = run_halves(t_low, t_high, g_low, g_high)
    t = (t64, t_low, t_high, shift(a, "x", 1), shift(b, "x", -1))
    g = (g256, g_low, g_high, shift(e, "y", 1), shift(f, "y", -1))
    weights = (gate_weight, up_weight, down_weight, gate_sib, up_sib, down_sib)
    early = run_early(where, t[0:3], g[0:3], weights)
    outs = run_main(where, t, g, weights, slot_tokens, slot_gates, early)
    a_own, a_down, a_up, a_low, a_high = outs[0:5]
    b_own, b_up, b_down, b_low, b_high = outs[5:10]
    dl_own, rows, grads = outs[10:]

    halves = [shift(a_low, "x", -1), shift(a_high, "x", 1)]
    halves += [shift(b_low, "y", 1), shift(b_high, "y", -1)]
    rows_sib = swap(rows)
    grads_sib = swap(run_relay(grads, halves))
    a_down, a_up, b_up, b_down = run_middle_sum((a_down, a_up, b_up, b_down), halves)
    gate_grad, up_grad, token = run_up(rows, rows_sib, dl_own, [a_down])
    ra = [a_own, shift(a_down, "x", -1), shift(a_up, "x", 1)]
    rb = [b_own, shift(b_up, "y", 1), shift(b_down, "y", -1)]
    q = run_first_sum(where, ra, rb, token)
    qa, qb = q[0:4], q[4:8]
    ra = [qa[0]] + [shift(qa[k], "y", k) for k in (1, 2, 3)]
    rb = [qb[0]] + [shift(qb[k], "x", -k) for k in (1, 2, 3)]
    down_grad, token = run_down(grads, grads_sib, dl_own, rows_sib)
    q = run_second_sum(where, ra, rb, token)
    input_grad, sums = run_last_sum([q[0]] + [shift(q[k], "z", k) for k in (1, 2, 3)])
    router_grad = run_router(where, sums, swap(sums), slot_tokens)
    return (input_grad, gate_grad, up_grad, down_grad, router_grad)


def solution(mesh):
    return jax.shard_map(
        on_device,
        mesh=mesh,
        in_specs=(
            P(("section", "et"), None),
            P("section", "et"),
            P(None, None, ("section", "et")),
            P(None, None, ("section", "et")),
            P(None, ("section", "et"), None),
            P(),
            P(),
            P(),
        ),
        out_specs=(
            P(("section", "et"), None),
            P(None, None, ("section", "et")),
            P(None, None, ("section", "et")),
            P(None, ("section", "et"), None),
            P(),
        ),
        check_vma=False,
    )
```

```python
import jax
import jax.numpy as jnp
from jax import lax
from jax.experimental import pallas as pl
from jax.experimental.pallas import tpu as pltpu
from jax.sharding import PartitionSpec as P

AXES = ("section", "et")
BF = jnp.bfloat16
F32 = jnp.float32
D = 6144
NX, NC, NY, NZ = 4, 2, 4, 4
H = 128
SHORT = 64
HALF = 256


def linear(x, c, y, z):
    return ((x * NC + c) * NY + y) * NZ + z


def shift_pairs(axis, step):
    pairs = []
    for x in range(NX):
        for c in range(NC):
            for y in range(NY):
                for z in range(NZ):
                    to = {
                        "x": ((x + step) % NX, c, y, z),
                        "y": (x, c, (y + step) % NY, z),
                        "z": (x, c, y, (z + step) % NZ),
                    }[axis]
                    pairs.append((linear(x, c, y, z), linear(*to)))
    return pairs


def shift(value, axis, step):
    return lax.ppermute(value, AXES, shift_pairs(axis, step))


def swap(value):
    pairs = [
        (linear(x, c, y, z), linear(x, 1 - c, y, z))
        for x in range(NX)
        for c in range(NC)
        for y in range(NY)
        for z in range(NZ)
    ]
    return lax.ppermute(value, AXES, pairs)


def position():
    section = lax.axis_index("section")
    et = lax.axis_index("et")
    return section // NC, section % NC, et // NZ, et % NZ


def nt(left, right):
    return lax.dot_general(left, right, (((1,), (1,)), ((), ())), preferred_element_type=F32)


def tn(left, right):
    return lax.dot_general(left, right, (((0,), (0,)), ((), ())), preferred_element_type=F32)


def total(first, rest):
    out = first.astype(F32)
    for r in rest:
        out = out + r.astype(F32)
    return out


KT = 1024
FT = 512
MIB = 2**20
WIDE = D // 2 + 384


def vmem_specs(n):
    return [pl.BlockSpec(memory_space=pltpu.VMEM)] * n


SMEM_SPEC = pl.BlockSpec(memory_space=pltpu.SMEM)


def pack_kernel(tokens, grads, out):
    out[0:64, :] = grads[...]
    rows = tokens[...].astype(F32)
    for b in range(0, 16, 4):
        four = [rows[:, (b + i) * 384 : (b + i + 1) * 384] for i in range(4)]
        out[64 + 4 * b : 80 + 4 * b, :] = jnp.concatenate(four, axis=0).astype(BF)


def run_pack(tokens, grads):
    return pl.pallas_call(
        pack_kernel,
        out_shape=jax.ShapeDtypeStruct((128, 384), BF),
        in_specs=vmem_specs(2),
        out_specs=vmem_specs(1)[0],
        compiler_params=pltpu.CompilerParams(vmem_limit_bytes=4 * MIB),
        name="pack",
    )(tokens, grads)


def first_stage_kernel(where, *refs):
    packed, t_out, g_out, buf = refs[0:4], refs[-3], refs[-2], refs[-1]
    for k in range(NZ):
        at = (where[2] - k) % NZ
        rows = packed[k][64:128, :].astype(F32)
        for b in range(16):
            buf[at, :, 384 * b : 384 * (b + 1)] = rows[4 * b : 4 * b + 4]
        start = pl.multiple_of(384 * at, 128)
        g_out[:, pl.ds(start, 384)] = packed[k][0:64, :]
    t_out[...] = jnp.concatenate([buf[k] for k in range(NZ)], axis=0).astype(BF)


def run_first_stage(where, packed, before):
    return pl.pallas_call(
        first_stage_kernel,
        out_shape=[jax.ShapeDtypeStruct((16, D), BF), jax.ShapeDtypeStruct((64, 1536), BF)],
        in_specs=[SMEM_SPEC] + vmem_specs(4) + [pl.BlockSpec(memory_space=pl.ANY)] * len(before),
        out_specs=vmem_specs(2),
        scratch_shapes=[pltpu.VMEM((NZ, 4, D), F32)],
        compiler_params=pltpu.CompilerParams(vmem_limit_bytes=4 * MIB),
        name="first_stage",
    )(where, *packed, *before)


def near_halves_kernel(t_low, t_high, g_low, g_high, a, b, c, d):
    a[...] = t_low[:, 0 : D // 2]
    b[...] = t_high[:, D // 2 : D]
    c[...] = g_low[0:32, :]
    d[...] = g_high[32:64, :]


def run_near_halves(t_low, t_high, g_low, g_high):
    return pl.pallas_call(
        near_halves_kernel,
        out_shape=[jax.ShapeDtypeStruct((16, D // 2), BF)] * 2
        + [jax.ShapeDtypeStruct((32, 1536), BF)] * 2,
        in_specs=vmem_specs(4),
        out_specs=vmem_specs(4),
        compiler_params=pltpu.CompilerParams(vmem_limit_bytes=4 * MIB),
        name="near_halves",
    )(t_low, t_high, g_low, g_high)


def second_stage_kernel(where, *refs):
    t, g, t_out, g_out = refs[0:5], refs[5:10], refs[10], refs[11]
    y = where[1]
    for piece, step in zip(t[0:3], (0, -1, 1)):
        start = pl.multiple_of(16 * ((y + step + NY) % NY), 16)
        t_out[pl.ds(start, 16), :] = piece[...]
    start = pl.multiple_of(16 * ((y + 2) % NY), 16)
    t_out[pl.ds(start, 16), 0 : D // 2] = t[3][...]
    t_out[pl.ds(start, 16), D // 2 : D] = t[4][...]
    for piece, at in zip(g, (0, 64, 192, 128, 160)):
        g_out[at : at + piece.shape[0], :] = piece[...]


def run_second_stage(where, t, g):
    return pl.pallas_call(
        second_stage_kernel,
        out_shape=[jax.ShapeDtypeStruct((64, D), BF), jax.ShapeDtypeStruct((HALF, 1536), BF)],
        in_specs=[SMEM_SPEC] + vmem_specs(10),
        out_specs=vmem_specs(2),
        compiler_params=pltpu.CompilerParams(vmem_limit_bytes=4 * MIB),
        name="second_stage",
    )(where, *t, *g)


def halves_kernel(t_low, t_high, g_low, g_high, a, b, c, d):
    a[...] = t_low[0:32, :]
    b[...] = t_high[32:64, :]
    c[...] = g_low[0:128, :]
    d[...] = g_high[128:256, :]


def run_halves(t_low, t_high, g_low, g_high):
    return pl.pallas_call(
        halves_kernel,
        out_shape=[jax.ShapeDtypeStruct((32, D), BF)] * 2
        + [jax.ShapeDtypeStruct((128, 1536), BF)] * 2,
        in_specs=vmem_specs(4),
        out_specs=vmem_specs(4),
        compiler_params=pltpu.CompilerParams(vmem_limit_bytes=4 * MIB),
        name="halves",
    )(t_low, t_high, g_low, g_high)


def relay_kernel(*refs):
    value, (out, sem) = refs[0], refs[-2:]
    copy = pltpu.make_async_copy(value, out, sem)
    copy.start()
    copy.wait()


def run_relay(value, before):
    hbm = [pl.BlockSpec(memory_space=pltpu.HBM)]
    return pl.pallas_call(
        relay_kernel,
        out_shape=jax.ShapeDtypeStruct(value.shape, value.dtype),
        in_specs=hbm * (1 + len(before)),
        out_specs=hbm[0],
        scratch_shapes=[pltpu.SemaphoreType.DMA],
        compiler_params=pltpu.CompilerParams(vmem_limit_bytes=1 * MIB),
        cost_estimate=pl.CostEstimate(flops=0, bytes_accessed=6_000_000, transcendentals=0),
        name="relay",
    )(value, *before)


def row_copies(pieces, rows, sem):
    places = (0, 64, 192, 128, 160)
    return [
        pltpu.make_async_copy(piece, rows.at[pl.ds(at, piece.shape[0]), :], sem.at[r])
        for r, (piece, at) in enumerate(zip(pieces, places))
    ]


def grad_copies(pieces, grads, sem, y):
    places = ((0, 0), (-1, 0), (1, 0), (2, 0), (2, 128))
    copies = []
    for j, (piece, (step, at)) in enumerate(zip(pieces, places)):
        start = pl.multiple_of(((y + step + NY) % NY) * 1536, 128)
        copies.append(
            pltpu.make_async_copy(
                piece, grads.at[pl.ds(at, piece.shape[0]), pl.ds(start, 1536)], sem.at[j]
            )
        )
    return copies


def split_three(value):
    high = value.astype(BF)
    rest = value - high.astype(F32)
    middle = rest.astype(BF)
    low = (rest - middle.astype(F32)).astype(BF)
    return jnp.concatenate([high, middle, low], axis=1)


def join_three(parts):
    out = parts.astype(F32)
    return out[:, 0:128] + out[:, 128:256] + out[:, 256:384]


def early_kernel(where, *refs):
    t, g, weights = refs[0:3], refs[3:6], (refs[6:9], refs[9:12])
    acc_g, acc_b, wv, dv, sem_w, sem_d = refs[12:18]
    y = where[1]
    tiles = D // KT

    def wide_copies(i):
        k = pl.ds(pl.multiple_of(i * KT, KT), KT)
        return [
            pltpu.make_async_copy(
                weights[s][n].at[:, k, :], wv.at[s, n, :, k, :], sem_w.at[i, s * 2 + n]
            )
            for s in range(2)
            for n in range(2)
        ]

    tall_copies = []
    for j, step in enumerate((0, -1, 1)):
        block = pl.ds(pl.multiple_of(((y + step + NY) % NY) * 1536, 128), 1536)
        tall_copies.append(
            [
                pltpu.make_async_copy(weights[s][2].at[:, :, block], dv.at[j, s], sem_d.at[j, s])
                for s in range(2)
            ]
        )
    for i in range(tiles):
        for copy in wide_copies(i):
            copy.start()
    for group in tall_copies:
        for copy in group:
            copy.start()
    acc_g[...] = jnp.zeros(acc_g.shape, F32)
    acc_b[...] = jnp.zeros(acc_b.shape, F32)

    @pl.loop(0, tiles)
    def _(i):
        for copy in wide_copies(i):
            copy.wait()
        k = pl.ds(pl.multiple_of(i * KT, KT), KT)
        wide = jnp.concatenate(
            [wv[s, n, e, k, :] for s in range(2) for e in range(2) for n in range(2)], axis=1
        )
        rows = jnp.concatenate([piece[:, k] for piece in t], axis=0)
        acc_g[...] += jnp.dot(rows, wide, preferred_element_type=F32)

    for j, group in enumerate(tall_copies):
        for copy in group:
            copy.wait()
        tall = jnp.concatenate([dv[j, s, e] for s in range(2) for e in range(2)], axis=0)
        acc_b[...] += nt(g[j][...], tall)


def run_early(where, t, g, weights):
    hbm = [pl.BlockSpec(memory_space=pltpu.HBM)]
    return pl.pallas_call(
        early_kernel,
        out_shape=[
            jax.ShapeDtypeStruct((192, 1024), F32),
            jax.ShapeDtypeStruct((HALF, 512), F32),
        ],
        in_specs=[SMEM_SPEC] + vmem_specs(6) + hbm * 6,
        out_specs=vmem_specs(2),
        scratch_shapes=[
            pltpu.VMEM((2, 2, 2, D, H), BF),
            pltpu.VMEM((3, 2, 2, H, 1536), BF),
            pltpu.SemaphoreType.DMA((D // KT, 4)),
            pltpu.SemaphoreType.DMA((3, 2)),
        ],
        compiler_params=pltpu.CompilerParams(vmem_limit_bytes=30 * MIB),
        cost_estimate=pl.CostEstimate(
            flops=3_600_000_000, bytes_accessed=20_000_000, transcendentals=0
        ),
        name="early",
    )(where, *t, *g, *weights)


def main_kernel(where, *refs):
    t_in, g_in = refs[0:5], refs[5:10]
    weights = (refs[10:13], refs[13:16])
    slots_ref, gates_ref, early_g, early_b = refs[16:20]
    pa_out, pb_out = refs[20:25], refs[25:30]
    own_out, rows_out, grads_out = refs[30:33]
    rows, grads, wv, dv, pa, pb = refs[33:39]
    acc_g, acc_b, deltas, tile, rbuf, packed = refs[39:45]
    sem_t, sem_g, sem_w, sem_d, sem_o = refs[45:50]
    x, y, core = where[0], where[1], where[4]
    copies_t = row_copies(t_in, rows, sem_t)
    copies_g = grad_copies(g_in, grads, sem_g, y)
    tiles = D // KT

    def wide_copies(i):
        k = pl.ds(pl.multiple_of(i * KT, KT), KT)
        return [
            pltpu.make_async_copy(
                weights[s][n].at[:, k, :], wv.at[s, n, :, k, :], sem_w.at[i, s * 2 + n]
            )
            for s in range(2)
            for n in range(2)
        ]

    far = pl.ds(pl.multiple_of(((y + 2) % NY) * 1536, 128), 1536)
    tall_copies = [
        pltpu.make_async_copy(weights[s][2].at[:, :, far], dv.at[s], sem_d.at[s]) for s in range(2)
    ]
    for copy in copies_t:
        copy.start()
    for i in range(tiles):
        for copy in wide_copies(i):
            copy.start()
    for copy in copies_g + tall_copies:
        copy.start()
    acc_g[0:128, :] = early_g[0:128, :]
    acc_g[128:192, :] = jnp.zeros((64, 1024), F32)
    acc_g[192:256, :] = early_g[128:192, :]
    scales = []
    slot = lax.broadcasted_iota(jnp.int32, (HALF, 256), 1)
    row = lax.broadcasted_iota(jnp.int32, (HALF, 256), 0)
    block = row // 64
    token = ((x - block + NX) % NX) * 128 + core * 64 + (row - block * 64)
    for e in range(2):
        hit = (token == slots_ref[e : e + 1, :]) & (slot < where[5 + e])
        gate = jnp.broadcast_to(gates_ref[e : e + 1, :], (HALF, 256))
        scales.append(jnp.sum(jnp.where(hit, gate, 0.0), axis=1, keepdims=True))
    for copy in copies_t:
        copy.wait()
    rows_copy = pltpu.make_async_copy(rows, rows_out.at[:, pl.ds(0, D)], sem_o.at[0])
    grads_copy = pltpu.make_async_copy(grads, grads_out, sem_o.at[1])

    @pl.loop(0, tiles)
    def _(i):
        for copy in wide_copies(i):
            copy.wait()
        k = pl.ds(pl.multiple_of(i * KT, KT), KT)
        wide = jnp.concatenate(
            [wv[s, n, e, k, :] for s in range(2) for e in range(2) for n in range(2)], axis=1
        )
        acc_g[128:192, :] += jnp.dot(rows[128:192, k], wide, preferred_element_type=F32)

    for copy in copies_g + tall_copies:
        copy.wait()
    tall = jnp.concatenate([dv[s, e] for s in range(2) for e in range(2)], axis=0)
    acc_b[...] = early_b[...] + nt(grads[:, far], tall)
    rows_copy.start()
    grads_copy.start()
    router = [0.0, 0.0]
    for s in range(2):
        for e in range(2):
            j = s * 2 + e
            pre_gate = acc_g[:, j * 256 : j * 256 + H]
            pre_up = acc_g[:, j * 256 + H : (j + 1) * 256]
            back = acc_b[:, j * H : (j + 1) * H]
            scale = scales[e]
            sigma = jax.nn.sigmoid(pre_gate)
            active = pre_gate * sigma
            hidden = active * pre_up
            router[e] += jnp.sum(hidden.astype(BF).astype(F32) * back, axis=1, keepdims=True)
            hidden_grad = back * scale
            gate_delta = (hidden_grad * pre_up * sigma * (1.0 + pre_gate * (1.0 - sigma))).astype(BF)
            up_delta = (hidden_grad * active).astype(BF)
            deltas[:, j * 256 : j * 256 + H] = gate_delta
            deltas[:, j * 256 + H : (j + 1) * 256] = up_delta
            packed[s, :, e * 256 : e * 256 + H] = gate_delta
            packed[s, :, e * 256 + H : (e + 1) * 256] = up_delta
            packed[s, :, 512 + e * H : 512 + (e + 1) * H] = (hidden * scale).astype(BF)
    own_copy = pltpu.make_async_copy(packed.at[0], own_out, sem_o.at[2])
    sib_copy = pltpu.make_async_copy(packed.at[1], rows_out.at[:, pl.ds(D, 768)], sem_o.at[3])
    own_copy.start()
    sib_copy.start()
    lane = lax.broadcasted_iota(jnp.int32, (HALF, 128), 1)
    spread = jnp.where(lane == 0, router[0], jnp.where(lane == 1, router[1], 0.0))
    for k in range(NX):
        to = pl.multiple_of(((x - k) % NX) * 64, 64)
        rbuf[pl.ds(to, 64), :] = spread[k * 64 : (k + 1) * 64]
    line = rbuf[...].T[0:2]
    four = [line[e : e + 1, h * 128 : (h + 1) * 128] for e in range(2) for h in range(2)]
    sums = split_three(jnp.concatenate(four + [jnp.zeros((12, 128), F32)], axis=0))
    for k in range(NX):
        pa[k, :, D // 2 :] = jnp.zeros((64, 384), BF)
        pa[k, 0:16, D // 2 :] = sums

    def partial(i):
        f = pl.ds(pl.multiple_of(i * FT, FT), FT)
        wide = jnp.concatenate(
            [wv[s, n, e, f, :] for s in range(2) for e in range(2) for n in range(2)], axis=1
        )
        return nt(deltas[...], wide)

    half = D // 2 // FT

    @pl.loop(0, half)
    def _(i):
        f = pl.ds(pl.multiple_of(i * FT, FT), FT)
        part = partial(i).astype(BF)
        for k in range(NX):
            pa[k, :, f] = part[k * 64 : (k + 1) * 64, :]

    parts = (pa.at[0], pa.at[1], pa.at[3], pa.at[2, pl.ds(0, 32), :], pa.at[2, pl.ds(32, 32), :])
    copies = [
        pltpu.make_async_copy(part, pa_out[k], sem_o.at[4 + k]) for k, part in enumerate(parts)
    ]
    for copy in copies:
        copy.start()

    @pl.loop(0, half)
    def _(i):
        f = pl.ds(pl.multiple_of(i * FT, FT), FT)
        tile[...] = partial(i + half).astype(BF)
        for k in range(NY):
            for b in range(NX):
                src = pl.multiple_of(b * 64 + ((y + k) % NY) * 16, 16)
                pb[k, b, :, f] = tile[pl.ds(src, 16), :]

    parts = (pb.at[0], pb.at[1], pb.at[3], pb.at[2, pl.ds(0, 2)], pb.at[2, pl.ds(2, 2)])
    more = [
        pltpu.make_async_copy(part, pb_out[k], sem_o.at[9 + k]) for k, part in enumerate(parts)
    ]
    for copy in more:
        copy.start()
    for copy in [rows_copy, grads_copy, own_copy, sib_copy] + copies + more:
        copy.wait()


def run_main(where, t, g, weights, slots, gates, early):
    hbm = [pl.BlockSpec(memory_space=pltpu.HBM)]
    out_shape = (
        [jax.ShapeDtypeStruct((64, WIDE), BF)] * 3
        + [jax.ShapeDtypeStruct((32, WIDE), BF)] * 2
        + [jax.ShapeDtypeStruct((4, 16, D // 2), BF)] * 3
        + [jax.ShapeDtypeStruct((2, 16, D // 2), BF)] * 2
        + [jax.ShapeDtypeStruct((HALF, 768), BF)]
        + [jax.ShapeDtypeStruct((HALF, D + 768), BF)]
        + [jax.ShapeDtypeStruct((HALF, D), BF)]
    )
    return pl.pallas_call(
        main_kernel,
        out_shape=out_shape,
        in_specs=[SMEM_SPEC] + hbm * 16 + vmem_specs(4),
        out_specs=hbm * 13,
        scratch_shapes=[
            pltpu.VMEM((HALF, D), BF),
            pltpu.VMEM((HALF, D), BF),
            pltpu.VMEM((2, 2, 2, D, H), BF),
            pltpu.VMEM((2, 2, H, 1536), BF),
            pltpu.VMEM((4, 64, WIDE), BF),
            pltpu.VMEM((4, 4, 16, D // 2), BF),
            pltpu.VMEM((HALF, 1024), F32),
            pltpu.VMEM((HALF, 512), F32),
            pltpu.VMEM((HALF, 1024), BF),
            pltpu.VMEM((HALF, FT), BF),
            pltpu.VMEM((HALF, 128), F32),
            pltpu.VMEM((2, HALF, 768), BF),
            pltpu.SemaphoreType.DMA((5,)),
            pltpu.SemaphoreType.DMA((5,)),
            pltpu.SemaphoreType.DMA((D // KT, 4)),
            pltpu.SemaphoreType.DMA((2,)),
            pltpu.SemaphoreType.DMA((14,)),
        ],
        compiler_params=pltpu.CompilerParams(vmem_limit_bytes=38 * MIB),
        cost_estimate=pl.CostEstimate(
            flops=8_000_000_000, bytes_accessed=30_000_000, transcendentals=262144
        ),
        name="main",
    )(where, *t, *g, *weights, slots, gates, *early)


def up_kernel(*refs):
    rows_own, rows_sib, own, sib = refs[0:4]
    gate_out, up_out, token = refs[-3:]
    token[...] = jnp.zeros(token.shape, F32)
    part = tn(rows_own[...], own[:, 0:512]) + tn(rows_sib[...], sib[:, 0:512])
    for e in range(2):
        gate_out[e] = part[:, e * 256 : e * 256 + H].astype(BF)
        up_out[e] = part[:, e * 256 + H : (e + 1) * 256].astype(BF)


def run_up(rows_own, rows_sib, own, before):
    tile = pl.BlockSpec((HALF, FT), lambda i: (0, i))
    whole = pl.BlockSpec((HALF, 768), lambda i: (0, 0))
    tail = pl.BlockSpec((HALF, 768), lambda i: (0, D // 768))
    out = pl.BlockSpec((2, FT, H), lambda i: (0, i, 0))
    return pl.pallas_call(
        up_kernel,
        grid=(D // FT,),
        out_shape=[
            jax.ShapeDtypeStruct((2, D, H), BF),
            jax.ShapeDtypeStruct((2, D, H), BF),
            jax.ShapeDtypeStruct((8, 128), F32),
        ],
        in_specs=[tile, tile, whole, tail]
        + [pl.BlockSpec(memory_space=pl.ANY)] * len(before),
        out_specs=[out, out, pl.BlockSpec((8, 128), lambda i: (0, 0))],
        compiler_params=pltpu.CompilerParams(
            dimension_semantics=("arbitrary",), vmem_limit_bytes=16 * MIB
        ),
        cost_estimate=pl.CostEstimate(
            flops=3_200_000_000, bytes_accessed=13_000_000, transcendentals=0
        ),
        name="up_grads",
    )(rows_own, rows_sib, own, rows_sib, *before)


def down_kernel(grads_own, grads_sib, own, sib, out, token, hidden):
    token[...] = jnp.zeros(token.shape, F32)

    @pl.when(pl.program_id(0) == 0)
    def _():
        hidden[:, 0:HALF] = own[:, 512:768].T
        hidden[:, HALF:512] = sib[:, 512:768].T

    part = jnp.dot(hidden[:, 0:HALF], grads_own[...], preferred_element_type=F32)
    part += jnp.dot(hidden[:, HALF:512], grads_sib[...], preferred_element_type=F32)
    for e in range(2):
        out[e] = part[e * H : (e + 1) * H].astype(BF)


def run_down(grads_own, grads_sib, own, rows_sib):
    tile = pl.BlockSpec((HALF, 2 * FT), lambda i: (0, i))
    whole = pl.BlockSpec((HALF, 768), lambda i: (0, 0))
    tail = pl.BlockSpec((HALF, 768), lambda i: (0, D // 768))
    return pl.pallas_call(
        down_kernel,
        grid=(D // FT // 2,),
        out_shape=[
            jax.ShapeDtypeStruct((2, H, D), BF),
            jax.ShapeDtypeStruct((8, 128), F32),
        ],
        in_specs=[tile, tile, whole, tail],
        out_specs=[
            pl.BlockSpec((2, H, 2 * FT), lambda i: (0, 0, i)),
            pl.BlockSpec((8, 128), lambda i: (0, 0)),
        ],
        scratch_shapes=[pltpu.VMEM((256, 512), BF)],
        compiler_params=pltpu.CompilerParams(
            dimension_semantics=("arbitrary",), vmem_limit_bytes=16 * MIB
        ),
        cost_estimate=pl.CostEstimate(
            flops=1_600_000_000, bytes_accessed=10_000_000, transcendentals=0
        ),
        name="down_grads",
    )(grads_own, grads_sib, own, rows_sib)


def middle_sum_kernel(*refs):
    a_down, a_up, b_up, b_down = refs[0:4]
    low_a, high_a, low_b, high_b = refs[4:8]
    out_a_down, out_a_up, out_b_up, out_b_down = refs[8:12]
    half = D // 2
    out_a_down[0:32, 0:half] = total(a_down[0:32, 0:half], [low_a[:, 0:half]]).astype(BF)
    out_a_down[32:64, :] = a_down[32:64, :]
    sums = join_three(a_down[0:16, half:]) + join_three(low_a[0:16, half:])
    out_a_down[0:16, half:] = split_three(sums)
    out_a_down[16:32, half:] = a_down[16:32, half:]
    out_a_up[0:32, :] = a_up[0:32, :]
    out_a_up[32:64, :] = total(a_up[32:64, :], [high_a[...]]).astype(BF)
    for k in range(2):
        out_b_up[k] = total(b_up[k], [low_b[k]]).astype(BF)
        out_b_up[2 + k] = b_up[2 + k]
        out_b_down[k] = b_down[k]
        out_b_down[2 + k] = total(b_down[2 + k], [high_b[k]]).astype(BF)


def run_middle_sum(blocks, halves):
    return pl.pallas_call(
        middle_sum_kernel,
        out_shape=[jax.ShapeDtypeStruct((64, WIDE), BF)] * 2
        + [jax.ShapeDtypeStruct((4, 16, D // 2), BF)] * 2,
        in_specs=vmem_specs(8),
        out_specs=vmem_specs(4),
        compiler_params=pltpu.CompilerParams(vmem_limit_bytes=8 * MIB),
        name="middle_sum",
    )(*blocks, *halves)


def first_sum_kernel(where, *refs):
    ra, rb, qa, qb, buf = refs[0:3], refs[3:6], refs[7:11], refs[11:15], refs[15]
    half = D // 2
    buf[...] = total(ra[0][:, 0:half], [r[:, 0:half] for r in ra[1:]]).astype(BF)
    sums = join_three(ra[0][0:16, half:])
    for r in ra[1:]:
        sums += join_three(r[0:16, half:])
    sums = split_three(sums)
    for k in range(NY):
        start = pl.multiple_of(((where[1] + k) % NY) * 16, 16)
        qa[k][:, 0:half] = buf[pl.ds(start, 16), :]
        qa[k][:, half:] = sums
    for k in range(NX):
        qb[k][...] = total(rb[0][k], [r[k] for r in rb[1:]]).astype(BF)


def run_first_sum(where, ra, rb, token):
    return pl.pallas_call(
        first_sum_kernel,
        out_shape=[jax.ShapeDtypeStruct((16, WIDE), BF)] * 4
        + [jax.ShapeDtypeStruct((16, D // 2), BF)] * 4,
        in_specs=[SMEM_SPEC] + vmem_specs(7),
        out_specs=vmem_specs(8),
        scratch_shapes=[pltpu.VMEM((64, D // 2), BF)],
        compiler_params=pltpu.CompilerParams(vmem_limit_bytes=8 * MIB),
        name="first_sum",
    )(where, *ra, *rb, token)


def second_sum_kernel(where, *refs):
    ra, rb, own, out, buf = refs[0:4], refs[4:8], refs[9], refs[10:13], refs[13]
    half = D // 2
    for n, r in enumerate((ra, rb)):
        part = total(r[0][:, 0:half], [p[:, 0:half] for p in r[1:]])
        for k in range(NZ):
            buf[k, :, n * half : (n + 1) * half] = part[4 * k : 4 * k + 4]
    sums = join_three(ra[0][:, half:])
    for r in ra[1:]:
        sums += join_three(r[:, half:])
    parts = split_three(sums)[0:4]
    for k in range(NZ):
        rows = buf[(where[2] + k) % NZ]
        if k == 0:
            own[:, 0:D] = rows
            own[:, D:] = sums[0:4]
        else:
            out[k - 1][:, 0:D] = rows.astype(BF)
            out[k - 1][:, D:] = parts


def run_second_sum(where, ra, rb, token):
    return pl.pallas_call(
        second_sum_kernel,
        out_shape=[jax.ShapeDtypeStruct((4, D + 128), F32)]
        + [jax.ShapeDtypeStruct((4, D + 384), BF)] * 3,
        in_specs=[SMEM_SPEC] + vmem_specs(9),
        out_specs=vmem_specs(4),
        scratch_shapes=[pltpu.VMEM((NZ, 4, D), F32)],
        compiler_params=pltpu.CompilerParams(vmem_limit_bytes=8 * MIB),
        name="second_sum",
    )(where, *ra, *rb, token)


def last_sum_kernel(own, *refs):
    out, sums_out = refs[3], refs[4]
    out[...] = total(own[:, 0:D], [r[:, 0:D] for r in refs[0:3]]).astype(BF)
    sums = own[:, D:]
    for r in refs[0:3]:
        sums += join_three(r[:, D:])
    sums_out[0:4, :] = sums
    sums_out[4:8, :] = jnp.zeros((4, 128), F32)


def run_last_sum(pieces):
    return pl.pallas_call(
        last_sum_kernel,
        out_shape=[jax.ShapeDtypeStruct((4, D), BF), jax.ShapeDtypeStruct((8, 128), F32)],
        in_specs=vmem_specs(4),
        out_specs=vmem_specs(2),
        compiler_params=pltpu.CompilerParams(vmem_limit_bytes=4 * MIB),
        name="last_sum",
    )(*pieces)


def router_kernel(where, own, other, slots_ref, out):
    first = jnp.where(where[4] == 0, own[...], other[...])
    second = jnp.where(where[4] == 0, other[...], own[...])
    slots = slots_ref[...].T
    index = lax.broadcasted_iota(jnp.int32, (256, 128), 1)
    spread = jnp.zeros((256, 128), F32)
    for e in range(2):
        picked = jnp.zeros((256, 1), F32)
        for core, values in enumerate((first, second)):
            for h in range(2):
                at = index + h * 128
                token = (at // 64) * 128 + core * 64 + at % 64
                hit = slots[:, e : e + 1] == token
                line = jnp.broadcast_to(values[2 * e + h : 2 * e + h + 1, :], (256, 128))
                picked += jnp.sum(jnp.where(hit, line, 0.0), axis=1, keepdims=True)
        spread = jnp.where(index == e, picked, spread)
    lines = spread.T
    at = lax.broadcasted_iota(jnp.int32, (1, 256), 1)
    for e in range(2):
        out[e : e + 1, :] = jnp.where(at < where[5 + e], lines[e : e + 1, :], 0.0)


def run_router(where, own, other, slots):
    return pl.pallas_call(
        router_kernel,
        out_shape=jax.ShapeDtypeStruct((2, 256), F32),
        in_specs=[SMEM_SPEC] + vmem_specs(3),
        out_specs=vmem_specs(1)[0],
        compiler_params=pltpu.CompilerParams(vmem_limit_bytes=4 * MIB),
        name="router",
    )(where, own, other, slots)


def on_device(
    tokens_in, out_grad, gate_weight, up_weight, down_weight, slot_tokens, slot_counts, slot_gates
):
    x, c, y, z = position()
    where = jnp.stack([x, y, z, c, c, slot_counts[0], slot_counts[1]]).astype(jnp.int32)
    gate_sib, up_sib = swap(gate_weight), swap(up_weight)

    packed = run_pack(tokens_in, out_grad)
    packed = [packed] + [shift(packed, "z", k) for k in (1, 2, 3)]
    t16, g64 = run_first_stage(where, packed, [gate_sib, up_sib])
    down_sib = swap(run_relay(down_weight, [t16]))
    t_low, t_high = shift(t16, "y", 1), shift(t16, "y", -1)
    g_low, g_high = shift(g64, "x", 1), shift(g64, "x", -1)
    a, b, e, f = run_near_halves(t_low, t_high, g_low, g_high)
    t = (t16, t_low, t_high, shift(a, "y", 1), shift(b, "y", -1))
    g = (g64, g_low, g_high, shift(e, "x", 1), shift(f, "x", -1))
    t64, g256 = run_second_stage(where, t, g)
    t_low, t_high = shift(t64, "x", 1), shift(t64, "x", -1)
    g_low, g_high = shift(g256, "y", 1), shift(g256, "y", -1)
    a, b, e, f = run_halves(t_low, t_high, g_low, g_high)
    t = (t64, t_low, t_high, shift(a, "x", 1), shift(b, "x", -1))
    g = (g256, g_low, g_high, shift(e, "y", 1), shift(f, "y", -1))
    weights = (gate_weight, up_weight, down_weight, gate_sib, up_sib, down_sib)
    early = run_early(where, t[0:3], g[0:3], weights)
    outs = run_main(where, t, g, weights, slot_tokens, slot_gates, early)
    a_own, a_down, a_up, a_low, a_high = outs[0:5]
    b_own, b_up, b_down, b_low, b_high = outs[5:10]
    dl_own, rows, grads = outs[10:]

    halves = [shift(a_low, "x", -1), shift(a_high, "x", 1)]
    halves += [shift(b_low, "y", 1), shift(b_high, "y", -1)]
    rows_sib = swap(rows)
    grads_sib = swap(run_relay(grads, halves))
    a_down, a_up, b_up, b_down = run_middle_sum((a_down, a_up, b_up, b_down), halves)
    gate_grad, up_grad, token = run_up(rows, rows_sib, dl_own, [a_down])
    ra = [a_own, shift(a_down, "x", -1), shift(a_up, "x", 1)]
    rb = [b_own, shift(b_up, "y", 1), shift(b_down, "y", -1)]
    q = run_first_sum(where, ra, rb, token)
    qa, qb = q[0:4], q[4:8]
    ra = [qa[0]] + [shift(qa[k], "y", k) for k in (1, 2, 3)]
    rb = [qb[0]] + [shift(qb[k], "x", -k) for k in (1, 2, 3)]
    down_grad, token = run_down(grads, grads_sib, dl_own, rows_sib)
    q = run_second_sum(where, ra, rb, token)
    input_grad, sums = run_last_sum([q[0]] + [shift(q[k], "z", k) for k in (1, 2, 3)])
    router_grad = run_router(where, sums, swap(sums), slot_tokens)
    return (input_grad, gate_grad, up_grad, down_grad, router_grad)


def solution(mesh):
    return jax.shard_map(
        on_device,
        mesh=mesh,
        in_specs=(
            P(("section", "et"), None),
            P("section", "et"),
            P(None, None, ("section", "et")),
            P(None, None, ("section", "et")),
            P(None, ("section", "et"), None),
            P(),
            P(),
            P(),
        ),
        out_specs=(
            P(("section", "et"), None),
            P(None, None, ("section", "et")),
            P(None, None, ("section", "et")),
            P(None, ("section", "et"), None),
            P(),
        ),
        check_vma=False,
    )
```

```python
import jax
import jax.numpy as jnp
from jax import lax
from jax.experimental import pallas as pl
from jax.experimental.pallas import tpu as pltpu
from jax.sharding import PartitionSpec as P

AXES = ("section", "et")
BF = jnp.bfloat16
F32 = jnp.float32
D = 6144
NX, NC, NY, NZ = 4, 2, 4, 4
H = 128
SHORT = 64
HALF = 256


def linear(x, c, y, z):
    return ((x * NC + c) * NY + y) * NZ + z


def shift_pairs(axis, step):
    pairs = []
    for x in range(NX):
        for c in range(NC):
            for y in range(NY):
                for z in range(NZ):
                    to = {
                        "x": ((x + step) % NX, c, y, z),
                        "y": (x, c, (y + step) % NY, z),
                        "z": (x, c, y, (z + step) % NZ),
                    }[axis]
                    pairs.append((linear(x, c, y, z), linear(*to)))
    return pairs


def shift(value, axis, step):
    return lax.ppermute(value, AXES, shift_pairs(axis, step))


def swap(value):
    pairs = [
        (linear(x, c, y, z), linear(x, 1 - c, y, z))
        for x in range(NX)
        for c in range(NC)
        for y in range(NY)
        for z in range(NZ)
    ]
    return lax.ppermute(value, AXES, pairs)


def position():
    section = lax.axis_index("section")
    et = lax.axis_index("et")
    return section // NC, section % NC, et // NZ, et % NZ


def nt(left, right):
    return lax.dot_general(left, right, (((1,), (1,)), ((), ())), preferred_element_type=F32)


def tn(left, right):
    return lax.dot_general(left, right, (((0,), (0,)), ((), ())), preferred_element_type=F32)


def total(first, rest):
    out = first.astype(F32)
    for r in rest:
        out = out + r.astype(F32)
    return out


KT = 1024
FT = 512
MIB = 2**20
WIDE = D // 2 + 384


def vmem_specs(n):
    return [pl.BlockSpec(memory_space=pltpu.VMEM)] * n


SMEM_SPEC = pl.BlockSpec(memory_space=pltpu.SMEM)


def pack_kernel(tokens, grads, out):
    out[0:64, :] = grads[...]
    rows = tokens[...].astype(F32)
    for b in range(0, 16, 4):
        four = [rows[:, (b + i) * 384 : (b + i + 1) * 384] for i in range(4)]
        out[64 + 4 * b : 80 + 4 * b, :] = jnp.concatenate(four, axis=0).astype(BF)


def run_pack(tokens, grads):
    return pl.pallas_call(
        pack_kernel,
        out_shape=jax.ShapeDtypeStruct((128, 384), BF),
        in_specs=vmem_specs(2),
        out_specs=vmem_specs(1)[0],
        compiler_params=pltpu.CompilerParams(vmem_limit_bytes=4 * MIB),
        name="pack",
    )(tokens, grads)


def first_stage_kernel(where, *refs):
    packed, t_out, g_out, buf = refs[0:4], refs[-3], refs[-2], refs[-1]
    for k in range(NZ):
        at = (where[2] - k) % NZ
        rows = packed[k][64:128, :].astype(F32)
        for b in range(16):
            buf[at, :, 384 * b : 384 * (b + 1)] = rows[4 * b : 4 * b + 4]
        start = pl.multiple_of(384 * at, 128)
        g_out[:, pl.ds(start, 384)] = packed[k][0:64, :]
    t_out[...] = jnp.concatenate([buf[k] for k in range(NZ)], axis=0).astype(BF)


def run_first_stage(where, packed, before):
    return pl.pallas_call(
        first_stage_kernel,
        out_shape=[jax.ShapeDtypeStruct((16, D), BF), jax.ShapeDtypeStruct((64, 1536), BF)],
        in_specs=[SMEM_SPEC] + vmem_specs(4) + [pl.BlockSpec(memory_space=pl.ANY)] * len(before),
        out_specs=vmem_specs(2),
        scratch_shapes=[pltpu.VMEM((NZ, 4, D), F32)],
        compiler_params=pltpu.CompilerParams(vmem_limit_bytes=4 * MIB),
        name="first_stage",
    )(where, *packed, *before)


def near_halves_kernel(t_low, t_high, g_low, g_high, a, b, c, d):
    a[...] = t_low[:, 0 : D // 2]
    b[...] = t_high[:, D // 2 : D]
    c[...] = g_low[0:32, :]
    d[...] = g_high[32:64, :]


def run_near_halves(t_low, t_high, g_low, g_high):
    return pl.pallas_call(
        near_halves_kernel,
        out_shape=[jax.ShapeDtypeStruct((16, D // 2), BF)] * 2
        + [jax.ShapeDtypeStruct((32, 1536), BF)] * 2,
        in_specs=vmem_specs(4),
        out_specs=vmem_specs(4),
        compiler_params=pltpu.CompilerParams(vmem_limit_bytes=4 * MIB),
        name="near_halves",
    )(t_low, t_high, g_low, g_high)


def second_stage_kernel(where, *refs):
    t, g, t_out, g_out = refs[0:5], refs[5:10], refs[10], refs[11]
    y = where[1]
    for piece, step in zip(t[0:3], (0, -1, 1)):
        start = pl.multiple_of(16 * ((y + step + NY) % NY), 16)
        t_out[pl.ds(start, 16), :] = piece[...]
    start = pl.multiple_of(16 * ((y + 2) % NY), 16)
    t_out[pl.ds(start, 16), 0 : D // 2] = t[3][...]
    t_out[pl.ds(start, 16), D // 2 : D] = t[4][...]
    for piece, at in zip(g, (0, 64, 192, 128, 160)):
        g_out[at : at + piece.shape[0], :] = piece[...]


def run_second_stage(where, t, g):
    return pl.pallas_call(
        second_stage_kernel,
        out_shape=[jax.ShapeDtypeStruct((64, D), BF), jax.ShapeDtypeStruct((HALF, 1536), BF)],
        in_specs=[SMEM_SPEC] + vmem_specs(10),
        out_specs=vmem_specs(2),
        compiler_params=pltpu.CompilerParams(vmem_limit_bytes=4 * MIB),
        name="second_stage",
    )(where, *t, *g)


def halves_kernel(t_low, t_high, g_low, g_high, a, b, c, d):
    a[...] = t_low[0:32, :]
    b[...] = t_high[32:64, :]
    c[...] = g_low[0:128, :]
    d[...] = g_high[128:256, :]


def run_halves(t_low, t_high, g_low, g_high):
    return pl.pallas_call(
        halves_kernel,
        out_shape=[jax.ShapeDtypeStruct((32, D), BF)] * 2
        + [jax.ShapeDtypeStruct((128, 1536), BF)] * 2,
        in_specs=vmem_specs(4),
        out_specs=vmem_specs(4),
        compiler_params=pltpu.CompilerParams(vmem_limit_bytes=4 * MIB),
        name="halves",
    )(t_low, t_high, g_low, g_high)


def relay_kernel(*refs):
    value, (out, sem) = refs[0], refs[-2:]
    copy = pltpu.make_async_copy(value, out, sem)
    copy.start()
    copy.wait()


def run_relay(value, before):
    hbm = [pl.BlockSpec(memory_space=pltpu.HBM)]
    return pl.pallas_call(
        relay_kernel,
        out_shape=jax.ShapeDtypeStruct(value.shape, value.dtype),
        in_specs=hbm * (1 + len(before)),
        out_specs=hbm[0],
        scratch_shapes=[pltpu.SemaphoreType.DMA],
        compiler_params=pltpu.CompilerParams(vmem_limit_bytes=1 * MIB),
        cost_estimate=pl.CostEstimate(flops=0, bytes_accessed=6_000_000, transcendentals=0),
        name="relay",
    )(value, *before)


def row_copies(pieces, rows, sem):
    places = (0, 64, 192, 128, 160)
    return [
        pltpu.make_async_copy(
            piece, rows.at[pl.ds(at, piece.shape[0]), pl.ds(0, D)], sem.at[r]
        )
        for r, (piece, at) in enumerate(zip(pieces, places))
    ]


def grad_copies(pieces, grads, sem, y):
    places = ((0, 0), (-1, 0), (1, 0), (2, 0), (2, 128))
    copies = []
    for j, (piece, (step, at)) in enumerate(zip(pieces, places)):
        start = pl.multiple_of(((y + step + NY) % NY) * 1536, 128)
        copies.append(
            pltpu.make_async_copy(
                piece, grads.at[pl.ds(at, piece.shape[0]), pl.ds(start, 1536)], sem.at[j]
            )
        )
    return copies


def split_three(value):
    high = value.astype(BF)
    rest = value - high.astype(F32)
    middle = rest.astype(BF)
    low = (rest - middle.astype(F32)).astype(BF)
    return jnp.concatenate([high, middle, low], axis=1)


def join_three(parts):
    out = parts.astype(F32)
    return out[:, 0:128] + out[:, 128:256] + out[:, 256:384]


def early_kernel(where, *refs):
    t, g, weights = refs[0:3], refs[3:6], (refs[6:9], refs[9:12])
    acc_g, acc_b, wv, dv, sem_w, sem_d = refs[12:18]
    y = where[1]
    tiles = D // KT

    def wide_copies(i):
        k = pl.ds(pl.multiple_of(i * KT, KT), KT)
        return [
            pltpu.make_async_copy(
                weights[s][n].at[:, k, :], wv.at[s, n, :, k, :], sem_w.at[i, s * 2 + n]
            )
            for s in range(2)
            for n in range(2)
        ]

    tall_copies = []
    for j, step in enumerate((0, -1, 1)):
        block = pl.ds(pl.multiple_of(((y + step + NY) % NY) * 1536, 128), 1536)
        tall_copies.append(
            [
                pltpu.make_async_copy(weights[s][2].at[:, :, block], dv.at[j, s], sem_d.at[j, s])
                for s in range(2)
            ]
        )
    for i in range(tiles):
        for copy in wide_copies(i):
            copy.start()
    for group in tall_copies:
        for copy in group:
            copy.start()
    acc_g[...] = jnp.zeros(acc_g.shape, F32)
    acc_b[...] = jnp.zeros(acc_b.shape, F32)

    @pl.loop(0, tiles)
    def _(i):
        for copy in wide_copies(i):
            copy.wait()
        k = pl.ds(pl.multiple_of(i * KT, KT), KT)
        wide = jnp.concatenate(
            [wv[s, n, e, k, :] for s in range(2) for e in range(2) for n in range(2)], axis=1
        )
        rows = jnp.concatenate([piece[:, k] for piece in t], axis=0)
        acc_g[...] += jnp.dot(rows, wide, preferred_element_type=F32)

    for j, group in enumerate(tall_copies):
        for copy in group:
            copy.wait()
        tall = jnp.concatenate([dv[j, s, e] for s in range(2) for e in range(2)], axis=0)
        acc_b[...] += nt(g[j][...], tall)


def run_early(where, t, g, weights):
    hbm = [pl.BlockSpec(memory_space=pltpu.HBM)]
    return pl.pallas_call(
        early_kernel,
        out_shape=[
            jax.ShapeDtypeStruct((192, 1024), F32),
            jax.ShapeDtypeStruct((HALF, 512), F32),
        ],
        in_specs=[SMEM_SPEC] + vmem_specs(6) + hbm * 6,
        out_specs=vmem_specs(2),
        scratch_shapes=[
            pltpu.VMEM((2, 2, 2, D, H), BF),
            pltpu.VMEM((3, 2, 2, H, 1536), BF),
            pltpu.SemaphoreType.DMA((D // KT, 4)),
            pltpu.SemaphoreType.DMA((3, 2)),
        ],
        compiler_params=pltpu.CompilerParams(vmem_limit_bytes=22 * MIB),
        cost_estimate=pl.CostEstimate(
            flops=3_600_000_000, bytes_accessed=20_000_000, transcendentals=0
        ),
        name="early",
    )(where, *t, *g, *weights)


def main_kernel(where, *refs):
    t_in, g_in = refs[0:5], refs[5:10]
    weights = (refs[10:13], refs[13:16])
    slots_ref, gates_ref, early_g, early_b = refs[16:20]
    pa_out, pb_out = refs[20:25], refs[25:30]
    own_out, rows_out, grads_out = refs[30:33]
    wv, dv, acc_g, acc_b, deltas, tile, rbuf = refs[33:40]
    sem_t, sem_g, sem_w, sem_d = refs[40:44]
    x, y, core = where[0], where[1], where[4]
    copies_t = row_copies(t_in, rows_out, sem_t)
    copies_g = grad_copies(g_in, grads_out, sem_g, y)
    tiles = D // KT

    def wide_copies(i):
        k = pl.ds(pl.multiple_of(i * KT, KT), KT)
        return [
            pltpu.make_async_copy(
                weights[s][n].at[:, k, :], wv.at[s, n, :, k, :], sem_w.at[i, s * 2 + n]
            )
            for s in range(2)
            for n in range(2)
        ]

    far = pl.ds(pl.multiple_of(((y + 2) % NY) * 1536, 128), 1536)
    tall_copies = [
        pltpu.make_async_copy(weights[s][2].at[:, :, far], dv.at[s], sem_d.at[s]) for s in range(2)
    ]
    for copy in copies_t:
        copy.start()
    for i in range(tiles):
        for copy in wide_copies(i):
            copy.start()
    for copy in copies_g + tall_copies:
        copy.start()
    acc_g[0:128, :] = early_g[0:128, :]
    acc_g[128:192, :] = jnp.zeros((64, 1024), F32)
    acc_g[192:256, :] = early_g[128:192, :]
    scales = []
    slot = lax.broadcasted_iota(jnp.int32, (HALF, 256), 1)
    row = lax.broadcasted_iota(jnp.int32, (HALF, 256), 0)
    block = row // 64
    token = ((x - block + NX) % NX) * 128 + core * 64 + (row - block * 64)
    for e in range(2):
        hit = (token == slots_ref[e : e + 1, :]) & (slot < where[5 + e])
        gate = jnp.broadcast_to(gates_ref[e : e + 1, :], (HALF, 256))
        scales.append(jnp.sum(jnp.where(hit, gate, 0.0), axis=1, keepdims=True))
    for copy in copies_t:
        copy.wait()

    @pl.loop(0, tiles)
    def _(i):
        for copy in wide_copies(i):
            copy.wait()
        k = pl.ds(pl.multiple_of(i * KT, KT), KT)
        wide = jnp.concatenate(
            [wv[s, n, e, k, :] for s in range(2) for e in range(2) for n in range(2)], axis=1
        )
        acc_g[128:192, :] += jnp.dot(rows_out[128:192, k], wide, preferred_element_type=F32)

    for copy in copies_g + tall_copies:
        copy.wait()
    tall = jnp.concatenate([dv[s, e] for s in range(2) for e in range(2)], axis=0)
    acc_b[...] = early_b[...] + nt(grads_out[:, far], tall)
    router = [0.0, 0.0]
    for s in range(2):
        for e in range(2):
            j = s * 2 + e
            pre_gate = acc_g[:, j * 256 : j * 256 + H]
            pre_up = acc_g[:, j * 256 + H : (j + 1) * 256]
            back = acc_b[:, j * H : (j + 1) * H]
            scale = scales[e]
            sigma = jax.nn.sigmoid(pre_gate)
            active = pre_gate * sigma
            hidden = active * pre_up
            router[e] += jnp.sum(hidden.astype(BF).astype(F32) * back, axis=1, keepdims=True)
            hidden_grad = back * scale
            gate_delta = (hidden_grad * pre_up * sigma * (1.0 + pre_gate * (1.0 - sigma))).astype(BF)
            up_delta = (hidden_grad * active).astype(BF)
            deltas[:, j * 256 : j * 256 + H] = gate_delta
            deltas[:, j * 256 + H : (j + 1) * 256] = up_delta
            out, at = (own_out, 0) if s == 0 else (rows_out, D)
            out[:, at + e * 256 : at + e * 256 + H] = gate_delta
            out[:, at + e * 256 + H : at + (e + 1) * 256] = up_delta
            at += 512 + e * H
            out[:, at : at + H] = (hidden * scale).astype(BF)
    lane = lax.broadcasted_iota(jnp.int32, (HALF, 128), 1)
    spread = jnp.where(lane == 0, router[0], jnp.where(lane == 1, router[1], 0.0))
    for k in range(NX):
        to = pl.multiple_of(((x - k) % NX) * 64, 64)
        rbuf[pl.ds(to, 64), :] = spread[k * 64 : (k + 1) * 64]
    line = rbuf[...].T[0:2]
    four = [line[e : e + 1, h * 128 : (h + 1) * 128] for e in range(2) for h in range(2)]
    sums = split_three(jnp.concatenate(four + [jnp.zeros((12, 128), F32)], axis=0))
    for out in pa_out:
        out[:, D // 2 :] = jnp.zeros((out.shape[0], 384), BF)
        out[0:16, D // 2 :] = sums

    def partial(i):
        f = pl.ds(pl.multiple_of(i * FT, FT), FT)
        wide = jnp.concatenate(
            [wv[s, n, e, f, :] for s in range(2) for e in range(2) for n in range(2)], axis=1
        )
        return nt(deltas[...], wide)

    half = D // 2 // FT

    @pl.loop(0, half)
    def _(i):
        f = pl.ds(pl.multiple_of(i * FT, FT), FT)
        part = partial(i).astype(BF)
        for out, at in zip(pa_out, (0, 64, 192, 128, 160)):
            out[:, f] = part[at : at + out.shape[0], :]

    @pl.loop(0, half)
    def _(i):
        f = pl.ds(pl.multiple_of(i * FT, FT), FT)
        tile[...] = partial(i + half).astype(BF)
        for out, k, first in zip(pb_out, (0, 1, 3, 2, 2), (0, 0, 0, 0, 2)):
            for b in range(out.shape[0]):
                src = pl.multiple_of((first + b) * 64 + ((y + k) % NY) * 16, 16)
                out[b, :, f] = tile[pl.ds(src, 16), :]


def run_main(where, t, g, weights, slots, gates, early):
    hbm = [pl.BlockSpec(memory_space=pltpu.HBM)]
    out_shape = (
        [jax.ShapeDtypeStruct((64, WIDE), BF)] * 3
        + [jax.ShapeDtypeStruct((32, WIDE), BF)] * 2
        + [jax.ShapeDtypeStruct((4, 16, D // 2), BF)] * 3
        + [jax.ShapeDtypeStruct((2, 16, D // 2), BF)] * 2
        + [jax.ShapeDtypeStruct((HALF, 768), BF)]
        + [jax.ShapeDtypeStruct((HALF, D + 768), BF)]
        + [jax.ShapeDtypeStruct((HALF, D), BF)]
    )
    return pl.pallas_call(
        main_kernel,
        out_shape=out_shape,
        in_specs=[SMEM_SPEC] + hbm * 16 + vmem_specs(4),
        out_specs=vmem_specs(13),
        scratch_shapes=[
            pltpu.VMEM((2, 2, 2, D, H), BF),
            pltpu.VMEM((2, 2, H, 1536), BF),
            pltpu.VMEM((HALF, 1024), F32),
            pltpu.VMEM((HALF, 512), F32),
            pltpu.VMEM((HALF, 1024), BF),
            pltpu.VMEM((HALF, FT), BF),
            pltpu.VMEM((HALF, 128), F32),
            pltpu.SemaphoreType.DMA((5,)),
            pltpu.SemaphoreType.DMA((5,)),
            pltpu.SemaphoreType.DMA((D // KT, 4)),
            pltpu.SemaphoreType.DMA((2,)),
        ],
        compiler_params=pltpu.CompilerParams(vmem_limit_bytes=21 * MIB),
        cost_estimate=pl.CostEstimate(
            flops=8_000_000_000, bytes_accessed=30_000_000, transcendentals=262144
        ),
        name="main",
    )(where, *t, *g, *weights, slots, gates, *early)


def up_kernel(*refs):
    rows_own, rows_sib, own, sib = refs[0:4]
    gate_out, up_out, token = refs[-3:]
    token[...] = jnp.zeros(token.shape, F32)
    part = tn(rows_own[...], own[:, 0:512]) + tn(rows_sib[...], sib[:, 0:512])
    for e in range(2):
        gate_out[e] = part[:, e * 256 : e * 256 + H].astype(BF)
        up_out[e] = part[:, e * 256 + H : (e + 1) * 256].astype(BF)


def run_up(rows_own, rows_sib, own, before):
    tile = pl.BlockSpec((HALF, FT), lambda i: (0, i))
    whole = pl.BlockSpec((HALF, 768), lambda i: (0, 0))
    tail = pl.BlockSpec((HALF, 768), lambda i: (0, D // 768))
    out = pl.BlockSpec((2, FT, H), lambda i: (0, i, 0))
    return pl.pallas_call(
        up_kernel,
        grid=(D // FT,),
        out_shape=[
            jax.ShapeDtypeStruct((2, D, H), BF),
            jax.ShapeDtypeStruct((2, D, H), BF),
            jax.ShapeDtypeStruct((8, 128), F32),
        ],
        in_specs=[tile, tile, whole, tail]
        + [pl.BlockSpec(memory_space=pl.ANY)] * len(before),
        out_specs=[out, out, pl.BlockSpec((8, 128), lambda i: (0, 0))],
        compiler_params=pltpu.CompilerParams(
            dimension_semantics=("arbitrary",), vmem_limit_bytes=16 * MIB
        ),
        cost_estimate=pl.CostEstimate(
            flops=3_200_000_000, bytes_accessed=13_000_000, transcendentals=0
        ),
        name="up_grads",
    )(rows_own, rows_sib, own, rows_sib, *before)


def down_kernel(grads_own, grads_sib, own, sib, out, token, hidden):
    token[...] = jnp.zeros(token.shape, F32)

    @pl.when(pl.program_id(0) == 0)
    def _():
        hidden[:, 0:HALF] = own[:, 512:768].T
        hidden[:, HALF:512] = sib[:, 512:768].T

    part = jnp.dot(hidden[:, 0:HALF], grads_own[...], preferred_element_type=F32)
    part += jnp.dot(hidden[:, HALF:512], grads_sib[...], preferred_element_type=F32)
    for e in range(2):
        out[e] = part[e * H : (e + 1) * H].astype(BF)


def run_down(grads_own, grads_sib, own, rows_sib):
    tile = pl.BlockSpec((HALF, 2 * FT), lambda i: (0, i))
    whole = pl.BlockSpec((HALF, 768), lambda i: (0, 0))
    tail = pl.BlockSpec((HALF, 768), lambda i: (0, D // 768))
    return pl.pallas_call(
        down_kernel,
        grid=(D // FT // 2,),
        out_shape=[
            jax.ShapeDtypeStruct((2, H, D), BF),
            jax.ShapeDtypeStruct((8, 128), F32),
        ],
        in_specs=[tile, tile, whole, tail],
        out_specs=[
            pl.BlockSpec((2, H, 2 * FT), lambda i: (0, 0, i)),
            pl.BlockSpec((8, 128), lambda i: (0, 0)),
        ],
        scratch_shapes=[pltpu.VMEM((256, 512), BF)],
        compiler_params=pltpu.CompilerParams(
            dimension_semantics=("arbitrary",), vmem_limit_bytes=16 * MIB
        ),
        cost_estimate=pl.CostEstimate(
            flops=1_600_000_000, bytes_accessed=10_000_000, transcendentals=0
        ),
        name="down_grads",
    )(grads_own, grads_sib, own, rows_sib)


def middle_sum_kernel(*refs):
    a_down, a_up, b_up, b_down = refs[0:4]
    low_a, high_a, low_b, high_b = refs[4:8]
    out_a_down, out_a_up, out_b_up, out_b_down = refs[8:12]
    half = D // 2
    out_a_down[0:32, 0:half] = total(a_down[0:32, 0:half], [low_a[:, 0:half]]).astype(BF)
    out_a_down[32:64, :] = a_down[32:64, :]
    sums = join_three(a_down[0:16, half:]) + join_three(low_a[0:16, half:])
    out_a_down[0:16, half:] = split_three(sums)
    out_a_down[16:32, half:] = a_down[16:32, half:]
    out_a_up[0:32, :] = a_up[0:32, :]
    out_a_up[32:64, :] = total(a_up[32:64, :], [high_a[...]]).astype(BF)
    for k in range(2):
        out_b_up[k] = total(b_up[k], [low_b[k]]).astype(BF)
        out_b_up[2 + k] = b_up[2 + k]
        out_b_down[k] = b_down[k]
        out_b_down[2 + k] = total(b_down[2 + k], [high_b[k]]).astype(BF)


def run_middle_sum(blocks, halves):
    return pl.pallas_call(
        middle_sum_kernel,
        out_shape=[jax.ShapeDtypeStruct((64, WIDE), BF)] * 2
        + [jax.ShapeDtypeStruct((4, 16, D // 2), BF)] * 2,
        in_specs=vmem_specs(8),
        out_specs=vmem_specs(4),
        compiler_params=pltpu.CompilerParams(vmem_limit_bytes=8 * MIB),
        name="middle_sum",
    )(*blocks, *halves)


def first_sum_kernel(where, *refs):
    ra, rb, qa, qb, buf = refs[0:3], refs[3:6], refs[7:11], refs[11:15], refs[15]
    half = D // 2
    buf[...] = total(ra[0][:, 0:half], [r[:, 0:half] for r in ra[1:]]).astype(BF)
    sums = join_three(ra[0][0:16, half:])
    for r in ra[1:]:
        sums += join_three(r[0:16, half:])
    sums = split_three(sums)
    for k in range(NY):
        start = pl.multiple_of(((where[1] + k) % NY) * 16, 16)
        qa[k][:, 0:half] = buf[pl.ds(start, 16), :]
        qa[k][:, half:] = sums
    for k in range(NX):
        qb[k][...] = total(rb[0][k], [r[k] for r in rb[1:]]).astype(BF)


def run_first_sum(where, ra, rb, token):
    return pl.pallas_call(
        first_sum_kernel,
        out_shape=[jax.ShapeDtypeStruct((16, WIDE), BF)] * 4
        + [jax.ShapeDtypeStruct((16, D // 2), BF)] * 4,
        in_specs=[SMEM_SPEC] + vmem_specs(7),
        out_specs=vmem_specs(8),
        scratch_shapes=[pltpu.VMEM((64, D // 2), BF)],
        compiler_params=pltpu.CompilerParams(vmem_limit_bytes=8 * MIB),
        name="first_sum",
    )(where, *ra, *rb, token)


def second_sum_kernel(where, *refs):
    ra, rb, own, out, buf = refs[0:4], refs[4:8], refs[9], refs[10:13], refs[13]
    half = D // 2
    for n, r in enumerate((ra, rb)):
        part = total(r[0][:, 0:half], [p[:, 0:half] for p in r[1:]])
        for k in range(NZ):
            buf[k, :, n * half : (n + 1) * half] = part[4 * k : 4 * k + 4]
    sums = join_three(ra[0][:, half:])
    for r in ra[1:]:
        sums += join_three(r[:, half:])
    parts = split_three(sums)[0:4]
    for k in range(NZ):
        rows = buf[(where[2] + k) % NZ]
        if k == 0:
            own[:, 0:D] = rows
            own[:, D:] = sums[0:4]
        else:
            out[k - 1][:, 0:D] = rows.astype(BF)
            out[k - 1][:, D:] = parts


def run_second_sum(where, ra, rb, token):
    return pl.pallas_call(
        second_sum_kernel,
        out_shape=[jax.ShapeDtypeStruct((4, D + 128), F32)]
        + [jax.ShapeDtypeStruct((4, D + 384), BF)] * 3,
        in_specs=[SMEM_SPEC] + vmem_specs(9),
        out_specs=vmem_specs(4),
        scratch_shapes=[pltpu.VMEM((NZ, 4, D), F32)],
        compiler_params=pltpu.CompilerParams(vmem_limit_bytes=8 * MIB),
        name="second_sum",
    )(where, *ra, *rb, token)


def last_sum_kernel(own, *refs):
    out, sums_out = refs[3], refs[4]
    out[...] = total(own[:, 0:D], [r[:, 0:D] for r in refs[0:3]]).astype(BF)
    sums = own[:, D:]
    for r in refs[0:3]:
        sums += join_three(r[:, D:])
    sums_out[0:4, :] = sums
    sums_out[4:8, :] = jnp.zeros((4, 128), F32)


def run_last_sum(pieces):
    return pl.pallas_call(
        last_sum_kernel,
        out_shape=[jax.ShapeDtypeStruct((4, D), BF), jax.ShapeDtypeStruct((8, 128), F32)],
        in_specs=vmem_specs(4),
        out_specs=vmem_specs(2),
        compiler_params=pltpu.CompilerParams(vmem_limit_bytes=4 * MIB),
        name="last_sum",
    )(*pieces)


def router_kernel(where, own, other, slots_ref, out):
    first = jnp.where(where[4] == 0, own[...], other[...])
    second = jnp.where(where[4] == 0, other[...], own[...])
    slots = slots_ref[...].T
    index = lax.broadcasted_iota(jnp.int32, (256, 128), 1)
    spread = jnp.zeros((256, 128), F32)
    for e in range(2):
        picked = jnp.zeros((256, 1), F32)
        for core, values in enumerate((first, second)):
            for h in range(2):
                at = index + h * 128
                token = (at // 64) * 128 + core * 64 + at % 64
                hit = slots[:, e : e + 1] == token
                line = jnp.broadcast_to(values[2 * e + h : 2 * e + h + 1, :], (256, 128))
                picked += jnp.sum(jnp.where(hit, line, 0.0), axis=1, keepdims=True)
        spread = jnp.where(index == e, picked, spread)
    lines = spread.T
    at = lax.broadcasted_iota(jnp.int32, (1, 256), 1)
    for e in range(2):
        out[e : e + 1, :] = jnp.where(at < where[5 + e], lines[e : e + 1, :], 0.0)


def run_router(where, own, other, slots):
    return pl.pallas_call(
        router_kernel,
        out_shape=jax.ShapeDtypeStruct((2, 256), F32),
        in_specs=[SMEM_SPEC] + vmem_specs(3),
        out_specs=vmem_specs(1)[0],
        compiler_params=pltpu.CompilerParams(vmem_limit_bytes=4 * MIB),
        name="router",
    )(where, own, other, slots)


def on_device(
    tokens_in, out_grad, gate_weight, up_weight, down_weight, slot_tokens, slot_counts, slot_gates
):
    x, c, y, z = position()
    where = jnp.stack([x, y, z, c, c, slot_counts[0], slot_counts[1]]).astype(jnp.int32)
    gate_sib, up_sib = swap(gate_weight), swap(up_weight)

    packed = run_pack(tokens_in, out_grad)
    packed = [packed] + [shift(packed, "z", k) for k in (1, 2, 3)]
    t16, g64 = run_first_stage(where, packed, [gate_sib, up_sib])
    down_sib = swap(run_relay(down_weight, [t16]))
    t_low, t_high = shift(t16, "y", 1), shift(t16, "y", -1)
    g_low, g_high = shift(g64, "x", 1), shift(g64, "x", -1)
    a, b, e, f = run_near_halves(t_low, t_high, g_low, g_high)
    t = (t16, t_low, t_high, shift(a, "y", 1), shift(b, "y", -1))
    g = (g64, g_low, g_high, shift(e, "x", 1), shift(f, "x", -1))
    t64, g256 = run_second_stage(where, t, g)
    t_low, t_high = shift(t64, "x", 1), shift(t64, "x", -1)
    g_low, g_high = shift(g256, "y", 1), shift(g256, "y", -1)
    a, b, e, f = run_halves(t_low, t_high, g_low, g_high)
    t = (t64, t_low, t_high, shift(a, "x", 1), shift(b, "x", -1))
    g = (g256, g_low, g_high, shift(e, "y", 1), shift(f, "y", -1))
    weights = (gate_weight, up_weight, down_weight, gate_sib, up_sib, down_sib)
    early = run_early(where, t[0:3], g[0:3], weights)
    outs = run_main(where, t, g, weights, slot_tokens, slot_gates, early)
    a_own, a_down, a_up, a_low, a_high = outs[0:5]
    b_own, b_up, b_down, b_low, b_high = outs[5:10]
    dl_own, rows, grads = outs[10:]

    halves = [shift(a_low, "x", -1), shift(a_high, "x", 1)]
    halves += [shift(b_low, "y", 1), shift(b_high, "y", -1)]
    rows_sib = swap(run_relay(rows, halves))
    a_down, a_up, b_up, b_down = run_middle_sum((a_down, a_up, b_up, b_down), halves)
    gate_grad, up_grad, token = run_up(rows, rows_sib, dl_own, [a_down])
    ra = [a_own, shift(a_down, "x", -1), shift(a_up, "x", 1)]
    rb = [b_own, shift(b_up, "y", 1), shift(b_down, "y", -1)]
    q = run_first_sum(where, ra, rb, token)
    qa, qb = q[0:4], q[4:8]
    grads_sib = swap(run_relay(grads, [qa[0]]))
    ra = [qa[0]] + [shift(qa[k], "y", k) for k in (1, 2, 3)]
    rb = [qb[0]] + [shift(qb[k], "x", -k) for k in (1, 2, 3)]
    down_grad, token = run_down(grads, grads_sib, dl_own, rows_sib)
    q = run_second_sum(where, ra, rb, token)
    input_grad, sums = run_last_sum([q[0]] + [shift(q[k], "z", k) for k in (1, 2, 3)])
    router_grad = run_router(where, sums, swap(sums), slot_tokens)
    return (input_grad, gate_grad, up_grad, down_grad, router_grad)


def solution(mesh):
    return jax.shard_map(
        on_device,
        mesh=mesh,
        in_specs=(
            P(("section", "et"), None),
            P("section", "et"),
            P(None, None, ("section", "et")),
            P(None, None, ("section", "et")),
            P(None, ("section", "et"), None),
            P(),
            P(),
            P(),
        ),
        out_specs=(
            P(("section", "et"), None),
            P(None, None, ("section", "et")),
            P(None, None, ("section", "et")),
            P(None, ("section", "et"), None),
            P(),
        ),
        check_vma=False,
    )
```

```python
import jax
import jax.numpy as jnp
from jax import lax
from jax.experimental import pallas as pl
from jax.experimental.pallas import tpu as pltpu
from jax.sharding import PartitionSpec as P

AXES = ("section", "et")
BF = jnp.bfloat16
F32 = jnp.float32
D = 6144
NX, NC, NY, NZ = 4, 2, 4, 4
H = 128
SHORT = 64
HALF = 256


def linear(x, c, y, z):
    return ((x * NC + c) * NY + y) * NZ + z


def shift_pairs(axis, step):
    pairs = []
    for x in range(NX):
        for c in range(NC):
            for y in range(NY):
                for z in range(NZ):
                    to = {
                        "x": ((x + step) % NX, c, y, z),
                        "y": (x, c, (y + step) % NY, z),
                        "z": (x, c, y, (z + step) % NZ),
                    }[axis]
                    pairs.append((linear(x, c, y, z), linear(*to)))
    return pairs


def shift(value, axis, step):
    return lax.ppermute(value, AXES, shift_pairs(axis, step))


def swap(value):
    pairs = [
        (linear(x, c, y, z), linear(x, 1 - c, y, z))
        for x in range(NX)
        for c in range(NC)
        for y in range(NY)
        for z in range(NZ)
    ]
    return lax.ppermute(value, AXES, pairs)


def position():
    section = lax.axis_index("section")
    et = lax.axis_index("et")
    return section // NC, section % NC, et // NZ, et % NZ


def nt(left, right):
    return lax.dot_general(left, right, (((1,), (1,)), ((), ())), preferred_element_type=F32)


def tn(left, right):
    return lax.dot_general(left, right, (((0,), (0,)), ((), ())), preferred_element_type=F32)


def total(first, rest):
    out = first.astype(F32)
    for r in rest:
        out = out + r.astype(F32)
    return out


KT = 1024
FT = 512
MIB = 2**20
WIDE = D // 2 + 384


def vmem_specs(n):
    return [pl.BlockSpec(memory_space=pltpu.VMEM)] * n


SMEM_SPEC = pl.BlockSpec(memory_space=pltpu.SMEM)


def pack_kernel(tokens, grads, out):
    out[0:64, :] = grads[...]
    rows = tokens[...].astype(F32)
    for b in range(0, 16, 4):
        four = [rows[:, (b + i) * 384 : (b + i + 1) * 384] for i in range(4)]
        out[64 + 4 * b : 80 + 4 * b, :] = jnp.concatenate(four, axis=0).astype(BF)


def run_pack(tokens, grads):
    return pl.pallas_call(
        pack_kernel,
        out_shape=jax.ShapeDtypeStruct((128, 384), BF),
        in_specs=vmem_specs(2),
        out_specs=vmem_specs(1)[0],
        compiler_params=pltpu.CompilerParams(vmem_limit_bytes=4 * MIB),
        name="pack",
    )(tokens, grads)


def first_stage_kernel(where, *refs):
    packed, t_out, g_out, buf = refs[0:4], refs[-3], refs[-2], refs[-1]
    for k in range(NZ):
        at = (where[2] - k) % NZ
        rows = packed[k][64:128, :].astype(F32)
        for b in range(16):
            buf[at, :, 384 * b : 384 * (b + 1)] = rows[4 * b : 4 * b + 4]
        start = pl.multiple_of(384 * at, 128)
        g_out[:, pl.ds(start, 384)] = packed[k][0:64, :]
    t_out[...] = jnp.concatenate([buf[k] for k in range(NZ)], axis=0).astype(BF)


def run_first_stage(where, packed, before):
    return pl.pallas_call(
        first_stage_kernel,
        out_shape=[jax.ShapeDtypeStruct((16, D), BF), jax.ShapeDtypeStruct((64, 1536), BF)],
        in_specs=[SMEM_SPEC] + vmem_specs(4) + [pl.BlockSpec(memory_space=pl.ANY)] * len(before),
        out_specs=vmem_specs(2),
        scratch_shapes=[pltpu.VMEM((NZ, 4, D), F32)],
        compiler_params=pltpu.CompilerParams(vmem_limit_bytes=4 * MIB),
        name="first_stage",
    )(where, *packed, *before)


def near_halves_kernel(t_low, t_high, g_low, g_high, a, b, c, d):
    a[...] = t_low[:, 0 : D // 2]
    b[...] = t_high[:, D // 2 : D]
    c[...] = g_low[0:32, :]
    d[...] = g_high[32:64, :]


def run_near_halves(t_low, t_high, g_low, g_high):
    return pl.pallas_call(
        near_halves_kernel,
        out_shape=[jax.ShapeDtypeStruct((16, D // 2), BF)] * 2
        + [jax.ShapeDtypeStruct((32, 1536), BF)] * 2,
        in_specs=vmem_specs(4),
        out_specs=vmem_specs(4),
        compiler_params=pltpu.CompilerParams(vmem_limit_bytes=4 * MIB),
        name="near_halves",
    )(t_low, t_high, g_low, g_high)


def second_stage_kernel(where, *refs):
    t, g, t_out, g_out = refs[0:5], refs[5:10], refs[10], refs[11]
    y = where[1]
    for piece, step in zip(t[0:3], (0, -1, 1)):
        start = pl.multiple_of(16 * ((y + step + NY) % NY), 16)
        t_out[pl.ds(start, 16), :] = piece[...]
    start = pl.multiple_of(16 * ((y + 2) % NY), 16)
    t_out[pl.ds(start, 16), 0 : D // 2] = t[3][...]
    t_out[pl.ds(start, 16), D // 2 : D] = t[4][...]
    for piece, at in zip(g, (0, 64, 192, 128, 160)):
        g_out[at : at + piece.shape[0], :] = piece[...]


def run_second_stage(where, t, g):
    return pl.pallas_call(
        second_stage_kernel,
        out_shape=[jax.ShapeDtypeStruct((64, D), BF), jax.ShapeDtypeStruct((HALF, 1536), BF)],
        in_specs=[SMEM_SPEC] + vmem_specs(10),
        out_specs=vmem_specs(2),
        compiler_params=pltpu.CompilerParams(vmem_limit_bytes=4 * MIB),
        name="second_stage",
    )(where, *t, *g)


def halves_kernel(t_low, t_high, g_low, g_high, a, b, c, d):
    a[...] = t_low[0:32, :]
    b[...] = t_high[32:64, :]
    c[...] = g_low[0:128, :]
    d[...] = g_high[128:256, :]


def run_halves(t_low, t_high, g_low, g_high):
    return pl.pallas_call(
        halves_kernel,
        out_shape=[jax.ShapeDtypeStruct((32, D), BF)] * 2
        + [jax.ShapeDtypeStruct((128, 1536), BF)] * 2,
        in_specs=vmem_specs(4),
        out_specs=vmem_specs(4),
        compiler_params=pltpu.CompilerParams(vmem_limit_bytes=4 * MIB),
        name="halves",
    )(t_low, t_high, g_low, g_high)


def relay_kernel(*refs):
    value, (out, sem) = refs[0], refs[-2:]
    copy = pltpu.make_async_copy(value, out, sem)
    copy.start()
    copy.wait()


def run_relay(value, before):
    hbm = [pl.BlockSpec(memory_space=pltpu.HBM)]
    return pl.pallas_call(
        relay_kernel,
        out_shape=jax.ShapeDtypeStruct(value.shape, value.dtype),
        in_specs=hbm * (1 + len(before)),
        out_specs=hbm[0],
        scratch_shapes=[pltpu.SemaphoreType.DMA],
        compiler_params=pltpu.CompilerParams(vmem_limit_bytes=1 * MIB),
        cost_estimate=pl.CostEstimate(flops=0, bytes_accessed=6_000_000, transcendentals=0),
        name="relay",
    )(value, *before)


def row_copies(pieces, rows, sem):
    places = (0, 64, 192, 128, 160)
    return [
        pltpu.make_async_copy(
            piece, rows.at[pl.ds(at, piece.shape[0]), pl.ds(0, D)], sem.at[r]
        )
        for r, (piece, at) in enumerate(zip(pieces, places))
    ]


def grad_copies(pieces, grads, sem, y):
    places = ((0, 0), (-1, 0), (1, 0), (2, 0), (2, 128))
    copies = []
    for j, (piece, (step, at)) in enumerate(zip(pieces, places)):
        start = pl.multiple_of(((y + step + NY) % NY) * 1536, 128)
        copies.append(
            pltpu.make_async_copy(
                piece, grads.at[pl.ds(at, piece.shape[0]), pl.ds(start, 1536)], sem.at[j]
            )
        )
    return copies


def split_three(value):
    high = value.astype(BF)
    rest = value - high.astype(F32)
    middle = rest.astype(BF)
    low = (rest - middle.astype(F32)).astype(BF)
    return jnp.concatenate([high, middle, low], axis=1)


def join_three(parts):
    out = parts.astype(F32)
    return out[:, 0:128] + out[:, 128:256] + out[:, 256:384]


def early_kernel(where, *refs):
    t, g, weights = refs[0:3], refs[3:6], (refs[6:9], refs[9:12])
    acc_g, acc_b, wv, dv, sem_w, sem_d = refs[12:18]
    y = where[1]
    tiles = D // KT

    def wide_copies(i):
        k = pl.ds(pl.multiple_of(i * KT, KT), KT)
        return [
            pltpu.make_async_copy(
                weights[s][n].at[:, k, :], wv.at[s, n, :, k, :], sem_w.at[i, s * 2 + n]
            )
            for s in range(2)
            for n in range(2)
        ]

    tall_copies = []
    for j, step in enumerate((0, -1, 1)):
        block = pl.ds(pl.multiple_of(((y + step + NY) % NY) * 1536, 128), 1536)
        tall_copies.append(
            [
                pltpu.make_async_copy(weights[s][2].at[:, :, block], dv.at[j, s], sem_d.at[j, s])
                for s in range(2)
            ]
        )
    for i in range(tiles):
        for copy in wide_copies(i):
            copy.start()
    for group in tall_copies:
        for copy in group:
            copy.start()
    acc_g[...] = jnp.zeros(acc_g.shape, F32)
    acc_b[...] = jnp.zeros(acc_b.shape, F32)

    @pl.loop(0, tiles)
    def _(i):
        for copy in wide_copies(i):
            copy.wait()
        k = pl.ds(pl.multiple_of(i * KT, KT), KT)
        wide = jnp.concatenate(
            [wv[s, n, e, k, :] for s in range(2) for e in range(2) for n in range(2)], axis=1
        )
        rows = jnp.concatenate([piece[:, k] for piece in t], axis=0)
        acc_g[...] += jnp.dot(rows, wide, preferred_element_type=F32)

    for j, group in enumerate(tall_copies):
        for copy in group:
            copy.wait()
        tall = jnp.concatenate([dv[j, s, e] for s in range(2) for e in range(2)], axis=0)
        acc_b[...] += nt(g[j][...], tall)


def run_early(where, t, g, weights):
    hbm = [pl.BlockSpec(memory_space=pltpu.HBM)]
    return pl.pallas_call(
        early_kernel,
        out_shape=[
            jax.ShapeDtypeStruct((192, 1024), F32),
            jax.ShapeDtypeStruct((HALF, 512), F32),
        ],
        in_specs=[SMEM_SPEC] + vmem_specs(6) + hbm * 6,
        out_specs=vmem_specs(2),
        scratch_shapes=[
            pltpu.VMEM((2, 2, 2, D, H), BF),
            pltpu.VMEM((3, 2, 2, H, 1536), BF),
            pltpu.SemaphoreType.DMA((D // KT, 4)),
            pltpu.SemaphoreType.DMA((3, 2)),
        ],
        compiler_params=pltpu.CompilerParams(vmem_limit_bytes=22 * MIB),
        cost_estimate=pl.CostEstimate(
            flops=3_600_000_000, bytes_accessed=20_000_000, transcendentals=0
        ),
        name="early",
    )(where, *t, *g, *weights)


def main_kernel(where, *refs):
    t_in, g_in = refs[0:5], refs[5:10]
    weights = (refs[10:13], refs[13:16])
    slots_ref, gates_ref, early_g, early_b = refs[16:20]
    pa_out, pb_out = refs[20:25], refs[25:30]
    own_out, rows_out, grads_out = refs[30:33]
    wv, dv, acc_g, acc_b, deltas, tile, rbuf = refs[33:40]
    sem_t, sem_g, sem_w, sem_d = refs[40:44]
    x, y, core = where[0], where[1], where[4]
    copies_t = row_copies(t_in, rows_out, sem_t)
    copies_g = grad_copies(g_in, grads_out, sem_g, y)
    tiles = D // KT

    def wide_copies(i):
        k = pl.ds(pl.multiple_of(i * KT, KT), KT)
        return [
            pltpu.make_async_copy(
                weights[s][n].at[:, k, :], wv.at[s, n, :, k, :], sem_w.at[i, s * 2 + n]
            )
            for s in range(2)
            for n in range(2)
        ]

    far = pl.ds(pl.multiple_of(((y + 2) % NY) * 1536, 128), 1536)
    tall_copies = [
        pltpu.make_async_copy(weights[s][2].at[:, :, far], dv.at[s], sem_d.at[s]) for s in range(2)
    ]
    for copy in copies_t:
        copy.start()
    for i in range(tiles):
        for copy in wide_copies(i):
            copy.start()
    for copy in copies_g + tall_copies:
        copy.start()
    acc_g[0:128, :] = early_g[0:128, :]
    acc_g[128:192, :] = jnp.zeros((64, 1024), F32)
    acc_g[192:256, :] = early_g[128:192, :]
    scales = []
    slot = lax.broadcasted_iota(jnp.int32, (HALF, 256), 1)
    row = lax.broadcasted_iota(jnp.int32, (HALF, 256), 0)
    block = row // 64
    token = ((x - block + NX) % NX) * 128 + core * 64 + (row - block * 64)
    for e in range(2):
        hit = (token == slots_ref[e : e + 1, :]) & (slot < where[5 + e])
        gate = jnp.broadcast_to(gates_ref[e : e + 1, :], (HALF, 256))
        scales.append(jnp.sum(jnp.where(hit, gate, 0.0), axis=1, keepdims=True))
    for copy in copies_t:
        copy.wait()

    @pl.loop(0, tiles)
    def _(i):
        for copy in wide_copies(i):
            copy.wait()
        k = pl.ds(pl.multiple_of(i * KT, KT), KT)
        wide = jnp.concatenate(
            [wv[s, n, e, k, :] for s in range(2) for e in range(2) for n in range(2)], axis=1
        )
        acc_g[128:192, :] += jnp.dot(rows_out[128:192, k], wide, preferred_element_type=F32)

    for copy in copies_g + tall_copies:
        copy.wait()
    tall = jnp.concatenate([dv[s, e] for s in range(2) for e in range(2)], axis=0)
    acc_b[...] = early_b[...] + nt(grads_out[:, far], tall)
    router = [0.0, 0.0]
    for s in range(2):
        for e in range(2):
            j = s * 2 + e
            pre_gate = acc_g[:, j * 256 : j * 256 + H]
            pre_up = acc_g[:, j * 256 + H : (j + 1) * 256]
            back = acc_b[:, j * H : (j + 1) * H]
            scale = scales[e]
            sigma = jax.nn.sigmoid(pre_gate)
            active = pre_gate * sigma
            hidden = active * pre_up
            router[e] += jnp.sum(hidden.astype(BF).astype(F32) * back, axis=1, keepdims=True)
            hidden_grad = back * scale
            gate_delta = (hidden_grad * pre_up * sigma * (1.0 + pre_gate * (1.0 - sigma))).astype(BF)
            up_delta = (hidden_grad * active).astype(BF)
            deltas[:, j * 256 : j * 256 + H] = gate_delta
            deltas[:, j * 256 + H : (j + 1) * 256] = up_delta
            out, at = (own_out, 0) if s == 0 else (rows_out, D)
            out[:, at + e * 256 : at + e * 256 + H] = gate_delta
            out[:, at + e * 256 + H : at + (e + 1) * 256] = up_delta
            at += 512 + e * H
            out[:, at : at + H] = (hidden * scale).astype(BF)
    lane = lax.broadcasted_iota(jnp.int32, (HALF, 128), 1)
    spread = jnp.where(lane == 0, router[0], jnp.where(lane == 1, router[1], 0.0))
    for k in range(NX):
        to = pl.multiple_of(((x - k) % NX) * 64, 64)
        rbuf[pl.ds(to, 64), :] = spread[k * 64 : (k + 1) * 64]
    line = rbuf[...].T[0:2]
    four = [line[e : e + 1, h * 128 : (h + 1) * 128] for e in range(2) for h in range(2)]
    sums = split_three(jnp.concatenate(four + [jnp.zeros((12, 128), F32)], axis=0))
    for out in pa_out:
        out[:, D // 2 :] = jnp.zeros((out.shape[0], 384), BF)
        out[0:16, D // 2 :] = sums

    def partial(i):
        f = pl.ds(pl.multiple_of(i * FT, FT), FT)
        wide = jnp.concatenate(
            [wv[s, n, e, f, :] for s in range(2) for e in range(2) for n in range(2)], axis=1
        )
        return nt(deltas[...], wide)

    half = D // 2 // FT

    @pl.loop(0, half)
    def _(i):
        f = pl.ds(pl.multiple_of(i * FT, FT), FT)
        part = partial(i).astype(BF)
        for out, at in zip(pa_out, (0, 64, 192, 128, 160)):
            out[:, f] = part[at : at + out.shape[0], :]

    @pl.loop(0, half)
    def _(i):
        f = pl.ds(pl.multiple_of(i * FT, FT), FT)
        tile[...] = partial(i + half).astype(BF)
        for out, k, first in zip(pb_out, (0, 1, 3, 2, 2), (0, 0, 0, 0, 2)):
            for b in range(out.shape[0]):
                src = pl.multiple_of((first + b) * 64 + ((y + k) % NY) * 16, 16)
                out[b, :, f] = tile[pl.ds(src, 16), :]


def run_main(where, t, g, weights, slots, gates, early):
    hbm = [pl.BlockSpec(memory_space=pltpu.HBM)]
    out_shape = (
        [jax.ShapeDtypeStruct((64, WIDE), BF)] * 3
        + [jax.ShapeDtypeStruct((32, WIDE), BF)] * 2
        + [jax.ShapeDtypeStruct((4, 16, D // 2), BF)] * 3
        + [jax.ShapeDtypeStruct((2, 16, D // 2), BF)] * 2
        + [jax.ShapeDtypeStruct((HALF, 768), BF)]
        + [jax.ShapeDtypeStruct((HALF, D + 768), BF)]
        + [jax.ShapeDtypeStruct((HALF, D), BF)]
    )
    return pl.pallas_call(
        main_kernel,
        out_shape=out_shape,
        in_specs=[SMEM_SPEC] + hbm * 16 + vmem_specs(4),
        out_specs=vmem_specs(13),
        scratch_shapes=[
            pltpu.VMEM((2, 2, 2, D, H), BF),
            pltpu.VMEM((2, 2, H, 1536), BF),
            pltpu.VMEM((HALF, 1024), F32),
            pltpu.VMEM((HALF, 512), F32),
            pltpu.VMEM((HALF, 1024), BF),
            pltpu.VMEM((HALF, FT), BF),
            pltpu.VMEM((HALF, 128), F32),
            pltpu.SemaphoreType.DMA((5,)),
            pltpu.SemaphoreType.DMA((5,)),
            pltpu.SemaphoreType.DMA((D // KT, 4)),
            pltpu.SemaphoreType.DMA((2,)),
        ],
        compiler_params=pltpu.CompilerParams(vmem_limit_bytes=21 * MIB),
        cost_estimate=pl.CostEstimate(
            flops=8_000_000_000, bytes_accessed=30_000_000, transcendentals=262144
        ),
        name="main",
    )(where, *t, *g, *weights, slots, gates, *early)


def up_kernel(*refs):
    rows_own, rows_sib, own, sib = refs[0:4]
    gate_out, up_out, token = refs[-3:]
    token[...] = jnp.zeros(token.shape, F32)
    part = tn(rows_own[...], own[:, 0:512]) + tn(rows_sib[...], sib[:, 0:512])
    for e in range(2):
        gate_out[e] = part[:, e * 256 : e * 256 + H].astype(BF)
        up_out[e] = part[:, e * 256 + H : (e + 1) * 256].astype(BF)


def run_up(rows_own, rows_sib, own, before):
    tile = pl.BlockSpec((HALF, FT), lambda i: (0, i))
    whole = pl.BlockSpec((HALF, 768), lambda i: (0, 0))
    tail = pl.BlockSpec((HALF, 768), lambda i: (0, D // 768))
    out = pl.BlockSpec((2, FT, H), lambda i: (0, i, 0))
    return pl.pallas_call(
        up_kernel,
        grid=(D // FT,),
        out_shape=[
            jax.ShapeDtypeStruct((2, D, H), BF),
            jax.ShapeDtypeStruct((2, D, H), BF),
            jax.ShapeDtypeStruct((8, 128), F32),
        ],
        in_specs=[tile, tile, whole, tail]
        + [pl.BlockSpec(memory_space=pl.ANY)] * len(before),
        out_specs=[out, out, pl.BlockSpec((8, 128), lambda i: (0, 0))],
        compiler_params=pltpu.CompilerParams(
            dimension_semantics=("arbitrary",), vmem_limit_bytes=16 * MIB
        ),
        cost_estimate=pl.CostEstimate(
            flops=3_200_000_000, bytes_accessed=13_000_000, transcendentals=0
        ),
        name="up_grads",
    )(rows_own, rows_sib, own, rows_sib, *before)


def down_kernel(grads_own, grads_sib, own, sib, out, token, hidden):
    token[...] = jnp.zeros(token.shape, F32)

    @pl.when(pl.program_id(0) == 0)
    def _():
        hidden[:, 0:HALF] = own[:, 512:768].T
        hidden[:, HALF:512] = sib[:, 512:768].T

    part = jnp.dot(hidden[:, 0:HALF], grads_own[...], preferred_element_type=F32)
    part += jnp.dot(hidden[:, HALF:512], grads_sib[...], preferred_element_type=F32)
    for e in range(2):
        out[e] = part[e * H : (e + 1) * H].astype(BF)


def run_down(grads_own, grads_sib, own, rows_sib):
    tile = pl.BlockSpec((HALF, 2 * FT), lambda i: (0, i))
    whole = pl.BlockSpec((HALF, 768), lambda i: (0, 0))
    tail = pl.BlockSpec((HALF, 768), lambda i: (0, D // 768))
    return pl.pallas_call(
        down_kernel,
        grid=(D // FT // 2,),
        out_shape=[
            jax.ShapeDtypeStruct((2, H, D), BF),
            jax.ShapeDtypeStruct((8, 128), F32),
        ],
        in_specs=[tile, tile, whole, tail],
        out_specs=[
            pl.BlockSpec((2, H, 2 * FT), lambda i: (0, 0, i)),
            pl.BlockSpec((8, 128), lambda i: (0, 0)),
        ],
        scratch_shapes=[pltpu.VMEM((256, 512), BF)],
        compiler_params=pltpu.CompilerParams(
            dimension_semantics=("arbitrary",), vmem_limit_bytes=16 * MIB
        ),
        cost_estimate=pl.CostEstimate(
            flops=1_600_000_000, bytes_accessed=10_000_000, transcendentals=0
        ),
        name="down_grads",
    )(grads_own, grads_sib, own, rows_sib)


def middle_sum_kernel(*refs):
    a_down, a_up, b_up, b_down = refs[0:4]
    low_a, high_a, low_b, high_b = refs[4:8]
    out_a_down, out_a_up, out_b_up, out_b_down = refs[8:12]
    half = D // 2
    out_a_down[0:32, 0:half] = total(a_down[0:32, 0:half], [low_a[:, 0:half]]).astype(BF)
    out_a_down[32:64, :] = a_down[32:64, :]
    sums = join_three(a_down[0:16, half:]) + join_three(low_a[0:16, half:])
    out_a_down[0:16, half:] = split_three(sums)
    out_a_down[16:32, half:] = a_down[16:32, half:]
    out_a_up[0:32, :] = a_up[0:32, :]
    out_a_up[32:64, :] = total(a_up[32:64, :], [high_a[...]]).astype(BF)
    for k in range(2):
        out_b_up[k] = total(b_up[k], [low_b[k]]).astype(BF)
        out_b_up[2 + k] = b_up[2 + k]
        out_b_down[k] = b_down[k]
        out_b_down[2 + k] = total(b_down[2 + k], [high_b[k]]).astype(BF)


def run_middle_sum(blocks, halves):
    return pl.pallas_call(
        middle_sum_kernel,
        out_shape=[jax.ShapeDtypeStruct((64, WIDE), BF)] * 2
        + [jax.ShapeDtypeStruct((4, 16, D // 2), BF)] * 2,
        in_specs=vmem_specs(8),
        out_specs=vmem_specs(4),
        compiler_params=pltpu.CompilerParams(vmem_limit_bytes=8 * MIB),
        name="middle_sum",
    )(*blocks, *halves)


def first_sum_kernel(where, *refs):
    ra, rb, qa, qb, buf = refs[0:3], refs[3:6], refs[7:11], refs[11:15], refs[15]
    half = D // 2
    buf[...] = total(ra[0][:, 0:half], [r[:, 0:half] for r in ra[1:]]).astype(BF)
    sums = join_three(ra[0][0:16, half:])
    for r in ra[1:]:
        sums += join_three(r[0:16, half:])
    sums = split_three(sums)
    for k in range(NY):
        start = pl.multiple_of(((where[1] + k) % NY) * 16, 16)
        qa[k][:, 0:half] = buf[pl.ds(start, 16), :]
        qa[k][:, half:] = sums
    for k in range(NX):
        qb[k][...] = total(rb[0][k], [r[k] for r in rb[1:]]).astype(BF)


def run_first_sum(where, ra, rb, token):
    return pl.pallas_call(
        first_sum_kernel,
        out_shape=[jax.ShapeDtypeStruct((16, WIDE), BF)] * 4
        + [jax.ShapeDtypeStruct((16, D // 2), BF)] * 4,
        in_specs=[SMEM_SPEC] + vmem_specs(7),
        out_specs=vmem_specs(8),
        scratch_shapes=[pltpu.VMEM((64, D // 2), BF)],
        compiler_params=pltpu.CompilerParams(vmem_limit_bytes=8 * MIB),
        name="first_sum",
    )(where, *ra, *rb, token)


def second_sum_kernel(where, *refs):
    ra, rb, own, out, buf = refs[0:4], refs[4:8], refs[9], refs[10:13], refs[13]
    half = D // 2
    for n, r in enumerate((ra, rb)):
        part = total(r[0][:, 0:half], [p[:, 0:half] for p in r[1:]])
        for k in range(NZ):
            buf[k, :, n * half : (n + 1) * half] = part[4 * k : 4 * k + 4]
    sums = join_three(ra[0][:, half:])
    for r in ra[1:]:
        sums += join_three(r[:, half:])
    parts = split_three(sums)[0:4]
    for k in range(NZ):
        rows = buf[(where[2] + k) % NZ]
        if k == 0:
            own[:, 0:D] = rows
            own[:, D:] = sums[0:4]
        else:
            out[k - 1][:, 0:D] = rows.astype(BF)
            out[k - 1][:, D:] = parts


def run_second_sum(where, ra, rb, token):
    return pl.pallas_call(
        second_sum_kernel,
        out_shape=[jax.ShapeDtypeStruct((4, D + 128), F32)]
        + [jax.ShapeDtypeStruct((4, D + 384), BF)] * 3,
        in_specs=[SMEM_SPEC] + vmem_specs(9),
        out_specs=vmem_specs(4),
        scratch_shapes=[pltpu.VMEM((NZ, 4, D), F32)],
        compiler_params=pltpu.CompilerParams(vmem_limit_bytes=8 * MIB),
        name="second_sum",
    )(where, *ra, *rb, token)


def last_sum_kernel(own, *refs):
    out, sums_out = refs[3], refs[4]
    out[...] = total(own[:, 0:D], [r[:, 0:D] for r in refs[0:3]]).astype(BF)
    sums = own[:, D:]
    for r in refs[0:3]:
        sums += join_three(r[:, D:])
    sums_out[0:4, :] = sums
    sums_out[4:8, :] = jnp.zeros((4, 128), F32)


def run_last_sum(pieces):
    return pl.pallas_call(
        last_sum_kernel,
        out_shape=[jax.ShapeDtypeStruct((4, D), BF), jax.ShapeDtypeStruct((8, 128), F32)],
        in_specs=vmem_specs(4),
        out_specs=vmem_specs(2),
        compiler_params=pltpu.CompilerParams(vmem_limit_bytes=4 * MIB),
        name="last_sum",
    )(*pieces)


def router_kernel(where, own, other, slots_ref, out):
    first = jnp.where(where[4] == 0, own[...], other[...])
    second = jnp.where(where[4] == 0, other[...], own[...])
    slots = slots_ref[...].T
    index = lax.broadcasted_iota(jnp.int32, (256, 128), 1)
    spread = jnp.zeros((256, 128), F32)
    for e in range(2):
        picked = jnp.zeros((256, 1), F32)
        for core, values in enumerate((first, second)):
            for h in range(2):
                at = index + h * 128
                token = (at // 64) * 128 + core * 64 + at % 64
                hit = slots[:, e : e + 1] == token
                line = jnp.broadcast_to(values[2 * e + h : 2 * e + h + 1, :], (256, 128))
                picked += jnp.sum(jnp.where(hit, line, 0.0), axis=1, keepdims=True)
        spread = jnp.where(index == e, picked, spread)
    lines = spread.T
    at = lax.broadcasted_iota(jnp.int32, (1, 256), 1)
    for e in range(2):
        out[e : e + 1, :] = jnp.where(at < where[5 + e], lines[e : e + 1, :], 0.0)


def run_router(where, own, other, slots):
    return pl.pallas_call(
        router_kernel,
        out_shape=jax.ShapeDtypeStruct((2, 256), F32),
        in_specs=[SMEM_SPEC] + vmem_specs(3),
        out_specs=vmem_specs(1)[0],
        compiler_params=pltpu.CompilerParams(vmem_limit_bytes=4 * MIB),
        name="router",
    )(where, own, other, slots)


def on_device(
    tokens_in, out_grad, gate_weight, up_weight, down_weight, slot_tokens, slot_counts, slot_gates
):
    x, c, y, z = position()
    where = jnp.stack([x, y, z, c, c, slot_counts[0], slot_counts[1]]).astype(jnp.int32)
    gate_sib, up_sib = swap(gate_weight), swap(up_weight)

    packed = run_pack(tokens_in, out_grad)
    packed = [packed] + [shift(packed, "z", k) for k in (1, 2, 3)]
    t16, g64 = run_first_stage(where, packed, [gate_sib, up_sib])
    down_sib = swap(run_relay(down_weight, [t16]))
    t_low, t_high = shift(t16, "y", 1), shift(t16, "y", -1)
    g_low, g_high = shift(g64, "x", 1), shift(g64, "x", -1)
    a, b, e, f = run_near_halves(t_low, t_high, g_low, g_high)
    t = (t16, t_low, t_high, shift(a, "y", 1), shift(b, "y", -1))
    g = (g64, g_low, g_high, shift(e, "x", 1), shift(f, "x", -1))
    t64, g256 = run_second_stage(where, t, g)
    t_low, t_high = shift(t64, "x", 1), shift(t64, "x", -1)
    g_low, g_high = shift(g256, "y", 1), shift(g256, "y", -1)
    a, b, e, f = run_halves(t_low, t_high, g_low, g_high)
    t = (t64, t_low, t_high, shift(a, "x", 1), shift(b, "x", -1))
    g = (g256, g_low, g_high, shift(e, "y", 1), shift(f, "y", -1))
    weights = (gate_weight, up_weight, down_weight, gate_sib, up_sib, down_sib)
    early = run_early(where, t[0:3], g[0:3], weights)
    outs = run_main(where, t, g, weights, slot_tokens, slot_gates, early)
    a_own, a_down, a_up, a_low, a_high = outs[0:5]
    b_own, b_up, b_down, b_low, b_high = outs[5:10]
    dl_own, rows, grads = outs[10:]

    halves = [shift(a_low, "x", -1), shift(a_high, "x", 1)]
    halves += [shift(b_low, "y", 1), shift(b_high, "y", -1)]
    rows_sib = swap(rows)
    grads_sib = swap(run_relay(grads, halves))
    a_down, a_up, b_up, b_down = run_middle_sum((a_down, a_up, b_up, b_down), halves)
    gate_grad, up_grad, token = run_up(rows, rows_sib, dl_own, [a_down])
    ra = [a_own, shift(a_down, "x", -1), shift(a_up, "x", 1)]
    rb = [b_own, shift(b_up, "y", 1), shift(b_down, "y", -1)]
    q = run_first_sum(where, ra, rb, token)
    qa, qb = q[0:4], q[4:8]
    ra = [qa[0]] + [shift(qa[k], "y", k) for k in (1, 2, 3)]
    rb = [qb[0]] + [shift(qb[k], "x", -k) for k in (1, 2, 3)]
    down_grad, token = run_down(grads, grads_sib, dl_own, rows_sib)
    q = run_second_sum(where, ra, rb, token)
    input_grad, sums = run_last_sum([q[0]] + [shift(q[k], "z", k) for k in (1, 2, 3)])
    router_grad = run_router(where, sums, swap(sums), slot_tokens)
    return (input_grad, gate_grad, up_grad, down_grad, router_grad)


def solution(mesh):
    return jax.shard_map(
        on_device,
        mesh=mesh,
        in_specs=(
            P(("section", "et"), None),
            P("section", "et"),
            P(None, None, ("section", "et")),
            P(None, None, ("section", "et")),
            P(None, ("section", "et"), None),
            P(),
            P(),
            P(),
        ),
        out_specs=(
            P(("section", "et"), None),
            P(None, None, ("section", "et")),
            P(None, None, ("section", "et")),
            P(None, ("section", "et"), None),
            P(),
        ),
        check_vma=False,
    )
```

```python
import jax
import jax.numpy as jnp
from jax import lax
from jax.experimental import pallas as pl
from jax.experimental.pallas import tpu as pltpu
from jax.sharding import PartitionSpec as P

AXES = ("section", "et")
BF = jnp.bfloat16
F32 = jnp.float32
D = 6144
NX, NC, NY, NZ = 4, 2, 4, 4
H = 128
SHORT = 64
HALF = 256


def linear(x, c, y, z):
    return ((x * NC + c) * NY + y) * NZ + z


def shift_pairs(axis, step):
    pairs = []
    for x in range(NX):
        for c in range(NC):
            for y in range(NY):
                for z in range(NZ):
                    to = {
                        "x": ((x + step) % NX, c, y, z),
                        "y": (x, c, (y + step) % NY, z),
                        "z": (x, c, y, (z + step) % NZ),
                    }[axis]
                    pairs.append((linear(x, c, y, z), linear(*to)))
    return pairs


def shift(value, axis, step):
    return lax.ppermute(value, AXES, shift_pairs(axis, step))


def swap(value):
    pairs = [
        (linear(x, c, y, z), linear(x, 1 - c, y, z))
        for x in range(NX)
        for c in range(NC)
        for y in range(NY)
        for z in range(NZ)
    ]
    return lax.ppermute(value, AXES, pairs)


def position():
    section = lax.axis_index("section")
    et = lax.axis_index("et")
    return section // NC, section % NC, et // NZ, et % NZ


def nt(left, right):
    return lax.dot_general(left, right, (((1,), (1,)), ((), ())), preferred_element_type=F32)


def tn(left, right):
    return lax.dot_general(left, right, (((0,), (0,)), ((), ())), preferred_element_type=F32)


def total(first, rest):
    out = first.astype(F32)
    for r in rest:
        out = out + r.astype(F32)
    return out


KT = 1024
FT = 512
MIB = 2**20
WIDE = D // 2 + 384


def vmem_specs(n):
    return [pl.BlockSpec(memory_space=pltpu.VMEM)] * n


SMEM_SPEC = pl.BlockSpec(memory_space=pltpu.SMEM)


def pack_kernel(tokens, grads, out):
    out[0:64, :] = grads[...]
    rows = tokens[...].astype(F32)
    for b in range(0, 16, 4):
        four = [rows[:, (b + i) * 384 : (b + i + 1) * 384] for i in range(4)]
        out[64 + 4 * b : 80 + 4 * b, :] = jnp.concatenate(four, axis=0).astype(BF)


def run_pack(tokens, grads):
    return pl.pallas_call(
        pack_kernel,
        out_shape=jax.ShapeDtypeStruct((128, 384), BF),
        in_specs=vmem_specs(2),
        out_specs=vmem_specs(1)[0],
        compiler_params=pltpu.CompilerParams(vmem_limit_bytes=4 * MIB),
        name="pack",
    )(tokens, grads)


def first_stage_kernel(where, *refs):
    packed, t_out, g_out, buf = refs[0:4], refs[-3], refs[-2], refs[-1]
    for k in range(NZ):
        at = (where[2] - k) % NZ
        rows = packed[k][64:128, :].astype(F32)
        for b in range(16):
            buf[at, :, 384 * b : 384 * (b + 1)] = rows[4 * b : 4 * b + 4]
        start = pl.multiple_of(384 * at, 128)
        g_out[:, pl.ds(start, 384)] = packed[k][0:64, :]
    t_out[...] = jnp.concatenate([buf[k] for k in range(NZ)], axis=0).astype(BF)


def run_first_stage(where, packed, before):
    return pl.pallas_call(
        first_stage_kernel,
        out_shape=[jax.ShapeDtypeStruct((16, D), BF), jax.ShapeDtypeStruct((64, 1536), BF)],
        in_specs=[SMEM_SPEC] + vmem_specs(4) + [pl.BlockSpec(memory_space=pl.ANY)] * len(before),
        out_specs=vmem_specs(2),
        scratch_shapes=[pltpu.VMEM((NZ, 4, D), F32)],
        compiler_params=pltpu.CompilerParams(vmem_limit_bytes=4 * MIB),
        name="first_stage",
    )(where, *packed, *before)


def near_halves_kernel(t_low, t_high, g_low, g_high, a, b, c, d):
    a[...] = t_low[:, 0 : D // 2]
    b[...] = t_high[:, D // 2 : D]
    c[...] = g_low[0:32, :]
    d[...] = g_high[32:64, :]


def run_near_halves(t_low, t_high, g_low, g_high):
    return pl.pallas_call(
        near_halves_kernel,
        out_shape=[jax.ShapeDtypeStruct((16, D // 2), BF)] * 2
        + [jax.ShapeDtypeStruct((32, 1536), BF)] * 2,
        in_specs=vmem_specs(4),
        out_specs=vmem_specs(4),
        compiler_params=pltpu.CompilerParams(vmem_limit_bytes=4 * MIB),
        name="near_halves",
    )(t_low, t_high, g_low, g_high)


def second_stage_kernel(where, *refs):
    t, g, t_out, g_out = refs[0:5], refs[5:10], refs[10], refs[11]
    y = where[1]
    for piece, step in zip(t[0:3], (0, -1, 1)):
        start = pl.multiple_of(16 * ((y + step + NY) % NY), 16)
        t_out[pl.ds(start, 16), :] = piece[...]
    start = pl.multiple_of(16 * ((y + 2) % NY), 16)
    t_out[pl.ds(start, 16), 0 : D // 2] = t[3][...]
    t_out[pl.ds(start, 16), D // 2 : D] = t[4][...]
    for piece, at in zip(g, (0, 64, 192, 128, 160)):
        g_out[at : at + piece.shape[0], :] = piece[...]


def run_second_stage(where, t, g):
    return pl.pallas_call(
        second_stage_kernel,
        out_shape=[jax.ShapeDtypeStruct((64, D), BF), jax.ShapeDtypeStruct((HALF, 1536), BF)],
        in_specs=[SMEM_SPEC] + vmem_specs(10),
        out_specs=vmem_specs(2),
        compiler_params=pltpu.CompilerParams(vmem_limit_bytes=4 * MIB),
        name="second_stage",
    )(where, *t, *g)


def halves_kernel(t_low, t_high, g_low, g_high, a, b, c, d):
    a[...] = t_low[0:32, :]
    b[...] = t_high[32:64, :]
    c[...] = g_low[0:128, :]
    d[...] = g_high[128:256, :]


def run_halves(t_low, t_high, g_low, g_high):
    return pl.pallas_call(
        halves_kernel,
        out_shape=[jax.ShapeDtypeStruct((32, D), BF)] * 2
        + [jax.ShapeDtypeStruct((128, 1536), BF)] * 2,
        in_specs=vmem_specs(4),
        out_specs=vmem_specs(4),
        compiler_params=pltpu.CompilerParams(vmem_limit_bytes=4 * MIB),
        name="halves",
    )(t_low, t_high, g_low, g_high)


def relay_kernel(*refs):
    value, (out, sem) = refs[0], refs[-2:]
    copy = pltpu.make_async_copy(value, out, sem)
    copy.start()
    copy.wait()


def run_relay(value, before):
    hbm = [pl.BlockSpec(memory_space=pltpu.HBM)]
    return pl.pallas_call(
        relay_kernel,
        out_shape=jax.ShapeDtypeStruct(value.shape, value.dtype),
        in_specs=hbm * (1 + len(before)),
        out_specs=hbm[0],
        scratch_shapes=[pltpu.SemaphoreType.DMA],
        compiler_params=pltpu.CompilerParams(vmem_limit_bytes=1 * MIB),
        cost_estimate=pl.CostEstimate(flops=0, bytes_accessed=6_000_000, transcendentals=0),
        name="relay",
    )(value, *before)


def row_copies(pieces, rows, sem):
    places = (0, 64, 192, 128, 160)
    return [
        pltpu.make_async_copy(
            piece, rows.at[pl.ds(at, piece.shape[0]), pl.ds(0, D)], sem.at[r]
        )
        for r, (piece, at) in enumerate(zip(pieces, places))
    ]


def grad_copies(pieces, grads, sem, y):
    places = ((0, 0), (-1, 0), (1, 0), (2, 0), (2, 128))
    copies = []
    for j, (piece, (step, at)) in enumerate(zip(pieces, places)):
        start = pl.multiple_of(((y + step + NY) % NY) * 1536, 128)
        copies.append(
            pltpu.make_async_copy(
                piece, grads.at[pl.ds(at, piece.shape[0]), pl.ds(start, 1536)], sem.at[j]
            )
        )
    return copies


def split_three(value):
    high = value.astype(BF)
    rest = value - high.astype(F32)
    middle = rest.astype(BF)
    low = (rest - middle.astype(F32)).astype(BF)
    return jnp.concatenate([high, middle, low], axis=1)


def join_three(parts):
    out = parts.astype(F32)
    return out[:, 0:128] + out[:, 128:256] + out[:, 256:384]


def early_kernel(where, *refs):
    t, g, weights = refs[0:3], refs[3:6], (refs[6:9], refs[9:12])
    acc_g, acc_b, wv, dv, sem_w, sem_d = refs[12:18]
    y = where[1]
    tiles = D // KT

    def wide_copies(i):
        k = pl.ds(pl.multiple_of(i * KT, KT), KT)
        return [
            pltpu.make_async_copy(
                weights[s][n].at[:, k, :], wv.at[s, n, :, k, :], sem_w.at[i, s * 2 + n]
            )
            for s in range(2)
            for n in range(2)
        ]

    tall_copies = []
    for j, step in enumerate((0, -1, 1)):
        block = pl.ds(pl.multiple_of(((y + step + NY) % NY) * 1536, 128), 1536)
        tall_copies.append(
            [
                pltpu.make_async_copy(weights[s][2].at[:, :, block], dv.at[j, s], sem_d.at[j, s])
                for s in range(2)
            ]
        )
    for i in range(tiles):
        for copy in wide_copies(i):
            copy.start()
    for group in tall_copies:
        for copy in group:
            copy.start()
    acc_g[...] = jnp.zeros(acc_g.shape, F32)
    acc_b[...] = jnp.zeros(acc_b.shape, F32)

    @pl.loop(0, tiles)
    def _(i):
        for copy in wide_copies(i):
            copy.wait()
        k = pl.ds(pl.multiple_of(i * KT, KT), KT)
        wide = jnp.concatenate(
            [wv[s, n, e, k, :] for s in range(2) for e in range(2) for n in range(2)], axis=1
        )
        rows = jnp.concatenate([piece[:, k] for piece in t], axis=0)
        acc_g[...] += jnp.dot(rows, wide, preferred_element_type=F32)

    for j, group in enumerate(tall_copies):
        for copy in group:
            copy.wait()
        tall = jnp.concatenate([dv[j, s, e] for s in range(2) for e in range(2)], axis=0)
        acc_b[...] += nt(g[j][...], tall)


def run_early(where, t, g, weights):
    hbm = [pl.BlockSpec(memory_space=pltpu.HBM)]
    return pl.pallas_call(
        early_kernel,
        out_shape=[
            jax.ShapeDtypeStruct((192, 1024), F32),
            jax.ShapeDtypeStruct((HALF, 512), F32),
        ],
        in_specs=[SMEM_SPEC] + vmem_specs(6) + hbm * 6,
        out_specs=vmem_specs(2),
        scratch_shapes=[
            pltpu.VMEM((2, 2, 2, D, H), BF),
            pltpu.VMEM((3, 2, 2, H, 1536), BF),
            pltpu.SemaphoreType.DMA((D // KT, 4)),
            pltpu.SemaphoreType.DMA((3, 2)),
        ],
        compiler_params=pltpu.CompilerParams(vmem_limit_bytes=22 * MIB),
        cost_estimate=pl.CostEstimate(
            flops=3_600_000_000, bytes_accessed=20_000_000, transcendentals=0
        ),
        name="early",
    )(where, *t, *g, *weights)


def main_kernel(where, *refs):
    t_in, g_in = refs[0:5], refs[5:10]
    weights = (refs[10:13], refs[13:16])
    slots_ref, gates_ref, early_g, early_b = refs[16:20]
    pa_out, pb_out = refs[20:25], refs[25:30]
    own_out, rows_out, grads_out = refs[30:33]
    wv, dv, acc_g, acc_b, deltas, tile, rbuf = refs[33:40]
    sem_t, sem_g, sem_w, sem_d = refs[40:44]
    x, y, core = where[0], where[1], where[4]
    copies_t = row_copies(t_in, rows_out, sem_t)
    copies_g = grad_copies(g_in, grads_out, sem_g, y)
    tiles = D // KT

    def wide_copies(i):
        k = pl.ds(pl.multiple_of(i * KT, KT), KT)
        return [
            pltpu.make_async_copy(
                weights[s][n].at[:, k, :], wv.at[s, n, :, k, :], sem_w.at[i, s * 2 + n]
            )
            for s in range(2)
            for n in range(2)
        ]

    far = pl.ds(pl.multiple_of(((y + 2) % NY) * 1536, 128), 1536)
    tall_copies = [
        pltpu.make_async_copy(weights[s][2].at[:, :, far], dv.at[s], sem_d.at[s]) for s in range(2)
    ]
    for copy in copies_t:
        copy.start()
    for i in range(tiles):
        for copy in wide_copies(i):
            copy.start()
    for copy in copies_g + tall_copies:
        copy.start()
    acc_g[0:128, :] = early_g[0:128, :]
    acc_g[128:192, :] = jnp.zeros((64, 1024), F32)
    acc_g[192:256, :] = early_g[128:192, :]
    scales = []
    slot = lax.broadcasted_iota(jnp.int32, (HALF, 256), 1)
    row = lax.broadcasted_iota(jnp.int32, (HALF, 256), 0)
    block = row // 64
    token = ((x - block + NX) % NX) * 128 + core * 64 + (row - block * 64)
    for e in range(2):
        hit = (token == slots_ref[e : e + 1, :]) & (slot < where[5 + e])
        gate = jnp.broadcast_to(gates_ref[e : e + 1, :], (HALF, 256))
        scales.append(jnp.sum(jnp.where(hit, gate, 0.0), axis=1, keepdims=True))
    for copy in copies_t:
        copy.wait()

    @pl.loop(0, tiles)
    def _(i):
        for copy in wide_copies(i):
            copy.wait()
        k = pl.ds(pl.multiple_of(i * KT, KT), KT)
        wide = jnp.concatenate(
            [wv[s, n, e, k, :] for s in range(2) for e in range(2) for n in range(2)], axis=1
        )
        acc_g[128:192, :] += jnp.dot(rows_out[128:192, k], wide, preferred_element_type=F32)

    for copy in copies_g + tall_copies:
        copy.wait()
    tall = jnp.concatenate([dv[s, e] for s in range(2) for e in range(2)], axis=0)
    acc_b[...] = early_b[...] + nt(grads_out[:, far], tall)
    router = [0.0, 0.0]
    for s in range(2):
        for e in range(2):
            j = s * 2 + e
            pre_gate = acc_g[:, j * 256 : j * 256 + H]
            pre_up = acc_g[:, j * 256 + H : (j + 1) * 256]
            back = acc_b[:, j * H : (j + 1) * H]
            scale = scales[e]
            sigma = jax.nn.sigmoid(pre_gate)
            active = pre_gate * sigma
            hidden = active * pre_up
            router[e] += jnp.sum(hidden.astype(BF).astype(F32) * back, axis=1, keepdims=True)
            hidden_grad = back * scale
            gate_delta = (hidden_grad * pre_up * sigma * (1.0 + pre_gate * (1.0 - sigma))).astype(BF)
            up_delta = (hidden_grad * active).astype(BF)
            deltas[:, j * 256 : j * 256 + H] = gate_delta
            deltas[:, j * 256 + H : (j + 1) * 256] = up_delta
            out, at = (own_out, 0) if s == 0 else (rows_out, D)
            out[:, at + e * 256 : at + e * 256 + H] = gate_delta
            out[:, at + e * 256 + H : at + (e + 1) * 256] = up_delta
            at += 512 + e * H
            out[:, at : at + H] = (hidden * scale).astype(BF)
    lane = lax.broadcasted_iota(jnp.int32, (HALF, 128), 1)
    spread = jnp.where(lane == 0, router[0], jnp.where(lane == 1, router[1], 0.0))
    for k in range(NX):
        to = pl.multiple_of(((x - k) % NX) * 64, 64)
        rbuf[pl.ds(to, 64), :] = spread[k * 64 : (k + 1) * 64]
    line = rbuf[...].T[0:2]
    four = [line[e : e + 1, h * 128 : (h + 1) * 128] for e in range(2) for h in range(2)]
    sums = split_three(jnp.concatenate(four + [jnp.zeros((12, 128), F32)], axis=0))
    for out in pa_out:
        out[:, D // 2 :] = jnp.zeros((out.shape[0], 384), BF)
        out[0:16, D // 2 :] = sums

    def partial(i):
        f = pl.ds(pl.multiple_of(i * FT, FT), FT)
        wide = jnp.concatenate(
            [wv[s, n, e, f, :] for s in range(2) for e in range(2) for n in range(2)], axis=1
        )
        return nt(deltas[...], wide)

    half = D // 2 // FT

    @pl.loop(0, half)
    def _(i):
        f = pl.ds(pl.multiple_of(i * FT, FT), FT)
        part = partial(i).astype(BF)
        for out, at in zip(pa_out, (0, 64, 192, 128, 160)):
            out[:, f] = part[at : at + out.shape[0], :]

    @pl.loop(0, half)
    def _(i):
        f = pl.ds(pl.multiple_of(i * FT, FT), FT)
        tile[...] = partial(i + half).astype(BF)
        for out, k, first in zip(pb_out, (0, 1, 3, 2, 2), (0, 0, 0, 0, 2)):
            for b in range(out.shape[0]):
                src = pl.multiple_of((first + b) * 64 + ((y + k) % NY) * 16, 16)
                out[b, :, f] = tile[pl.ds(src, 16), :]


def run_main(where, t, g, weights, slots, gates, early):
    hbm = [pl.BlockSpec(memory_space=pltpu.HBM)]
    out_shape = (
        [jax.ShapeDtypeStruct((64, WIDE), BF)] * 3
        + [jax.ShapeDtypeStruct((32, WIDE), BF)] * 2
        + [jax.ShapeDtypeStruct((4, 16, D // 2), BF)] * 3
        + [jax.ShapeDtypeStruct((2, 16, D // 2), BF)] * 2
        + [jax.ShapeDtypeStruct((HALF, 768), BF)]
        + [jax.ShapeDtypeStruct((HALF, D + 768), BF)]
        + [jax.ShapeDtypeStruct((HALF, D), BF)]
    )
    return pl.pallas_call(
        main_kernel,
        out_shape=out_shape,
        in_specs=[SMEM_SPEC] + hbm * 16 + vmem_specs(4),
        out_specs=vmem_specs(13),
        scratch_shapes=[
            pltpu.VMEM((2, 2, 2, D, H), BF),
            pltpu.VMEM((2, 2, H, 1536), BF),
            pltpu.VMEM((HALF, 1024), F32),
            pltpu.VMEM((HALF, 512), F32),
            pltpu.VMEM((HALF, 1024), BF),
            pltpu.VMEM((HALF, FT), BF),
            pltpu.VMEM((HALF, 128), F32),
            pltpu.SemaphoreType.DMA((5,)),
            pltpu.SemaphoreType.DMA((5,)),
            pltpu.SemaphoreType.DMA((D // KT, 4)),
            pltpu.SemaphoreType.DMA((2,)),
        ],
        compiler_params=pltpu.CompilerParams(vmem_limit_bytes=21 * MIB),
        cost_estimate=pl.CostEstimate(
            flops=8_000_000_000, bytes_accessed=30_000_000, transcendentals=262144
        ),
        name="main",
    )(where, *t, *g, *weights, slots, gates, *early)


def up_kernel(*refs):
    rows_own, rows_sib, own, sib = refs[0:4]
    gate_out, up_out, token = refs[-3:]
    token[...] = jnp.zeros(token.shape, F32)
    part = tn(rows_own[...], own[:, 0:512]) + tn(rows_sib[...], sib[:, 0:512])
    for e in range(2):
        gate_out[e] = part[:, e * 256 : e * 256 + H].astype(BF)
        up_out[e] = part[:, e * 256 + H : (e + 1) * 256].astype(BF)


def run_up(rows_own, rows_sib, own, before):
    tile = pl.BlockSpec((HALF, 3 * FT), lambda i: (0, i))
    whole = pl.BlockSpec((HALF, 768), lambda i: (0, 0))
    tail = pl.BlockSpec((HALF, 768), lambda i: (0, D // 768))
    out = pl.BlockSpec((2, 3 * FT, H), lambda i: (0, i, 0))
    return pl.pallas_call(
        up_kernel,
        grid=(D // (3 * FT),),
        out_shape=[
            jax.ShapeDtypeStruct((2, D, H), BF),
            jax.ShapeDtypeStruct((2, D, H), BF),
            jax.ShapeDtypeStruct((8, 128), F32),
        ],
        in_specs=[tile, tile, whole, tail]
        + [pl.BlockSpec(memory_space=pl.ANY)] * len(before),
        out_specs=[out, out, pl.BlockSpec((8, 128), lambda i: (0, 0))],
        compiler_params=pltpu.CompilerParams(
            dimension_semantics=("arbitrary",), vmem_limit_bytes=16 * MIB
        ),
        cost_estimate=pl.CostEstimate(
            flops=3_200_000_000, bytes_accessed=13_000_000, transcendentals=0
        ),
        name="up_grads",
    )(rows_own, rows_sib, own, rows_sib, *before)


def down_kernel(grads_own, grads_sib, own, sib, out, token, hidden):
    token[...] = jnp.zeros(token.shape, F32)

    @pl.when(pl.program_id(0) == 0)
    def _():
        hidden[:, 0:HALF] = own[:, 512:768].T
        hidden[:, HALF:512] = sib[:, 512:768].T

    part = jnp.dot(hidden[:, 0:HALF], grads_own[...], preferred_element_type=F32)
    part += jnp.dot(hidden[:, HALF:512], grads_sib[...], preferred_element_type=F32)
    for e in range(2):
        out[e] = part[e * H : (e + 1) * H].astype(BF)


def run_down(grads_own, grads_sib, own, rows_sib):
    tile = pl.BlockSpec((HALF, 4 * FT), lambda i: (0, i))
    whole = pl.BlockSpec((HALF, 768), lambda i: (0, 0))
    tail = pl.BlockSpec((HALF, 768), lambda i: (0, D // 768))
    return pl.pallas_call(
        down_kernel,
        grid=(D // (4 * FT),),
        out_shape=[
            jax.ShapeDtypeStruct((2, H, D), BF),
            jax.ShapeDtypeStruct((8, 128), F32),
        ],
        in_specs=[tile, tile, whole, tail],
        out_specs=[
            pl.BlockSpec((2, H, 4 * FT), lambda i: (0, 0, i)),
            pl.BlockSpec((8, 128), lambda i: (0, 0)),
        ],
        scratch_shapes=[pltpu.VMEM((256, 512), BF)],
        compiler_params=pltpu.CompilerParams(
            dimension_semantics=("arbitrary",), vmem_limit_bytes=16 * MIB
        ),
        cost_estimate=pl.CostEstimate(
            flops=1_600_000_000, bytes_accessed=10_000_000, transcendentals=0
        ),
        name="down_grads",
    )(grads_own, grads_sib, own, rows_sib)


def middle_sum_kernel(*refs):
    a_down, a_up, b_up, b_down = refs[0:4]
    low_a, high_a, low_b, high_b = refs[4:8]
    out_a_down, out_a_up, out_b_up, out_b_down = refs[8:12]
    half = D // 2
    out_a_down[0:32, 0:half] = total(a_down[0:32, 0:half], [low_a[:, 0:half]]).astype(BF)
    out_a_down[32:64, :] = a_down[32:64, :]
    sums = join_three(a_down[0:16, half:]) + join_three(low_a[0:16, half:])
    out_a_down[0:16, half:] = split_three(sums)
    out_a_down[16:32, half:] = a_down[16:32, half:]
    out_a_up[0:32, :] = a_up[0:32, :]
    out_a_up[32:64, :] = total(a_up[32:64, :], [high_a[...]]).astype(BF)
    for k in range(2):
        out_b_up[k] = total(b_up[k], [low_b[k]]).astype(BF)
        out_b_up[2 + k] = b_up[2 + k]
        out_b_down[k] = b_down[k]
        out_b_down[2 + k] = total(b_down[2 + k], [high_b[k]]).astype(BF)


def run_middle_sum(blocks, halves):
    return pl.pallas_call(
        middle_sum_kernel,
        out_shape=[jax.ShapeDtypeStruct((64, WIDE), BF)] * 2
        + [jax.ShapeDtypeStruct((4, 16, D // 2), BF)] * 2,
        in_specs=vmem_specs(8),
        out_specs=vmem_specs(4),
        compiler_params=pltpu.CompilerParams(vmem_limit_bytes=8 * MIB),
        name="middle_sum",
    )(*blocks, *halves)


def first_sum_kernel(where, *refs):
    ra, rb, qa, qb, buf = refs[0:3], refs[3:6], refs[7:11], refs[11:15], refs[15]
    half = D // 2
    buf[...] = total(ra[0][:, 0:half], [r[:, 0:half] for r in ra[1:]]).astype(BF)
    sums = join_three(ra[0][0:16, half:])
    for r in ra[1:]:
        sums += join_three(r[0:16, half:])
    sums = split_three(sums)
    for k in range(NY):
        start = pl.multiple_of(((where[1] + k) % NY) * 16, 16)
        qa[k][:, 0:half] = buf[pl.ds(start, 16), :]
        qa[k][:, half:] = sums
    for k in range(NX):
        qb[k][...] = total(rb[0][k], [r[k] for r in rb[1:]]).astype(BF)


def run_first_sum(where, ra, rb, token):
    return pl.pallas_call(
        first_sum_kernel,
        out_shape=[jax.ShapeDtypeStruct((16, WIDE), BF)] * 4
        + [jax.ShapeDtypeStruct((16, D // 2), BF)] * 4,
        in_specs=[SMEM_SPEC] + vmem_specs(7),
        out_specs=vmem_specs(8),
        scratch_shapes=[pltpu.VMEM((64, D // 2), BF)],
        compiler_params=pltpu.CompilerParams(vmem_limit_bytes=8 * MIB),
        name="first_sum",
    )(where, *ra, *rb, token)


def second_sum_kernel(where, *refs):
    ra, rb, own, out, buf = refs[0:4], refs[4:8], refs[9], refs[10:13], refs[13]
    half = D // 2
    for n, r in enumerate((ra, rb)):
        part = total(r[0][:, 0:half], [p[:, 0:half] for p in r[1:]])
        for k in range(NZ):
            buf[k, :, n * half : (n + 1) * half] = part[4 * k : 4 * k + 4]
    sums = join_three(ra[0][:, half:])
    for r in ra[1:]:
        sums += join_three(r[:, half:])
    parts = split_three(sums)[0:4]
    for k in range(NZ):
        rows = buf[(where[2] + k) % NZ]
        if k == 0:
            own[:, 0:D] = rows
            own[:, D:] = sums[0:4]
        else:
            out[k - 1][:, 0:D] = rows.astype(BF)
            out[k - 1][:, D:] = parts


def run_second_sum(where, ra, rb, token):
    return pl.pallas_call(
        second_sum_kernel,
        out_shape=[jax.ShapeDtypeStruct((4, D + 128), F32)]
        + [jax.ShapeDtypeStruct((4, D + 384), BF)] * 3,
        in_specs=[SMEM_SPEC] + vmem_specs(9),
        out_specs=vmem_specs(4),
        scratch_shapes=[pltpu.VMEM((NZ, 4, D), F32)],
        compiler_params=pltpu.CompilerParams(vmem_limit_bytes=8 * MIB),
        name="second_sum",
    )(where, *ra, *rb, token)


def last_sum_kernel(own, *refs):
    out, sums_out = refs[3], refs[4]
    out[...] = total(own[:, 0:D], [r[:, 0:D] for r in refs[0:3]]).astype(BF)
    sums = own[:, D:]
    for r in refs[0:3]:
        sums += join_three(r[:, D:])
    sums_out[0:4, :] = sums
    sums_out[4:8, :] = jnp.zeros((4, 128), F32)


def run_last_sum(pieces):
    return pl.pallas_call(
        last_sum_kernel,
        out_shape=[jax.ShapeDtypeStruct((4, D), BF), jax.ShapeDtypeStruct((8, 128), F32)],
        in_specs=vmem_specs(4),
        out_specs=vmem_specs(2),
        compiler_params=pltpu.CompilerParams(vmem_limit_bytes=4 * MIB),
        name="last_sum",
    )(*pieces)


def router_kernel(where, own, other, slots_ref, out):
    first = jnp.where(where[4] == 0, own[...], other[...])
    second = jnp.where(where[4] == 0, other[...], own[...])
    slots = slots_ref[...].T
    index = lax.broadcasted_iota(jnp.int32, (256, 128), 1)
    spread = jnp.zeros((256, 128), F32)
    for e in range(2):
        picked = jnp.zeros((256, 1), F32)
        for core, values in enumerate((first, second)):
            for h in range(2):
                at = index + h * 128
                token = (at // 64) * 128 + core * 64 + at % 64
                hit = slots[:, e : e + 1] == token
                line = jnp.broadcast_to(values[2 * e + h : 2 * e + h + 1, :], (256, 128))
                picked += jnp.sum(jnp.where(hit, line, 0.0), axis=1, keepdims=True)
        spread = jnp.where(index == e, picked, spread)
    lines = spread.T
    at = lax.broadcasted_iota(jnp.int32, (1, 256), 1)
    for e in range(2):
        out[e : e + 1, :] = jnp.where(at < where[5 + e], lines[e : e + 1, :], 0.0)


def run_router(where, own, other, slots):
    return pl.pallas_call(
        router_kernel,
        out_shape=jax.ShapeDtypeStruct((2, 256), F32),
        in_specs=[SMEM_SPEC] + vmem_specs(3),
        out_specs=vmem_specs(1)[0],
        compiler_params=pltpu.CompilerParams(vmem_limit_bytes=4 * MIB),
        name="router",
    )(where, own, other, slots)


def on_device(
    tokens_in, out_grad, gate_weight, up_weight, down_weight, slot_tokens, slot_counts, slot_gates
):
    x, c, y, z = position()
    where = jnp.stack([x, y, z, c, c, slot_counts[0], slot_counts[1]]).astype(jnp.int32)
    gate_sib, up_sib = swap(gate_weight), swap(up_weight)

    packed = run_pack(tokens_in, out_grad)
    packed = [packed] + [shift(packed, "z", k) for k in (1, 2, 3)]
    t16, g64 = run_first_stage(where, packed, [gate_sib, up_sib])
    down_sib = swap(run_relay(down_weight, [t16]))
    t_low, t_high = shift(t16, "y", 1), shift(t16, "y", -1)
    g_low, g_high = shift(g64, "x", 1), shift(g64, "x", -1)
    a, b, e, f = run_near_halves(t_low, t_high, g_low, g_high)
    t = (t16, t_low, t_high, shift(a, "y", 1), shift(b, "y", -1))
    g = (g64, g_low, g_high, shift(e, "x", 1), shift(f, "x", -1))
    t64, g256 = run_second_stage(where, t, g)
    t_low, t_high = shift(t64, "x", 1), shift(t64, "x", -1)
    g_low, g_high = shift(g256, "y", 1), shift(g256, "y", -1)
    a, b, e, f = run_halves(t_low, t_high, g_low, g_high)
    t = (t64, t_low, t_high, shift(a, "x", 1), shift(b, "x", -1))
    g = (g256, g_low, g_high, shift(e, "y", 1), shift(f, "y", -1))
    weights = (gate_weight, up_weight, down_weight, gate_sib, up_sib, down_sib)
    early = run_early(where, t[0:3], g[0:3], weights)
    outs = run_main(where, t, g, weights, slot_tokens, slot_gates, early)
    a_own, a_down, a_up, a_low, a_high = outs[0:5]
    b_own, b_up, b_down, b_low, b_high = outs[5:10]
    dl_own, rows, grads = outs[10:]

    halves = [shift(a_low, "x", -1), shift(a_high, "x", 1)]
    halves += [shift(b_low, "y", 1), shift(b_high, "y", -1)]
    rows_sib = swap(rows)
    grads_sib = swap(run_relay(grads, halves))
    a_down, a_up, b_up, b_down = run_middle_sum((a_down, a_up, b_up, b_down), halves)
    gate_grad, up_grad, token = run_up(rows, rows_sib, dl_own, [a_down])
    ra = [a_own, shift(a_down, "x", -1), shift(a_up, "x", 1)]
    rb = [b_own, shift(b_up, "y", 1), shift(b_down, "y", -1)]
    q = run_first_sum(where, ra, rb, token)
    qa, qb = q[0:4], q[4:8]
    ra = [qa[0]] + [shift(qa[k], "y", k) for k in (1, 2, 3)]
    rb = [qb[0]] + [shift(qb[k], "x", -k) for k in (1, 2, 3)]
    down_grad, token = run_down(grads, grads_sib, dl_own, rows_sib)
    q = run_second_sum(where, ra, rb, token)
    input_grad, sums = run_last_sum([q[0]] + [shift(q[k], "z", k) for k in (1, 2, 3)])
    router_grad = run_router(where, sums, swap(sums), slot_tokens)
    return (input_grad, gate_grad, up_grad, down_grad, router_grad)


def solution(mesh):
    return jax.shard_map(
        on_device,
        mesh=mesh,
        in_specs=(
            P(("section", "et"), None),
            P("section", "et"),
            P(None, None, ("section", "et")),
            P(None, None, ("section", "et")),
            P(None, ("section", "et"), None),
            P(),
            P(),
            P(),
        ),
        out_specs=(
            P(("section", "et"), None),
            P(None, None, ("section", "et")),
            P(None, None, ("section", "et")),
            P(None, ("section", "et"), None),
            P(),
        ),
        check_vma=False,
    )
```

```python
import jax
import jax.numpy as jnp
from jax import lax
from jax.experimental import pallas as pl
from jax.experimental.pallas import tpu as pltpu
from jax.sharding import PartitionSpec as P

AXES = ("section", "et")
BF = jnp.bfloat16
F32 = jnp.float32
D = 6144
NX, NC, NY, NZ = 4, 2, 4, 4
H = 128
SHORT = 64
HALF = 256


def linear(x, c, y, z):
    return ((x * NC + c) * NY + y) * NZ + z


def shift_pairs(axis, step):
    pairs = []
    for x in range(NX):
        for c in range(NC):
            for y in range(NY):
                for z in range(NZ):
                    to = {
                        "x": ((x + step) % NX, c, y, z),
                        "y": (x, c, (y + step) % NY, z),
                        "z": (x, c, y, (z + step) % NZ),
                    }[axis]
                    pairs.append((linear(x, c, y, z), linear(*to)))
    return pairs


def shift(value, axis, step):
    return lax.ppermute(value, AXES, shift_pairs(axis, step))


def swap(value):
    pairs = [
        (linear(x, c, y, z), linear(x, 1 - c, y, z))
        for x in range(NX)
        for c in range(NC)
        for y in range(NY)
        for z in range(NZ)
    ]
    return lax.ppermute(value, AXES, pairs)


def position():
    section = lax.axis_index("section")
    et = lax.axis_index("et")
    return section // NC, section % NC, et // NZ, et % NZ


def nt(left, right):
    return lax.dot_general(left, right, (((1,), (1,)), ((), ())), preferred_element_type=F32)


def tn(left, right):
    return lax.dot_general(left, right, (((0,), (0,)), ((), ())), preferred_element_type=F32)


def total(first, rest):
    out = first.astype(F32)
    for r in rest:
        out = out + r.astype(F32)
    return out


KT = 1024
FT = 512
MIB = 2**20
WIDE = D // 2 + 384


def vmem_specs(n):
    return [pl.BlockSpec(memory_space=pltpu.VMEM)] * n


SMEM_SPEC = pl.BlockSpec(memory_space=pltpu.SMEM)


def pack_kernel(tokens, grads, out):
    out[0:64, :] = grads[...]
    rows = tokens[...].astype(F32)
    for b in range(0, 16, 4):
        four = [rows[:, (b + i) * 384 : (b + i + 1) * 384] for i in range(4)]
        out[64 + 4 * b : 80 + 4 * b, :] = jnp.concatenate(four, axis=0).astype(BF)


def run_pack(tokens, grads):
    return pl.pallas_call(
        pack_kernel,
        out_shape=jax.ShapeDtypeStruct((128, 384), BF),
        in_specs=vmem_specs(2),
        out_specs=vmem_specs(1)[0],
        compiler_params=pltpu.CompilerParams(vmem_limit_bytes=4 * MIB),
        name="pack",
    )(tokens, grads)


def first_stage_kernel(where, *refs):
    packed, t_out, g_out, buf = refs[0:4], refs[-3], refs[-2], refs[-1]
    for k in range(NZ):
        at = (where[2] - k) % NZ
        rows = packed[k][64:128, :].astype(F32)
        for b in range(16):
            buf[at, :, 384 * b : 384 * (b + 1)] = rows[4 * b : 4 * b + 4]
        start = pl.multiple_of(384 * at, 128)
        g_out[:, pl.ds(start, 384)] = packed[k][0:64, :]
    t_out[...] = jnp.concatenate([buf[k] for k in range(NZ)], axis=0).astype(BF)


def run_first_stage(where, packed, before):
    return pl.pallas_call(
        first_stage_kernel,
        out_shape=[jax.ShapeDtypeStruct((16, D), BF), jax.ShapeDtypeStruct((64, 1536), BF)],
        in_specs=[SMEM_SPEC] + vmem_specs(4) + [pl.BlockSpec(memory_space=pl.ANY)] * len(before),
        out_specs=vmem_specs(2),
        scratch_shapes=[pltpu.VMEM((NZ, 4, D), F32)],
        compiler_params=pltpu.CompilerParams(vmem_limit_bytes=4 * MIB),
        name="first_stage",
    )(where, *packed, *before)


def near_halves_kernel(t_low, t_high, g_low, g_high, a, b, c, d):
    a[...] = t_low[:, 0 : D // 2]
    b[...] = t_high[:, D // 2 : D]
    c[...] = g_low[0:32, :]
    d[...] = g_high[32:64, :]


def run_near_halves(t_low, t_high, g_low, g_high):
    return pl.pallas_call(
        near_halves_kernel,
        out_shape=[jax.ShapeDtypeStruct((16, D // 2), BF)] * 2
        + [jax.ShapeDtypeStruct((32, 1536), BF)] * 2,
        in_specs=vmem_specs(4),
        out_specs=vmem_specs(4),
        compiler_params=pltpu.CompilerParams(vmem_limit_bytes=4 * MIB),
        name="near_halves",
    )(t_low, t_high, g_low, g_high)


def second_stage_kernel(where, *refs):
    t, g, t_out, g_out = refs[0:5], refs[5:10], refs[10], refs[11]
    y = where[1]
    for piece, step in zip(t[0:3], (0, -1, 1)):
        start = pl.multiple_of(16 * ((y + step + NY) % NY), 16)
        t_out[pl.ds(start, 16), :] = piece[...]
    start = pl.multiple_of(16 * ((y + 2) % NY), 16)
    t_out[pl.ds(start, 16), 0 : D // 2] = t[3][...]
    t_out[pl.ds(start, 16), D // 2 : D] = t[4][...]
    for piece, at in zip(g, (0, 64, 192, 128, 160)):
        g_out[at : at + piece.shape[0], :] = piece[...]


def run_second_stage(where, t, g):
    return pl.pallas_call(
        second_stage_kernel,
        out_shape=[jax.ShapeDtypeStruct((64, D), BF), jax.ShapeDtypeStruct((HALF, 1536), BF)],
        in_specs=[SMEM_SPEC] + vmem_specs(10),
        out_specs=vmem_specs(2),
        compiler_params=pltpu.CompilerParams(vmem_limit_bytes=4 * MIB),
        name="second_stage",
    )(where, *t, *g)


def halves_kernel(t_low, t_high, g_low, g_high, a, b, c, d):
    a[...] = t_low[0:32, :]
    b[...] = t_high[32:64, :]
    c[...] = g_low[0:128, :]
    d[...] = g_high[128:256, :]


def run_halves(t_low, t_high, g_low, g_high):
    return pl.pallas_call(
        halves_kernel,
        out_shape=[jax.ShapeDtypeStruct((32, D), BF)] * 2
        + [jax.ShapeDtypeStruct((128, 1536), BF)] * 2,
        in_specs=vmem_specs(4),
        out_specs=vmem_specs(4),
        compiler_params=pltpu.CompilerParams(vmem_limit_bytes=4 * MIB),
        name="halves",
    )(t_low, t_high, g_low, g_high)


def relay_kernel(*refs):
    value, (out, sem) = refs[0], refs[-2:]
    copy = pltpu.make_async_copy(value, out, sem)
    copy.start()
    copy.wait()


def run_relay(value, before):
    hbm = [pl.BlockSpec(memory_space=pltpu.HBM)]
    return pl.pallas_call(
        relay_kernel,
        out_shape=jax.ShapeDtypeStruct(value.shape, value.dtype),
        in_specs=hbm * (1 + len(before)),
        out_specs=hbm[0],
        scratch_shapes=[pltpu.SemaphoreType.DMA],
        compiler_params=pltpu.CompilerParams(vmem_limit_bytes=1 * MIB),
        cost_estimate=pl.CostEstimate(flops=0, bytes_accessed=6_000_000, transcendentals=0),
        name="relay",
    )(value, *before)


def row_copies(pieces, rows, sem):
    places = (0, 64, 192, 128, 160)
    return [
        pltpu.make_async_copy(
            piece, rows.at[pl.ds(at, piece.shape[0]), pl.ds(0, D)], sem.at[r]
        )
        for r, (piece, at) in enumerate(zip(pieces, places))
    ]


def grad_copies(pieces, grads, sem, y):
    places = ((0, 0), (-1, 0), (1, 0), (2, 0), (2, 128))
    copies = []
    for j, (piece, (step, at)) in enumerate(zip(pieces, places)):
        start = pl.multiple_of(((y + step + NY) % NY) * 1536, 128)
        copies.append(
            pltpu.make_async_copy(
                piece, grads.at[pl.ds(at, piece.shape[0]), pl.ds(start, 1536)], sem.at[j]
            )
        )
    return copies


def split_three(value):
    high = value.astype(BF)
    rest = value - high.astype(F32)
    middle = rest.astype(BF)
    low = (rest - middle.astype(F32)).astype(BF)
    return jnp.concatenate([high, middle, low], axis=1)


def join_three(parts):
    out = parts.astype(F32)
    return out[:, 0:128] + out[:, 128:256] + out[:, 256:384]


def early_kernel(where, *refs):
    t, g, weights = refs[0:3], refs[3:6], (refs[6:9], refs[9:12])
    acc_g, acc_b, wv, dv, sem_w, sem_d = refs[12:18]
    y = where[1]
    tiles = D // KT

    def wide_copies(i):
        k = pl.ds(pl.multiple_of(i * KT, KT), KT)
        return [
            pltpu.make_async_copy(
                weights[s][n].at[:, k, :], wv.at[s, n, :, k, :], sem_w.at[i, s * 2 + n]
            )
            for s in range(2)
            for n in range(2)
        ]

    tall_copies = []
    for j, step in enumerate((0, -1, 1)):
        block = pl.ds(pl.multiple_of(((y + step + NY) % NY) * 1536, 128), 1536)
        tall_copies.append(
            [
                pltpu.make_async_copy(weights[s][2].at[:, :, block], dv.at[j, s], sem_d.at[j, s])
                for s in range(2)
            ]
        )
    for i in range(tiles):
        for copy in wide_copies(i):
            copy.start()
    for group in tall_copies:
        for copy in group:
            copy.start()
    acc_g[...] = jnp.zeros(acc_g.shape, F32)
    acc_b[...] = jnp.zeros(acc_b.shape, F32)

    @pl.loop(0, tiles)
    def _(i):
        for copy in wide_copies(i):
            copy.wait()
        k = pl.ds(pl.multiple_of(i * KT, KT), KT)
        wide = jnp.concatenate(
            [wv[s, n, e, k, :] for s in range(2) for e in range(2) for n in range(2)], axis=1
        )
        rows = jnp.concatenate([piece[:, k] for piece in t], axis=0)
        acc_g[...] += jnp.dot(rows, wide, preferred_element_type=F32)

    for j, group in enumerate(tall_copies):
        for copy in group:
            copy.wait()
        tall = jnp.concatenate([dv[j, s, e] for s in range(2) for e in range(2)], axis=0)
        acc_b[...] += nt(g[j][...], tall)


def run_early(where, t, g, weights):
    hbm = [pl.BlockSpec(memory_space=pltpu.HBM)]
    return pl.pallas_call(
        early_kernel,
        out_shape=[
            jax.ShapeDtypeStruct((192, 1024), F32),
            jax.ShapeDtypeStruct((HALF, 512), F32),
        ],
        in_specs=[SMEM_SPEC] + vmem_specs(6) + hbm * 6,
        out_specs=vmem_specs(2),
        scratch_shapes=[
            pltpu.VMEM((2, 2, 2, D, H), BF),
            pltpu.VMEM((3, 2, 2, H, 1536), BF),
            pltpu.SemaphoreType.DMA((D // KT, 4)),
            pltpu.SemaphoreType.DMA((3, 2)),
        ],
        compiler_params=pltpu.CompilerParams(vmem_limit_bytes=22 * MIB),
        cost_estimate=pl.CostEstimate(
            flops=3_600_000_000, bytes_accessed=20_000_000, transcendentals=0
        ),
        name="early",
    )(where, *t, *g, *weights)


def main_kernel(where, *refs):
    t_in, g_in = refs[0:5], refs[5:10]
    weights = (refs[10:13], refs[13:16])
    slots_ref, gates_ref, early_g, early_b = refs[16:20]
    pa_out, pb_out = refs[20:25], refs[25:30]
    own_out, rows_out, grads_out = refs[30:33]
    wv, dv, acc_g, acc_b, deltas, tile, rbuf = refs[33:40]
    sem_t, sem_g, sem_w, sem_d = refs[40:44]
    x, y, core = where[0], where[1], where[4]
    copies_t = row_copies(t_in, rows_out, sem_t)
    copies_g = grad_copies(g_in, grads_out, sem_g, y)
    tiles = D // KT

    def wide_copies(i):
        k = pl.ds(pl.multiple_of(i * KT, KT), KT)
        return [
            pltpu.make_async_copy(
                weights[s][n].at[:, k, :], wv.at[s, n, :, k, :], sem_w.at[i, s * 2 + n]
            )
            for s in range(2)
            for n in range(2)
        ]

    far = pl.ds(pl.multiple_of(((y + 2) % NY) * 1536, 128), 1536)
    tall_copies = [
        pltpu.make_async_copy(weights[s][2].at[:, :, far], dv.at[s], sem_d.at[s]) for s in range(2)
    ]
    for copy in copies_t:
        copy.start()
    for i in range(tiles):
        for copy in wide_copies(i):
            copy.start()
    for copy in copies_g + tall_copies:
        copy.start()
    acc_g[0:128, :] = early_g[0:128, :]
    acc_g[128:192, :] = jnp.zeros((64, 1024), F32)
    acc_g[192:256, :] = early_g[128:192, :]
    scales = []
    slot = lax.broadcasted_iota(jnp.int32, (HALF, 256), 1)
    row = lax.broadcasted_iota(jnp.int32, (HALF, 256), 0)
    block = row // 64
    token = ((x - block + NX) % NX) * 128 + core * 64 + (row - block * 64)
    for e in range(2):
        hit = (token == slots_ref[e : e + 1, :]) & (slot < where[5 + e])
        gate = jnp.broadcast_to(gates_ref[e : e + 1, :], (HALF, 256))
        scales.append(jnp.sum(jnp.where(hit, gate, 0.0), axis=1, keepdims=True))
    for copy in copies_t:
        copy.wait()

    @pl.loop(0, tiles)
    def _(i):
        for copy in wide_copies(i):
            copy.wait()
        k = pl.ds(pl.multiple_of(i * KT, KT), KT)
        wide = jnp.concatenate(
            [wv[s, n, e, k, :] for s in range(2) for e in range(2) for n in range(2)], axis=1
        )
        acc_g[128:192, :] += jnp.dot(rows_out[128:192, k], wide, preferred_element_type=F32)

    for copy in copies_g + tall_copies:
        copy.wait()
    tall = jnp.concatenate([dv[s, e] for s in range(2) for e in range(2)], axis=0)
    acc_b[...] = early_b[...] + nt(grads_out[:, far], tall)
    router = [0.0, 0.0]
    for s in range(2):
        for e in range(2):
            j = s * 2 + e
            pre_gate = acc_g[:, j * 256 : j * 256 + H]
            pre_up = acc_g[:, j * 256 + H : (j + 1) * 256]
            back = acc_b[:, j * H : (j + 1) * H]
            scale = scales[e]
            sigma = jax.nn.sigmoid(pre_gate)
            active = pre_gate * sigma
            hidden = active * pre_up
            router[e] += jnp.sum(hidden.astype(BF).astype(F32) * back, axis=1, keepdims=True)
            hidden_grad = back * scale
            gate_delta = (hidden_grad * pre_up * sigma * (1.0 + pre_gate * (1.0 - sigma))).astype(BF)
            up_delta = (hidden_grad * active).astype(BF)
            deltas[:, j * 256 : j * 256 + H] = gate_delta
            deltas[:, j * 256 + H : (j + 1) * 256] = up_delta
            out, at = (own_out, 0) if s == 0 else (rows_out, D)
            out[:, at + e * 256 : at + e * 256 + H] = gate_delta
            out[:, at + e * 256 + H : at + (e + 1) * 256] = up_delta
            at += 512 + e * H
            out[:, at : at + H] = (hidden * scale).astype(BF)
    lane = lax.broadcasted_iota(jnp.int32, (HALF, 128), 1)
    spread = jnp.where(lane == 0, router[0], jnp.where(lane == 1, router[1], 0.0))
    for k in range(NX):
        to = pl.multiple_of(((x - k) % NX) * 64, 64)
        rbuf[pl.ds(to, 64), :] = spread[k * 64 : (k + 1) * 64]
    line = rbuf[...].T[0:2]
    four = [line[e : e + 1, h * 128 : (h + 1) * 128] for e in range(2) for h in range(2)]
    sums = split_three(jnp.concatenate(four + [jnp.zeros((12, 128), F32)], axis=0))
    for out in pa_out:
        out[:, D // 2 :] = jnp.zeros((out.shape[0], 384), BF)
        out[0:16, D // 2 :] = sums

    def partial(i):
        f = pl.ds(pl.multiple_of(i * FT, FT), FT)
        wide = jnp.concatenate(
            [wv[s, n, e, f, :] for s in range(2) for e in range(2) for n in range(2)], axis=1
        )
        return nt(deltas[...], wide)

    half = D // 2 // FT

    @pl.loop(0, half)
    def _(i):
        f = pl.ds(pl.multiple_of(i * FT, FT), FT)
        part = partial(i).astype(BF)
        for out, at in zip(pa_out, (0, 64, 192, 128, 160)):
            out[:, f] = part[at : at + out.shape[0], :]

    @pl.loop(0, half)
    def _(i):
        f = pl.ds(pl.multiple_of(i * FT, FT), FT)
        tile[...] = partial(i + half).astype(BF)
        for out, k, first in zip(pb_out, (0, 1, 3, 2, 2), (0, 0, 0, 0, 2)):
            for b in range(out.shape[0]):
                src = pl.multiple_of((first + b) * 64 + ((y + k) % NY) * 16, 16)
                out[b, :, f] = tile[pl.ds(src, 16), :]


def run_main(where, t, g, weights, slots, gates, early):
    hbm = [pl.BlockSpec(memory_space=pltpu.HBM)]
    out_shape = (
        [jax.ShapeDtypeStruct((64, WIDE), BF)] * 3
        + [jax.ShapeDtypeStruct((32, WIDE), BF)] * 2
        + [jax.ShapeDtypeStruct((4, 16, D // 2), BF)] * 3
        + [jax.ShapeDtypeStruct((2, 16, D // 2), BF)] * 2
        + [jax.ShapeDtypeStruct((HALF, 768), BF)]
        + [jax.ShapeDtypeStruct((HALF, D + 768), BF)]
        + [jax.ShapeDtypeStruct((HALF, D), BF)]
    )
    return pl.pallas_call(
        main_kernel,
        out_shape=out_shape,
        in_specs=[SMEM_SPEC] + hbm * 16 + vmem_specs(4),
        out_specs=vmem_specs(13),
        scratch_shapes=[
            pltpu.VMEM((2, 2, 2, D, H), BF),
            pltpu.VMEM((2, 2, H, 1536), BF),
            pltpu.VMEM((HALF, 1024), F32),
            pltpu.VMEM((HALF, 512), F32),
            pltpu.VMEM((HALF, 1024), BF),
            pltpu.VMEM((HALF, FT), BF),
            pltpu.VMEM((HALF, 128), F32),
            pltpu.SemaphoreType.DMA((5,)),
            pltpu.SemaphoreType.DMA((5,)),
            pltpu.SemaphoreType.DMA((D // KT, 4)),
            pltpu.SemaphoreType.DMA((2,)),
        ],
        compiler_params=pltpu.CompilerParams(vmem_limit_bytes=21 * MIB),
        cost_estimate=pl.CostEstimate(
            flops=8_000_000_000, bytes_accessed=30_000_000, transcendentals=262144
        ),
        name="main",
    )(where, *t, *g, *weights, slots, gates, *early)


def up_kernel(*refs):
    rows_own, rows_sib, own, sib = refs[0:4]
    gate_out, up_out, token = refs[-3:]
    token[...] = jnp.zeros(token.shape, F32)
    part = tn(rows_own[...], own[:, 0:512]) + tn(rows_sib[...], sib[:, 0:512])
    for e in range(2):
        gate_out[e] = part[:, e * 256 : e * 256 + H].astype(BF)
        up_out[e] = part[:, e * 256 + H : (e + 1) * 256].astype(BF)


def run_up(rows_own, rows_sib, own, before):
    tile = pl.BlockSpec((HALF, 3 * FT), lambda i: (0, i))
    whole = pl.BlockSpec((HALF, 768), lambda i: (0, 0))
    tail = pl.BlockSpec((HALF, 768), lambda i: (0, D // 768))
    out = pl.BlockSpec((2, 3 * FT, H), lambda i: (0, i, 0))
    return pl.pallas_call(
        up_kernel,
        grid=(D // (3 * FT),),
        out_shape=[
            jax.ShapeDtypeStruct((2, D, H), BF),
            jax.ShapeDtypeStruct((2, D, H), BF),
            jax.ShapeDtypeStruct((8, 128), F32),
        ],
        in_specs=[tile, tile, whole, tail]
        + [pl.BlockSpec(memory_space=pl.ANY)] * len(before),
        out_specs=[out, out, pl.BlockSpec((8, 128), lambda i: (0, 0))],
        compiler_params=pltpu.CompilerParams(
            dimension_semantics=("arbitrary",), vmem_limit_bytes=16 * MIB
        ),
        cost_estimate=pl.CostEstimate(
            flops=3_200_000_000, bytes_accessed=13_000_000, transcendentals=0
        ),
        name="up_grads",
    )(rows_own, rows_sib, own, rows_sib, *before)


def down_kernel(grads_own, grads_sib, own, sib, out, token, hidden):
    token[...] = jnp.zeros(token.shape, F32)

    @pl.when(pl.program_id(0) == 0)
    def _():
        hidden[:, 0:HALF] = own[:, 512:768].T
        hidden[:, HALF:512] = sib[:, 512:768].T

    part = jnp.dot(hidden[:, 0:HALF], grads_own[...], preferred_element_type=F32)
    part += jnp.dot(hidden[:, HALF:512], grads_sib[...], preferred_element_type=F32)
    for e in range(2):
        out[e] = part[e * H : (e + 1) * H].astype(BF)


def run_down(grads_own, grads_sib, own, rows_sib):
    tile = pl.BlockSpec((HALF, 4 * FT), lambda i: (0, i))
    whole = pl.BlockSpec((HALF, 768), lambda i: (0, 0))
    tail = pl.BlockSpec((HALF, 768), lambda i: (0, D // 768))
    return pl.pallas_call(
        down_kernel,
        grid=(D // (4 * FT),),
        out_shape=[
            jax.ShapeDtypeStruct((2, H, D), BF),
            jax.ShapeDtypeStruct((8, 128), F32),
        ],
        in_specs=[tile, tile, whole, tail],
        out_specs=[
            pl.BlockSpec((2, H, 4 * FT), lambda i: (0, 0, i)),
            pl.BlockSpec((8, 128), lambda i: (0, 0)),
        ],
        scratch_shapes=[pltpu.VMEM((256, 512), BF)],
        compiler_params=pltpu.CompilerParams(
            dimension_semantics=("arbitrary",), vmem_limit_bytes=16 * MIB
        ),
        cost_estimate=pl.CostEstimate(
            flops=1_600_000_000, bytes_accessed=10_000_000, transcendentals=0
        ),
        name="down_grads",
    )(grads_own, grads_sib, own, rows_sib)


def middle_sum_kernel(*refs):
    a_down, a_up, b_up, b_down = refs[0:4]
    low_a, high_a, low_b, high_b = refs[4:8]
    out_a_down, out_a_up, out_b_up, out_b_down = refs[8:12]
    half = D // 2
    out_a_down[0:32, 0:half] = total(a_down[0:32, 0:half], [low_a[:, 0:half]]).astype(BF)
    out_a_down[32:64, :] = a_down[32:64, :]
    sums = join_three(a_down[0:16, half:]) + join_three(low_a[0:16, half:])
    out_a_down[0:16, half:] = split_three(sums)
    out_a_down[16:32, half:] = a_down[16:32, half:]
    out_a_up[0:32, :] = a_up[0:32, :]
    out_a_up[32:64, :] = total(a_up[32:64, :], [high_a[...]]).astype(BF)
    for k in range(2):
        out_b_up[k] = total(b_up[k], [low_b[k]]).astype(BF)
        out_b_up[2 + k] = b_up[2 + k]
        out_b_down[k] = b_down[k]
        out_b_down[2 + k] = total(b_down[2 + k], [high_b[k]]).astype(BF)


def run_middle_sum(blocks, halves):
    return pl.pallas_call(
        middle_sum_kernel,
        out_shape=[jax.ShapeDtypeStruct((64, WIDE), BF)] * 2
        + [jax.ShapeDtypeStruct((4, 16, D // 2), BF)] * 2,
        in_specs=vmem_specs(8),
        out_specs=vmem_specs(4),
        compiler_params=pltpu.CompilerParams(vmem_limit_bytes=8 * MIB),
        name="middle_sum",
    )(*blocks, *halves)


def first_sum_kernel(where, *refs):
    ra, rb, qa, qb, buf = refs[0:3], refs[3:6], refs[8:12], refs[12:16], refs[16]
    half = D // 2
    buf[...] = total(ra[0][:, 0:half], [r[:, 0:half] for r in ra[1:]]).astype(BF)
    sums = join_three(ra[0][0:16, half:])
    for r in ra[1:]:
        sums += join_three(r[0:16, half:])
    sums = split_three(sums)
    for k in range(NY):
        start = pl.multiple_of(((where[1] + k) % NY) * 16, 16)
        qa[k][:, 0:half] = buf[pl.ds(start, 16), :]
        qa[k][:, half:] = sums
    for k in range(NX):
        qb[k][...] = total(rb[0][k], [r[k] for r in rb[1:]]).astype(BF)


def run_first_sum(where, ra, rb, token, other):
    return pl.pallas_call(
        first_sum_kernel,
        out_shape=[jax.ShapeDtypeStruct((16, WIDE), BF)] * 4
        + [jax.ShapeDtypeStruct((16, D // 2), BF)] * 4,
        in_specs=[SMEM_SPEC] + vmem_specs(8),
        out_specs=vmem_specs(8),
        scratch_shapes=[pltpu.VMEM((64, D // 2), BF)],
        compiler_params=pltpu.CompilerParams(vmem_limit_bytes=8 * MIB),
        name="first_sum",
    )(where, *ra, *rb, token, other)


def second_sum_kernel(where, *refs):
    ra, rb, own, out, buf = refs[0:4], refs[4:8], refs[8], refs[9:12], refs[12]
    half = D // 2
    for n, r in enumerate((ra, rb)):
        part = total(r[0][:, 0:half], [p[:, 0:half] for p in r[1:]])
        for k in range(NZ):
            buf[k, :, n * half : (n + 1) * half] = part[4 * k : 4 * k + 4]
    sums = join_three(ra[0][:, half:])
    for r in ra[1:]:
        sums += join_three(r[:, half:])
    parts = split_three(sums)[0:4]
    for k in range(NZ):
        rows = buf[(where[2] + k) % NZ]
        if k == 0:
            own[:, 0:D] = rows
            own[:, D:] = sums[0:4]
        else:
            out[k - 1][:, 0:D] = rows.astype(BF)
            out[k - 1][:, D:] = parts


def run_second_sum(where, ra, rb):
    return pl.pallas_call(
        second_sum_kernel,
        out_shape=[jax.ShapeDtypeStruct((4, D + 128), F32)]
        + [jax.ShapeDtypeStruct((4, D + 384), BF)] * 3,
        in_specs=[SMEM_SPEC] + vmem_specs(8),
        out_specs=vmem_specs(4),
        scratch_shapes=[pltpu.VMEM((NZ, 4, D), F32)],
        compiler_params=pltpu.CompilerParams(vmem_limit_bytes=8 * MIB),
        name="second_sum",
    )(where, *ra, *rb)


def last_sum_kernel(own, *refs):
    out, sums_out = refs[3], refs[4]
    out[...] = total(own[:, 0:D], [r[:, 0:D] for r in refs[0:3]]).astype(BF)
    sums = own[:, D:]
    for r in refs[0:3]:
        sums += join_three(r[:, D:])
    sums_out[0:4, :] = sums
    sums_out[4:8, :] = jnp.zeros((4, 128), F32)


def run_last_sum(pieces):
    return pl.pallas_call(
        last_sum_kernel,
        out_shape=[jax.ShapeDtypeStruct((4, D), BF), jax.ShapeDtypeStruct((8, 128), F32)],
        in_specs=vmem_specs(4),
        out_specs=vmem_specs(2),
        compiler_params=pltpu.CompilerParams(vmem_limit_bytes=4 * MIB),
        name="last_sum",
    )(*pieces)


def router_kernel(where, own, other, slots_ref, out):
    first = jnp.where(where[4] == 0, own[...], other[...])
    second = jnp.where(where[4] == 0, other[...], own[...])
    slots = slots_ref[...].T
    index = lax.broadcasted_iota(jnp.int32, (256, 128), 1)
    spread = jnp.zeros((256, 128), F32)
    for e in range(2):
        picked = jnp.zeros((256, 1), F32)
        for core, values in enumerate((first, second)):
            for h in range(2):
                at = index + h * 128
                token = (at // 64) * 128 + core * 64 + at % 64
                hit = slots[:, e : e + 1] == token
                line = jnp.broadcast_to(values[2 * e + h : 2 * e + h + 1, :], (256, 128))
                picked += jnp.sum(jnp.where(hit, line, 0.0), axis=1, keepdims=True)
        spread = jnp.where(index == e, picked, spread)
    lines = spread.T
    at = lax.broadcasted_iota(jnp.int32, (1, 256), 1)
    for e in range(2):
        out[e : e + 1, :] = jnp.where(at < where[5 + e], lines[e : e + 1, :], 0.0)


def run_router(where, own, other, slots):
    return pl.pallas_call(
        router_kernel,
        out_shape=jax.ShapeDtypeStruct((2, 256), F32),
        in_specs=[SMEM_SPEC] + vmem_specs(3),
        out_specs=vmem_specs(1)[0],
        compiler_params=pltpu.CompilerParams(vmem_limit_bytes=4 * MIB),
        name="router",
    )(where, own, other, slots)


def on_device(
    tokens_in, out_grad, gate_weight, up_weight, down_weight, slot_tokens, slot_counts, slot_gates
):
    x, c, y, z = position()
    where = jnp.stack([x, y, z, c, c, slot_counts[0], slot_counts[1]]).astype(jnp.int32)
    gate_sib, up_sib = swap(gate_weight), swap(up_weight)

    packed = run_pack(tokens_in, out_grad)
    packed = [packed] + [shift(packed, "z", k) for k in (1, 2, 3)]
    t16, g64 = run_first_stage(where, packed, [gate_sib, up_sib])
    down_sib = swap(run_relay(down_weight, [t16]))
    t_low, t_high = shift(t16, "y", 1), shift(t16, "y", -1)
    g_low, g_high = shift(g64, "x", 1), shift(g64, "x", -1)
    a, b, e, f = run_near_halves(t_low, t_high, g_low, g_high)
    t = (t16, t_low, t_high, shift(a, "y", 1), shift(b, "y", -1))
    g = (g64, g_low, g_high, shift(e, "x", 1), shift(f, "x", -1))
    t64, g256 = run_second_stage(where, t, g)
    t_low, t_high = shift(t64, "x", 1), shift(t64, "x", -1)
    g_low, g_high = shift(g256, "y", 1), shift(g256, "y", -1)
    a, b, e, f = run_halves(t_low, t_high, g_low, g_high)
    t = (t64, t_low, t_high, shift(a, "x", 1), shift(b, "x", -1))
    g = (g256, g_low, g_high, shift(e, "y", 1), shift(f, "y", -1))
    weights = (gate_weight, up_weight, down_weight, gate_sib, up_sib, down_sib)
    early = run_early(where, t[0:3], g[0:3], weights)
    outs = run_main(where, t, g, weights, slot_tokens, slot_gates, early)
    a_own, a_down, a_up, a_low, a_high = outs[0:5]
    b_own, b_up, b_down, b_low, b_high = outs[5:10]
    dl_own, rows, grads = outs[10:]

    halves = [shift(a_low, "x", -1), shift(a_high, "x", 1)]
    halves += [shift(b_low, "y", 1), shift(b_high, "y", -1)]
    rows_sib = swap(rows)
    grads_sib = swap(run_relay(grads, halves))
    a_down, a_up, b_up, b_down = run_middle_sum((a_down, a_up, b_up, b_down), halves)
    gate_grad, up_grad, token = run_up(rows, rows_sib, dl_own, [a_down])
    ra = [a_own, shift(a_down, "x", -1), shift(a_up, "x", 1)]
    rb = [b_own, shift(b_up, "y", 1), shift(b_down, "y", -1)]
    down_grad, other = run_down(grads, grads_sib, dl_own, rows_sib)
    q = run_first_sum(where, ra, rb, token, other)
    qa, qb = q[0:4], q[4:8]
    ra = [qa[0]] + [shift(qa[k], "y", k) for k in (1, 2, 3)]
    rb = [qb[0]] + [shift(qb[k], "x", -k) for k in (1, 2, 3)]
    q = run_second_sum(where, ra, rb)
    input_grad, sums = run_last_sum([q[0]] + [shift(q[k], "z", k) for k in (1, 2, 3)])
    router_grad = run_router(where, sums, swap(sums), slot_tokens)
    return (input_grad, gate_grad, up_grad, down_grad, router_grad)


def solution(mesh):
    return jax.shard_map(
        on_device,
        mesh=mesh,
        in_specs=(
            P(("section", "et"), None),
            P("section", "et"),
            P(None, None, ("section", "et")),
            P(None, None, ("section", "et")),
            P(None, ("section", "et"), None),
            P(),
            P(),
            P(),
        ),
        out_specs=(
            P(("section", "et"), None),
            P(None, None, ("section", "et")),
            P(None, None, ("section", "et")),
            P(None, ("section", "et"), None),
            P(),
        ),
        check_vma=False,
    )
```

```python
import jax
import jax.numpy as jnp
from jax import lax
from jax.experimental import pallas as pl
from jax.experimental.pallas import tpu as pltpu
from jax.sharding import PartitionSpec as P

AXES = ("section", "et")
BF = jnp.bfloat16
F32 = jnp.float32
D = 6144
NX, NC, NY, NZ = 4, 2, 4, 4
H = 128
SHORT = 64
HALF = 256


def linear(x, c, y, z):
    return ((x * NC + c) * NY + y) * NZ + z


def shift_pairs(axis, step):
    pairs = []
    for x in range(NX):
        for c in range(NC):
            for y in range(NY):
                for z in range(NZ):
                    to = {
                        "x": ((x + step) % NX, c, y, z),
                        "y": (x, c, (y + step) % NY, z),
                        "z": (x, c, y, (z + step) % NZ),
                    }[axis]
                    pairs.append((linear(x, c, y, z), linear(*to)))
    return pairs


def shift(value, axis, step):
    return lax.ppermute(value, AXES, shift_pairs(axis, step))


def swap(value):
    pairs = [
        (linear(x, c, y, z), linear(x, 1 - c, y, z))
        for x in range(NX)
        for c in range(NC)
        for y in range(NY)
        for z in range(NZ)
    ]
    return lax.ppermute(value, AXES, pairs)


def position():
    section = lax.axis_index("section")
    et = lax.axis_index("et")
    return section // NC, section % NC, et // NZ, et % NZ


def nt(left, right):
    return lax.dot_general(left, right, (((1,), (1,)), ((), ())), preferred_element_type=F32)


def tn(left, right):
    return lax.dot_general(left, right, (((0,), (0,)), ((), ())), preferred_element_type=F32)


def total(first, rest):
    out = first.astype(F32)
    for r in rest:
        out = out + r.astype(F32)
    return out


KT = 1024
FT = 512
WT = 1024
MIB = 2**20
WIDE = D // 2 + 384


def vmem_specs(n):
    return [pl.BlockSpec(memory_space=pltpu.VMEM)] * n


SMEM_SPEC = pl.BlockSpec(memory_space=pltpu.SMEM)


def pack_kernel(tokens, grads, out):
    out[0:64, :] = grads[...]
    rows = tokens[...].astype(F32)
    for b in range(0, 16, 4):
        four = [rows[:, (b + i) * 384 : (b + i + 1) * 384] for i in range(4)]
        out[64 + 4 * b : 80 + 4 * b, :] = jnp.concatenate(four, axis=0).astype(BF)


def run_pack(tokens, grads):
    return pl.pallas_call(
        pack_kernel,
        out_shape=jax.ShapeDtypeStruct((128, 384), BF),
        in_specs=vmem_specs(2),
        out_specs=vmem_specs(1)[0],
        compiler_params=pltpu.CompilerParams(vmem_limit_bytes=4 * MIB),
        name="pack",
    )(tokens, grads)


def first_stage_kernel(where, *refs):
    packed, t_out, g_out, buf = refs[0:4], refs[-3], refs[-2], refs[-1]
    for k in range(NZ):
        at = (where[2] - k) % NZ
        rows = packed[k][64:128, :].astype(F32)
        for b in range(16):
            buf[at, :, 384 * b : 384 * (b + 1)] = rows[4 * b : 4 * b + 4]
        start = pl.multiple_of(384 * at, 128)
        g_out[:, pl.ds(start, 384)] = packed[k][0:64, :]
    t_out[...] = jnp.concatenate([buf[k] for k in range(NZ)], axis=0).astype(BF)


def run_first_stage(where, packed, before):
    return pl.pallas_call(
        first_stage_kernel,
        out_shape=[jax.ShapeDtypeStruct((16, D), BF), jax.ShapeDtypeStruct((64, 1536), BF)],
        in_specs=[SMEM_SPEC] + vmem_specs(4) + [pl.BlockSpec(memory_space=pl.ANY)] * len(before),
        out_specs=vmem_specs(2),
        scratch_shapes=[pltpu.VMEM((NZ, 4, D), F32)],
        compiler_params=pltpu.CompilerParams(vmem_limit_bytes=4 * MIB),
        name="first_stage",
    )(where, *packed, *before)


def near_halves_kernel(t_low, t_high, g_low, g_high, a, b, c, d):
    a[...] = t_low[:, 0 : D // 2]
    b[...] = t_high[:, D // 2 : D]
    c[...] = g_low[0:32, :]
    d[...] = g_high[32:64, :]


def run_near_halves(t_low, t_high, g_low, g_high):
    return pl.pallas_call(
        near_halves_kernel,
        out_shape=[jax.ShapeDtypeStruct((16, D // 2), BF)] * 2
        + [jax.ShapeDtypeStruct((32, 1536), BF)] * 2,
        in_specs=vmem_specs(4),
        out_specs=vmem_specs(4),
        compiler_params=pltpu.CompilerParams(vmem_limit_bytes=4 * MIB),
        name="near_halves",
    )(t_low, t_high, g_low, g_high)


def second_stage_kernel(where, *refs):
    t, g, t_out, g_out = refs[0:5], refs[5:10], refs[10], refs[11]
    y = where[1]
    for piece, step in zip(t[0:3], (0, -1, 1)):
        start = pl.multiple_of(16 * ((y + step + NY) % NY), 16)
        t_out[pl.ds(start, 16), :] = piece[...]
    start = pl.multiple_of(16 * ((y + 2) % NY), 16)
    t_out[pl.ds(start, 16), 0 : D // 2] = t[3][...]
    t_out[pl.ds(start, 16), D // 2 : D] = t[4][...]
    for piece, at in zip(g, (0, 64, 192, 128, 160)):
        g_out[at : at + piece.shape[0], :] = piece[...]


def run_second_stage(where, t, g):
    return pl.pallas_call(
        second_stage_kernel,
        out_shape=[jax.ShapeDtypeStruct((64, D), BF), jax.ShapeDtypeStruct((HALF, 1536), BF)],
        in_specs=[SMEM_SPEC] + vmem_specs(10),
        out_specs=vmem_specs(2),
        compiler_params=pltpu.CompilerParams(vmem_limit_bytes=4 * MIB),
        name="second_stage",
    )(where, *t, *g)


def halves_kernel(t_low, t_high, g_low, g_high, a, b, c, d):
    a[...] = t_low[0:32, :]
    b[...] = t_high[32:64, :]
    c[...] = g_low[0:128, :]
    d[...] = g_high[128:256, :]


def run_halves(t_low, t_high, g_low, g_high):
    return pl.pallas_call(
        halves_kernel,
        out_shape=[jax.ShapeDtypeStruct((32, D), BF)] * 2
        + [jax.ShapeDtypeStruct((128, 1536), BF)] * 2,
        in_specs=vmem_specs(4),
        out_specs=vmem_specs(4),
        compiler_params=pltpu.CompilerParams(vmem_limit_bytes=4 * MIB),
        name="halves",
    )(t_low, t_high, g_low, g_high)


def relay_kernel(*refs):
    value, (out, sem) = refs[0], refs[-2:]
    copy = pltpu.make_async_copy(value, out, sem)
    copy.start()
    copy.wait()


def run_relay(value, before):
    hbm = [pl.BlockSpec(memory_space=pltpu.HBM)]
    return pl.pallas_call(
        relay_kernel,
        out_shape=jax.ShapeDtypeStruct(value.shape, value.dtype),
        in_specs=hbm * (1 + len(before)),
        out_specs=hbm[0],
        scratch_shapes=[pltpu.SemaphoreType.DMA],
        compiler_params=pltpu.CompilerParams(vmem_limit_bytes=1 * MIB),
        cost_estimate=pl.CostEstimate(flops=0, bytes_accessed=6_000_000, transcendentals=0),
        name="relay",
    )(value, *before)


def row_copies(pieces, rows, sem):
    places = (0, 64, 192, 128, 160)
    return [
        pltpu.make_async_copy(
            piece, rows.at[pl.ds(at, piece.shape[0]), pl.ds(0, D)], sem.at[r]
        )
        for r, (piece, at) in enumerate(zip(pieces, places))
    ]


def grad_copies(pieces, grads, sem, y):
    places = ((0, 0), (-1, 0), (1, 0), (2, 0), (2, 128))
    copies = []
    for j, (piece, (step, at)) in enumerate(zip(pieces, places)):
        start = pl.multiple_of(((y + step + NY) % NY) * 1536, 128)
        copies.append(
            pltpu.make_async_copy(
                piece, grads.at[pl.ds(at, piece.shape[0]), pl.ds(start, 1536)], sem.at[j]
            )
        )
    return copies


def split_three(value):
    high = value.astype(BF)
    rest = value - high.astype(F32)
    middle = rest.astype(BF)
    low = (rest - middle.astype(F32)).astype(BF)
    return jnp.concatenate([high, middle, low], axis=1)


def join_three(parts):
    out = parts.astype(F32)
    return out[:, 0:128] + out[:, 128:256] + out[:, 256:384]


def early_kernel(where, *refs):
    t, g, weights = refs[0:3], refs[3:6], (refs[6:9], refs[9:12])
    acc_g, acc_b, wv, dv, sem_w, sem_d = refs[12:18]
    y = where[1]
    tiles = D // KT

    def wide_copies(i):
        k = pl.ds(pl.multiple_of(i * KT, KT), KT)
        return [
            pltpu.make_async_copy(
                weights[s][n].at[:, k, :], wv.at[s, n, :, k, :], sem_w.at[i, s * 2 + n]
            )
            for s in range(2)
            for n in range(2)
        ]

    tall_copies = []
    for j, step in enumerate((0, -1, 1)):
        block = pl.ds(pl.multiple_of(((y + step + NY) % NY) * 1536, 128), 1536)
        tall_copies.append(
            [
                pltpu.make_async_copy(weights[s][2].at[:, :, block], dv.at[j, s], sem_d.at[j, s])
                for s in range(2)
            ]
        )
    for i in range(tiles):
        for copy in wide_copies(i):
            copy.start()
    for group in tall_copies:
        for copy in group:
            copy.start()
    acc_g[...] = jnp.zeros(acc_g.shape, F32)
    acc_b[...] = jnp.zeros(acc_b.shape, F32)

    @pl.loop(0, tiles)
    def _(i):
        for copy in wide_copies(i):
            copy.wait()
        k = pl.ds(pl.multiple_of(i * KT, KT), KT)
        wide = jnp.concatenate(
            [wv[s, n, e, k, :] for s in range(2) for e in range(2) for n in range(2)], axis=1
        )
        rows = jnp.concatenate([piece[:, k] for piece in t], axis=0)
        acc_g[...] += jnp.dot(rows, wide, preferred_element_type=F32)

    for j, group in enumerate(tall_copies):
        for copy in group:
            copy.wait()
        tall = jnp.concatenate([dv[j, s, e] for s in range(2) for e in range(2)], axis=0)
        acc_b[...] += nt(g[j][...], tall)


def run_early(where, t, g, weights):
    hbm = [pl.BlockSpec(memory_space=pltpu.HBM)]
    return pl.pallas_call(
        early_kernel,
        out_shape=[
            jax.ShapeDtypeStruct((192, 1024), F32),
            jax.ShapeDtypeStruct((HALF, 512), F32),
        ],
        in_specs=[SMEM_SPEC] + vmem_specs(6) + hbm * 6,
        out_specs=vmem_specs(2),
        scratch_shapes=[
            pltpu.VMEM((2, 2, 2, D, H), BF),
            pltpu.VMEM((3, 2, 2, H, 1536), BF),
            pltpu.SemaphoreType.DMA((D // KT, 4)),
            pltpu.SemaphoreType.DMA((3, 2)),
        ],
        compiler_params=pltpu.CompilerParams(vmem_limit_bytes=22 * MIB),
        cost_estimate=pl.CostEstimate(
            flops=3_600_000_000, bytes_accessed=20_000_000, transcendentals=0
        ),
        name="early",
    )(where, *t, *g, *weights)


def main_kernel(where, *refs):
    t_in, g_in = refs[0:5], refs[5:10]
    weights = (refs[10:13], refs[13:16])
    slots_ref, gates_ref, early_g, early_b = refs[16:20]
    pa_out, pb_out = refs[20:25], refs[25:30]
    own_out, rows_out, grads_out = refs[30:33]
    wv, dv, acc_g, acc_b, deltas, tile, rbuf = refs[33:40]
    sem_t, sem_g, sem_w, sem_d = refs[40:44]
    x, y, core = where[0], where[1], where[4]
    copies_t = row_copies(t_in, rows_out, sem_t)
    copies_g = grad_copies(g_in, grads_out, sem_g, y)
    tiles = D // KT

    def wide_copies(i):
        k = pl.ds(pl.multiple_of(i * KT, KT), KT)
        return [
            pltpu.make_async_copy(
                weights[s][n].at[:, k, :], wv.at[s, n, :, k, :], sem_w.at[i, s * 2 + n]
            )
            for s in range(2)
            for n in range(2)
        ]

    far = pl.ds(pl.multiple_of(((y + 2) % NY) * 1536, 128), 1536)
    tall_copies = [
        pltpu.make_async_copy(weights[s][2].at[:, :, far], dv.at[s], sem_d.at[s]) for s in range(2)
    ]
    for copy in copies_t:
        copy.start()
    for i in range(tiles):
        for copy in wide_copies(i):
            copy.start()
    for copy in copies_g + tall_copies:
        copy.start()
    acc_g[0:128, :] = early_g[0:128, :]
    acc_g[128:192, :] = jnp.zeros((64, 1024), F32)
    acc_g[192:256, :] = early_g[128:192, :]
    scales = []
    slot = lax.broadcasted_iota(jnp.int32, (HALF, 256), 1)
    row = lax.broadcasted_iota(jnp.int32, (HALF, 256), 0)
    block = row // 64
    token = ((x - block + NX) % NX) * 128 + core * 64 + (row - block * 64)
    for e in range(2):
        hit = (token == slots_ref[e : e + 1, :]) & (slot < where[5 + e])
        gate = jnp.broadcast_to(gates_ref[e : e + 1, :], (HALF, 256))
        scales.append(jnp.sum(jnp.where(hit, gate, 0.0), axis=1, keepdims=True))
    for copy in copies_t:
        copy.wait()

    @pl.loop(0, tiles)
    def _(i):
        for copy in wide_copies(i):
            copy.wait()
        k = pl.ds(pl.multiple_of(i * KT, KT), KT)
        wide = jnp.concatenate(
            [wv[s, n, e, k, :] for s in range(2) for e in range(2) for n in range(2)], axis=1
        )
        acc_g[128:192, :] += jnp.dot(rows_out[128:192, k], wide, preferred_element_type=F32)

    for copy in copies_g + tall_copies:
        copy.wait()
    tall = jnp.concatenate([dv[s, e] for s in range(2) for e in range(2)], axis=0)
    acc_b[...] = early_b[...] + nt(grads_out[:, far], tall)
    router = [0.0, 0.0]
    for s in range(2):
        for e in range(2):
            j = s * 2 + e
            pre_gate = acc_g[:, j * 256 : j * 256 + H]
            pre_up = acc_g[:, j * 256 + H : (j + 1) * 256]
            back = acc_b[:, j * H : (j + 1) * H]
            scale = scales[e]
            sigma = jax.nn.sigmoid(pre_gate)
            active = pre_gate * sigma
            hidden = active * pre_up
            router[e] += jnp.sum(hidden.astype(BF).astype(F32) * back, axis=1, keepdims=True)
            hidden_grad = back * scale
            gate_delta = (hidden_grad * pre_up * sigma * (1.0 + pre_gate * (1.0 - sigma))).astype(BF)
            up_delta = (hidden_grad * active).astype(BF)
            deltas[:, j * 256 : j * 256 + H] = gate_delta
            deltas[:, j * 256 + H : (j + 1) * 256] = up_delta
            out, at = (own_out, 0) if s == 0 else (rows_out, D)
            out[:, at + e * 256 : at + e * 256 + H] = gate_delta
            out[:, at + e * 256 + H : at + (e + 1) * 256] = up_delta
            at += 512 + e * H
            out[:, at : at + H] = (hidden * scale).astype(BF)
    lane = lax.broadcasted_iota(jnp.int32, (HALF, 128), 1)
    spread = jnp.where(lane == 0, router[0], jnp.where(lane == 1, router[1], 0.0))
    for k in range(NX):
        to = pl.multiple_of(((x - k) % NX) * 64, 64)
        rbuf[pl.ds(to, 64), :] = spread[k * 64 : (k + 1) * 64]
    line = rbuf[...].T[0:2]
    four = [line[e : e + 1, h * 128 : (h + 1) * 128] for e in range(2) for h in range(2)]
    sums = split_three(jnp.concatenate(four + [jnp.zeros((12, 128), F32)], axis=0))
    for out in pa_out:
        out[:, D // 2 :] = jnp.zeros((out.shape[0], 384), BF)
        out[0:16, D // 2 :] = sums

    def partial(i):
        f = pl.ds(pl.multiple_of(i * WT, WT), WT)
        wide = jnp.concatenate(
            [wv[s, n, e, f, :] for s in range(2) for e in range(2) for n in range(2)], axis=1
        )
        return nt(deltas[...], wide)

    half = D // 2 // WT

    @pl.loop(0, half)
    def _(i):
        f = pl.ds(pl.multiple_of(i * WT, WT), WT)
        part = partial(i).astype(BF)
        for out, at in zip(pa_out, (0, 64, 192, 128, 160)):
            out[:, f] = part[at : at + out.shape[0], :]

    @pl.loop(0, half)
    def _(i):
        f = pl.ds(pl.multiple_of(i * WT, WT), WT)
        tile[...] = partial(i + half).astype(BF)
        for out, k, first in zip(pb_out, (0, 1, 3, 2, 2), (0, 0, 0, 0, 2)):
            for b in range(out.shape[0]):
                src = pl.multiple_of((first + b) * 64 + ((y + k) % NY) * 16, 16)
                out[b, :, f] = tile[pl.ds(src, 16), :]


def run_main(where, t, g, weights, slots, gates, early):
    hbm = [pl.BlockSpec(memory_space=pltpu.HBM)]
    out_shape = (
        [jax.ShapeDtypeStruct((64, WIDE), BF)] * 3
        + [jax.ShapeDtypeStruct((32, WIDE), BF)] * 2
        + [jax.ShapeDtypeStruct((4, 16, D // 2), BF)] * 3
        + [jax.ShapeDtypeStruct((2, 16, D // 2), BF)] * 2
        + [jax.ShapeDtypeStruct((HALF, 768), BF)]
        + [jax.ShapeDtypeStruct((HALF, D + 768), BF)]
        + [jax.ShapeDtypeStruct((HALF, D), BF)]
    )
    return pl.pallas_call(
        main_kernel,
        out_shape=out_shape,
        in_specs=[SMEM_SPEC] + hbm * 16 + vmem_specs(4),
        out_specs=vmem_specs(13),
        scratch_shapes=[
            pltpu.VMEM((2, 2, 2, D, H), BF),
            pltpu.VMEM((2, 2, H, 1536), BF),
            pltpu.VMEM((HALF, 1024), F32),
            pltpu.VMEM((HALF, 512), F32),
            pltpu.VMEM((HALF, 1024), BF),
            pltpu.VMEM((HALF, WT), BF),
            pltpu.VMEM((HALF, 128), F32),
            pltpu.SemaphoreType.DMA((5,)),
            pltpu.SemaphoreType.DMA((5,)),
            pltpu.SemaphoreType.DMA((D // KT, 4)),
            pltpu.SemaphoreType.DMA((2,)),
        ],
        compiler_params=pltpu.CompilerParams(vmem_limit_bytes=24 * MIB),
        cost_estimate=pl.CostEstimate(
            flops=8_000_000_000, bytes_accessed=30_000_000, transcendentals=262144
        ),
        name="main",
    )(where, *t, *g, *weights, slots, gates, *early)


def up_kernel(*refs):
    rows_own, rows_sib, own, sib = refs[0:4]
    gate_out, up_out, token = refs[-3:]
    token[...] = jnp.zeros(token.shape, F32)
    part = tn(rows_own[...], own[:, 0:512]) + tn(rows_sib[...], sib[:, 0:512])
    for e in range(2):
        gate_out[e] = part[:, e * 256 : e * 256 + H].astype(BF)
        up_out[e] = part[:, e * 256 + H : (e + 1) * 256].astype(BF)


def run_up(rows_own, rows_sib, own, before):
    tile = pl.BlockSpec((HALF, 3 * FT), lambda i: (0, i))
    whole = pl.BlockSpec((HALF, 768), lambda i: (0, 0))
    tail = pl.BlockSpec((HALF, 768), lambda i: (0, D // 768))
    out = pl.BlockSpec((2, 3 * FT, H), lambda i: (0, i, 0))
    return pl.pallas_call(
        up_kernel,
        grid=(D // (3 * FT),),
        out_shape=[
            jax.ShapeDtypeStruct((2, D, H), BF),
            jax.ShapeDtypeStruct((2, D, H), BF),
            jax.ShapeDtypeStruct((8, 128), F32),
        ],
        in_specs=[tile, tile, whole, tail]
        + [pl.BlockSpec(memory_space=pl.ANY)] * len(before),
        out_specs=[out, out, pl.BlockSpec((8, 128), lambda i: (0, 0))],
        compiler_params=pltpu.CompilerParams(
            dimension_semantics=("arbitrary",), vmem_limit_bytes=16 * MIB
        ),
        cost_estimate=pl.CostEstimate(
            flops=3_200_000_000, bytes_accessed=13_000_000, transcendentals=0
        ),
        name="up_grads",
    )(rows_own, rows_sib, own, rows_sib, *before)


def down_kernel(grads_own, grads_sib, own, sib, out, token, hidden):
    token[...] = jnp.zeros(token.shape, F32)

    @pl.when(pl.program_id(0) == 0)
    def _():
        hidden[:, 0:HALF] = own[:, 512:768].T
        hidden[:, HALF:512] = sib[:, 512:768].T

    part = jnp.dot(hidden[:, 0:HALF], grads_own[...], preferred_element_type=F32)
    part += jnp.dot(hidden[:, HALF:512], grads_sib[...], preferred_element_type=F32)
    for e in range(2):
        out[e] = part[e * H : (e + 1) * H].astype(BF)


def run_down(grads_own, grads_sib, own, rows_sib):
    tile = pl.BlockSpec((HALF, 4 * FT), lambda i: (0, i))
    whole = pl.BlockSpec((HALF, 768), lambda i: (0, 0))
    tail = pl.BlockSpec((HALF, 768), lambda i: (0, D // 768))
    return pl.pallas_call(
        down_kernel,
        grid=(D // (4 * FT),),
        out_shape=[
            jax.ShapeDtypeStruct((2, H, D), BF),
            jax.ShapeDtypeStruct((8, 128), F32),
        ],
        in_specs=[tile, tile, whole, tail],
        out_specs=[
            pl.BlockSpec((2, H, 4 * FT), lambda i: (0, 0, i)),
            pl.BlockSpec((8, 128), lambda i: (0, 0)),
        ],
        scratch_shapes=[pltpu.VMEM((256, 512), BF)],
        compiler_params=pltpu.CompilerParams(
            dimension_semantics=("arbitrary",), vmem_limit_bytes=16 * MIB
        ),
        cost_estimate=pl.CostEstimate(
            flops=1_600_000_000, bytes_accessed=10_000_000, transcendentals=0
        ),
        name="down_grads",
    )(grads_own, grads_sib, own, rows_sib)


def middle_sum_kernel(*refs):
    a_down, a_up, b_up, b_down = refs[0:4]
    low_a, high_a, low_b, high_b = refs[4:8]
    out_a_down, out_a_up, out_b_up, out_b_down = refs[8:12]
    half = D // 2
    out_a_down[0:32, 0:half] = total(a_down[0:32, 0:half], [low_a[:, 0:half]]).astype(BF)
    out_a_down[32:64, :] = a_down[32:64, :]
    sums = join_three(a_down[0:16, half:]) + join_three(low_a[0:16, half:])
    out_a_down[0:16, half:] = split_three(sums)
    out_a_down[16:32, half:] = a_down[16:32, half:]
    out_a_up[0:32, :] = a_up[0:32, :]
    out_a_up[32:64, :] = total(a_up[32:64, :], [high_a[...]]).astype(BF)
    for k in range(2):
        out_b_up[k] = total(b_up[k], [low_b[k]]).astype(BF)
        out_b_up[2 + k] = b_up[2 + k]
        out_b_down[k] = b_down[k]
        out_b_down[2 + k] = total(b_down[2 + k], [high_b[k]]).astype(BF)


def run_middle_sum(blocks, halves):
    return pl.pallas_call(
        middle_sum_kernel,
        out_shape=[jax.ShapeDtypeStruct((64, WIDE), BF)] * 2
        + [jax.ShapeDtypeStruct((4, 16, D // 2), BF)] * 2,
        in_specs=vmem_specs(8),
        out_specs=vmem_specs(4),
        compiler_params=pltpu.CompilerParams(vmem_limit_bytes=8 * MIB),
        name="middle_sum",
    )(*blocks, *halves)


def first_sum_kernel(where, *refs):
    ra, rb, qa, qb, buf = refs[0:3], refs[3:6], refs[7:11], refs[11:15], refs[15]
    half = D // 2
    buf[...] = total(ra[0][:, 0:half], [r[:, 0:half] for r in ra[1:]]).astype(BF)
    sums = join_three(ra[0][0:16, half:])
    for r in ra[1:]:
        sums += join_three(r[0:16, half:])
    sums = split_three(sums)
    for k in range(NY):
        start = pl.multiple_of(((where[1] + k) % NY) * 16, 16)
        qa[k][:, 0:half] = buf[pl.ds(start, 16), :]
        qa[k][:, half:] = sums
    for k in range(NX):
        qb[k][...] = total(rb[0][k], [r[k] for r in rb[1:]]).astype(BF)


def run_first_sum(where, ra, rb, token):
    return pl.pallas_call(
        first_sum_kernel,
        out_shape=[jax.ShapeDtypeStruct((16, WIDE), BF)] * 4
        + [jax.ShapeDtypeStruct((16, D // 2), BF)] * 4,
        in_specs=[SMEM_SPEC] + vmem_specs(7),
        out_specs=vmem_specs(8),
        scratch_shapes=[pltpu.VMEM((64, D // 2), BF)],
        compiler_params=pltpu.CompilerParams(vmem_limit_bytes=8 * MIB),
        name="first_sum",
    )(where, *ra, *rb, token)


def second_sum_kernel(where, *refs):
    ra, rb, own, out, buf = refs[0:4], refs[4:8], refs[9], refs[10:13], refs[13]
    half = D // 2
    for n, r in enumerate((ra, rb)):
        part = total(r[0][:, 0:half], [p[:, 0:half] for p in r[1:]])
        for k in range(NZ):
            buf[k, :, n * half : (n + 1) * half] = part[4 * k : 4 * k + 4]
    sums = join_three(ra[0][:, half:])
    for r in ra[1:]:
        sums += join_three(r[:, half:])
    parts = split_three(sums)[0:4]
    for k in range(NZ):
        rows = buf[(where[2] + k) % NZ]
        if k == 0:
            own[:, 0:D] = rows
            own[:, D:] = sums[0:4]
        else:
            out[k - 1][:, 0:D] = rows.astype(BF)
            out[k - 1][:, D:] = parts


def run_second_sum(where, ra, rb, token):
    return pl.pallas_call(
        second_sum_kernel,
        out_shape=[jax.ShapeDtypeStruct((4, D + 128), F32)]
        + [jax.ShapeDtypeStruct((4, D + 384), BF)] * 3,
        in_specs=[SMEM_SPEC] + vmem_specs(9),
        out_specs=vmem_specs(4),
        scratch_shapes=[pltpu.VMEM((NZ, 4, D), F32)],
        compiler_params=pltpu.CompilerParams(vmem_limit_bytes=8 * MIB),
        name="second_sum",
    )(where, *ra, *rb, token)


def last_sum_kernel(own, *refs):
    out, sums_out = refs[3], refs[4]
    out[...] = total(own[:, 0:D], [r[:, 0:D] for r in refs[0:3]]).astype(BF)
    sums = own[:, D:]
    for r in refs[0:3]:
        sums += join_three(r[:, D:])
    sums_out[0:4, :] = sums
    sums_out[4:8, :] = jnp.zeros((4, 128), F32)


def run_last_sum(pieces):
    return pl.pallas_call(
        last_sum_kernel,
        out_shape=[jax.ShapeDtypeStruct((4, D), BF), jax.ShapeDtypeStruct((8, 128), F32)],
        in_specs=vmem_specs(4),
        out_specs=vmem_specs(2),
        compiler_params=pltpu.CompilerParams(vmem_limit_bytes=4 * MIB),
        name="last_sum",
    )(*pieces)


def router_kernel(where, own, other, slots_ref, out):
    first = jnp.where(where[4] == 0, own[...], other[...])
    second = jnp.where(where[4] == 0, other[...], own[...])
    slots = slots_ref[...].T
    index = lax.broadcasted_iota(jnp.int32, (256, 128), 1)
    spread = jnp.zeros((256, 128), F32)
    for e in range(2):
        picked = jnp.zeros((256, 1), F32)
        for core, values in enumerate((first, second)):
            for h in range(2):
                at = index + h * 128
                token = (at // 64) * 128 + core * 64 + at % 64
                hit = slots[:, e : e + 1] == token
                line = jnp.broadcast_to(values[2 * e + h : 2 * e + h + 1, :], (256, 128))
                picked += jnp.sum(jnp.where(hit, line, 0.0), axis=1, keepdims=True)
        spread = jnp.where(index == e, picked, spread)
    lines = spread.T
    at = lax.broadcasted_iota(jnp.int32, (1, 256), 1)
    for e in range(2):
        out[e : e + 1, :] = jnp.where(at < where[5 + e], lines[e : e + 1, :], 0.0)


def run_router(where, own, other, slots):
    return pl.pallas_call(
        router_kernel,
        out_shape=jax.ShapeDtypeStruct((2, 256), F32),
        in_specs=[SMEM_SPEC] + vmem_specs(3),
        out_specs=vmem_specs(1)[0],
        compiler_params=pltpu.CompilerParams(vmem_limit_bytes=4 * MIB),
        name="router",
    )(where, own, other, slots)


def on_device(
    tokens_in, out_grad, gate_weight, up_weight, down_weight, slot_tokens, slot_counts, slot_gates
):
    x, c, y, z = position()
    where = jnp.stack([x, y, z, c, c, slot_counts[0], slot_counts[1]]).astype(jnp.int32)
    gate_sib, up_sib = swap(gate_weight), swap(up_weight)

    packed = run_pack(tokens_in, out_grad)
    packed = [packed] + [shift(packed, "z", k) for k in (1, 2, 3)]
    t16, g64 = run_first_stage(where, packed, [gate_sib, up_sib])
    down_sib = swap(run_relay(down_weight, [t16]))
    t_low, t_high = shift(t16, "y", 1), shift(t16, "y", -1)
    g_low, g_high = shift(g64, "x", 1), shift(g64, "x", -1)
    a, b, e, f = run_near_halves(t_low, t_high, g_low, g_high)
    t = (t16, t_low, t_high, shift(a, "y", 1), shift(b, "y", -1))
    g = (g64, g_low, g_high, shift(e, "x", 1), shift(f, "x", -1))
    t64, g256 = run_second_stage(where, t, g)
    t_low, t_high = shift(t64, "x", 1), shift(t64, "x", -1)
    g_low, g_high = shift(g256, "y", 1), shift(g256, "y", -1)
    a, b, e, f = run_halves(t_low, t_high, g_low, g_high)
    t = (t64, t_low, t_high, shift(a, "x", 1), shift(b, "x", -1))
    g = (g256, g_low, g_high, shift(e, "y", 1), shift(f, "y", -1))
    weights = (gate_weight, up_weight, down_weight, gate_sib, up_sib, down_sib)
    early = run_early(where, t[0:3], g[0:3], weights)
    outs = run_main(where, t, g, weights, slot_tokens, slot_gates, early)
    a_own, a_down, a_up, a_low, a_high = outs[0:5]
    b_own, b_up, b_down, b_low, b_high = outs[5:10]
    dl_own, rows, grads = outs[10:]

    halves = [shift(a_low, "x", -1), shift(a_high, "x", 1)]
    halves += [shift(b_low, "y", 1), shift(b_high, "y", -1)]
    rows_sib = swap(rows)
    grads_sib = swap(run_relay(grads, halves))
    a_down, a_up, b_up, b_down = run_middle_sum((a_down, a_up, b_up, b_down), halves)
    gate_grad, up_grad, token = run_up(rows, rows_sib, dl_own, [a_down])
    ra = [a_own, shift(a_down, "x", -1), shift(a_up, "x", 1)]
    rb = [b_own, shift(b_up, "y", 1), shift(b_down, "y", -1)]
    q = run_first_sum(where, ra, rb, token)
    qa, qb = q[0:4], q[4:8]
    ra = [qa[0]] + [shift(qa[k], "y", k) for k in (1, 2, 3)]
    rb = [qb[0]] + [shift(qb[k], "x", -k) for k in (1, 2, 3)]
    down_grad, token = run_down(grads, grads_sib, dl_own, rows_sib)
    q = run_second_sum(where, ra, rb, token)
    input_grad, sums = run_last_sum([q[0]] + [shift(q[k], "z", k) for k in (1, 2, 3)])
    router_grad = run_router(where, sums, swap(sums), slot_tokens)
    return (input_grad, gate_grad, up_grad, down_grad, router_grad)


def solution(mesh):
    return jax.shard_map(
        on_device,
        mesh=mesh,
        in_specs=(
            P(("section", "et"), None),
            P("section", "et"),
            P(None, None, ("section", "et")),
            P(None, None, ("section", "et")),
            P(None, ("section", "et"), None),
            P(),
            P(),
            P(),
        ),
        out_specs=(
            P(("section", "et"), None),
            P(None, None, ("section", "et")),
            P(None, None, ("section", "et")),
            P(None, ("section", "et"), None),
            P(),
        ),
        check_vma=False,
    )
```
